32 devices in a mesh: band: 4 (over y, x), seq: 8 (over z, core).
Axes of the slice: x: 2, y: 2, z: 4, core: 2. Of those that a mesh axis runs over, the one named last changes fastest.
Arguments:
- frames: bfloat16 [8, 1024, 768], P('band', 'seq'), may hold values from -6 to 6
- caption: bfloat16 [8, 256, 768], P('band', 'seq'), may hold values from -6 to 6
- timesteps: int32 [8], replicated, may hold values from 0 to 999
- cap_len: int32 [8], replicated, may hold values from 5 to 256, as said below
- attn_in: bfloat16 [768, 2304], replicated, may hold values from -0.21875 to 0.21875
- attn_out: bfloat16 [768, 768], replicated, may hold values from -0.875 to 0.875
- cross_query: bfloat16 [768, 768], replicated, may hold values from -0.21875 to 0.21875
- cross_keyval: bfloat16 [768, 1536], replicated, may hold values from -0.21875 to 0.21875
- cross_out: bfloat16 [768, 768], replicated, may hold values from -0.625 to 0.625
- mlp_up: bfloat16 [768, 3072], replicated, may hold values from -0.21875 to 0.21875
- up_bias: bfloat16 [3072], replicated, may hold values from -3 to 3
- mlp_down: bfloat16 [3072, 768], replicated, may hold values from -0.109375 to 0.109375
- down_bias: bfloat16 [768], replicated, may hold values from -3 to 3
- ada_weight: bfloat16 [768, 6912], replicated, may hold values from -0.21875 to 0.21875
- ada_bias: bfloat16 [6912], replicated, may hold values from -3 to 3
- time_first: bfloat16 [256, 768], replicated, may hold values from -0.375 to 0.375
- first_bias: bfloat16 [768], replicated, may hold values from -3 to 3
- time_second: bfloat16 [768, 768], replicated, may hold values from -0.21875 to 0.21875
- second_bias: bfloat16 [768], replicated, may hold values from -3 to 3
- cotangent: bfloat16 [8, 1024, 768], P('band', 'seq'), may hold values from -6 to 6
Outputs:
- out: bfloat16 [8, 1024, 768], P('band', 'seq')
- grad_frames: float32 [8, 1024, 768], P('band', 'seq')
- grad_caption: float32 [8, 256, 768], P('band', 'seq')
- grad_attn_in: float32 [768, 2304], P('seq')
- grad_attn_out: float32 [768, 768], P('seq')
- grad_cross_query: float32 [768, 768], P('seq')
- grad_cross_keyval: float32 [768, 1536], P('seq')
- grad_cross_out: float32 [768, 768], P('seq')
- grad_mlp_up: float32 [768, 3072], P('seq')
- grad_up_bias: float32 [3072], P('seq')
- grad_mlp_down: float32 [3072, 768], P('seq')
- grad_down_bias: float32 [768], P('seq')
- grad_ada_weight: float32 [768, 6912], P('seq')
- grad_ada_bias: float32 [6912], P('seq')
- grad_time_first: float32 [256, 768], P('seq')
- grad_first_bias: float32 [768], P('seq')
- grad_time_second: float32 [768, 768], P('seq')
- grad_second_bias: float32 [768], P('seq')
The draws below stay inside these ranges and needn't reach their ends.
Inputs may be any that keep to these rules, and one draw needn't show every extreme that they name: `cap_len`: in each group of 2 consecutive items (one band index) some caption uses all 256 tokens.
All inputs are finite; a program needn't handle non-finite values.
Results may differ from the reference program's by a relative error of at most 0.028.
Values may be sent and summed in bfloat16 or wider, within the bound.
No kernel may reach another device: no remote copies, remote signals or barrier semaphores. Data moves between devices by JAX's collectives and lax.ppermute only.
A program may use at most 384 MiB of HBM per device.

```python
import math
import jax
import jax.numpy as jnp
from jax import lax

D = 768
HEADS = 12
HEAD = 64
FF = 3072
TEMB = 256
CAP = 256
IB = 2
FRAMES = 1024
ITEMS = 8


def draw_cap_len(key, part):
    key = jax.random.fold_in(key, 11)
    first, second = jax.random.split(key)
    lengths = jax.random.randint(first, (ITEMS,), 5, CAP + 1)
    chosen = jax.random.randint(second, (ITEMS // IB,), 0, IB)
    places = jnp.arange(ITEMS // IB, dtype=jnp.int32) * IB + chosen
    lengths = lengths.at[places].set(CAP)
    return lengths.astype(jnp.int32)


def plant(values, rng, least, largest):
    spot = [jax.random.randint(jax.random.fold_in(rng, axis), (), 0, length) for axis, length in enumerate(values.shape)]
    longest = values.shape.index(max(values.shape))
    neighbour = spot[:longest] + [(spot[longest] + 1) % values.shape[longest]] + spot[longest + 1:]
    return values.at[tuple(spot)].set(least).at[tuple(neighbour)].set(largest)


def levels(rng, shape, cuts, least, high):
    def one(axis_at, blocks):
        draws = jax.random.uniform(jax.random.fold_in(jax.random.fold_in(rng, 6), axis_at), (blocks,), jnp.float32, least / len(cuts), high / len(cuts))
        return jnp.repeat(jnp.exp(draws), shape[axis_at] // blocks).reshape((-1,) + (1,) * (len(shape) - axis_at - 1))

    factor_of = one(*cuts[0])
    for cut in cuts[1:]:
        factor_of = factor_of * one(*cut)
    return factor_of


def noise(key, extent, scale, limit, shards=(), held_as=jnp.bfloat16):
    array = scale * jax.random.normal(key, extent, jnp.float32)
    if shards:
        array = array * levels(key, extent, shards, -0.22, 0.18)
    return jnp.clip(array, -limit, limit).astype(held_as)


def setup_inputs(seed: int = 0) -> dict:
    splits = jax.random.split(jax.random.key(seed), 21)
    return {
        "frames": noise(splits[0], (ITEMS, FRAMES, D), 1.0, 6.0, ((0, 4), (1, 8))),
        "caption": noise(splits[1], (ITEMS, CAP, D), 1.0, 6.0, ((0, 4), (1, 8))),
        "timesteps": plant(jax.random.randint(splits[2], (ITEMS,), 0, 1000), jax.random.fold_in(splits[2], 1), 0, 999).astype(jnp.int32),
        "cap_len": draw_cap_len(jax.random.fold_in(splits[20], 71), 0),
        "attn_in": noise(splits[4], (D, 3 * D), D ** -0.5, 0.21875),
        "attn_out": noise(splits[5], (D, D), (D // 16) ** -0.5, 0.875),
        "cross_query": noise(splits[6], (D, D), D ** -0.5, 0.21875),
        "cross_keyval": noise(splits[7], (D, 2 * D), D ** -0.5, 0.21875),
        "cross_out": noise(splits[8], (D, D), (D // 8) ** -0.5, 0.625),
        "mlp_up": noise(splits[9], (D, FF), D ** -0.5, 0.21875),
        "up_bias": noise(splits[10], (FF,), 0.5, 3.0),
        "mlp_down": noise(splits[11], (FF, D), FF ** -0.5, 0.109375),
        "down_bias": noise(splits[12], (D,), 0.5, 3.0),
        "ada_weight": noise(splits[13], (D, 9 * D), D ** -0.5, 0.21875),
        "ada_bias": noise(splits[14], (9 * D,), 0.5, 3.0),
        "time_first": noise(splits[15], (TEMB, D), TEMB ** -0.5, 0.375),
        "first_bias": noise(splits[16], (D,), 0.5, 3.0),
        "time_second": noise(splits[17], (D, D), D ** -0.5, 0.21875),
        "second_bias": noise(splits[18], (D,), 0.5, 3.0),
        "cotangent": noise(splits[19], (ITEMS, FRAMES, D), 1.0, 6.0, ((0, 4), (1, 8))),
    }


HIGH = lax.Precision.HIGHEST
EPSILON = 1e-06
NEGATIVE = -1e+30

@jax.custom_vjp
def low(v):
    return lax.optimization_barrier(v.astype(jnp.bfloat16)).astype(jnp.float32)

@jax.custom_vjp
def low_back(v):
    return v

def low_keep(v):
    return (low(v), None)

def low_pass(kept, grad):
    return (grad,)

def back_keep(v):
    return (v, None)

def back_low(kept, grad):
    return (low(grad),)
low.defvjp(low_keep, low_pass)
low_back.defvjp(back_keep, back_low)

def matmul(left, right):
    return jnp.dot(left, right, precision=HIGH)

def sinusoid(steps):
    half = TEMB // 2
    freq = jnp.exp(-math.log(10000.0) * jnp.arange(half, dtype=jnp.float32) / half)
    angle = steps.astype(jnp.float32)[:, None] * freq[None, :]
    return jnp.concatenate([jnp.cos(angle), jnp.sin(angle)], axis=1)

def layer_norm(value):
    mean = lax.optimization_barrier(jnp.mean(value, axis=-1, keepdims=True))
    centred = value - mean
    spread = lax.optimization_barrier(jnp.mean(centred * centred, axis=-1, keepdims=True))
    return centred * lax.rsqrt(spread + EPSILON)

def attend(query, keys, values, mask):
    scores = jnp.einsum('qhe,khe->hqk', query, keys, precision=HIGH) * HEAD ** (-0.5)
    scores = low_back(scores)
    scores = jnp.where(mask[None, None, :], scores, NEGATIVE)
    probs = jax.nn.softmax(scores, axis=-1)
    return jnp.einsum('hqk,khe->qhe', low(probs), values, precision=HIGH)

def block_attend(query, keys, values, mask):
    count = query.shape[0]
    rows = math.gcd(count, 512)
    blocks = query.reshape(count // rows, rows, HEADS, HEAD)
    mixed = lax.map(jax.checkpoint(lambda block: attend(block, keys, values, mask)), blocks)
    return mixed.reshape(count, D)

def item_forward(frames, caption, length, modulation, weights):
    attn_in, attn_out, cross_query, cross_keyval, cross_out, mlp_up, up_bias, mlp_down, down_bias = weights
    parts = modulation.reshape(9, D)
    h1 = low(layer_norm(frames) * (1.0 + parts[1]) + parts[0])
    joined = matmul(h1, attn_in)
    query = low_back(low(joined[:, :D])).reshape(FRAMES, HEADS, HEAD)
    keys = low_back(low(joined[:, D:2 * D])).reshape(FRAMES, HEADS, HEAD)
    values = low_back(low(joined[:, 2 * D:])).reshape(FRAMES, HEADS, HEAD)
    every = jnp.arange(FRAMES) >= 0
    mixed = low_back(low(block_attend(query, keys, values, every)))
    attn = low_back(matmul(mixed, attn_out))
    first = frames + parts[2] * attn
    h2 = low(layer_norm(first) * (1.0 + parts[4]) + parts[3])
    query2 = low_back(low(matmul(h2, cross_query))).reshape(FRAMES, HEADS, HEAD)
    cap_joined = matmul(caption, cross_keyval)
    keys2 = low_back(low(cap_joined[:, :D])).reshape(CAP, HEADS, HEAD)
    values2 = low_back(low(cap_joined[:, D:])).reshape(CAP, HEADS, HEAD)
    used = jnp.arange(CAP) < length
    mixed2 = low_back(low(block_attend(query2, keys2, values2, used)))
    attn2 = low_back(matmul(mixed2, cross_out))
    second = first + parts[5] * attn2
    h3 = low(layer_norm(second) * (1.0 + parts[7]) + parts[6])
    upper = low_back(matmul(h3, mlp_up) + up_bias)
    acted = low(jax.nn.gelu(upper))
    lower = low_back(matmul(acted, mlp_down) + down_bias)
    return second + parts[8] * lower

def forward(timesteps, cap_len, frames, caption, attn_in, attn_out, cross_query, cross_keyval, cross_out, mlp_up, up_bias, mlp_down, down_bias, ada_weight, ada_bias, time_first, first_bias, time_second, second_bias):
    embed = sinusoid(timesteps)
    inner = jax.nn.silu(matmul(embed, time_first) + first_bias)
    cond = matmul(inner, time_second) + second_bias
    modulation = matmul(jax.nn.silu(cond), ada_weight) + ada_bias
    weights = (attn_in, attn_out, cross_query, cross_keyval, cross_out, mlp_up, up_bias, mlp_down, down_bias)

    def one_item(pack):
        return item_forward(pack[0], pack[1], pack[2], pack[3], weights)
    return lax.map(jax.checkpoint(one_item), (frames, caption, cap_len, modulation))

def reference(frames, caption, timesteps, cap_len, attn_in, attn_out, cross_query, cross_keyval, cross_out, mlp_up, up_bias, mlp_down, down_bias, ada_weight, ada_bias, time_first, first_bias, time_second, second_bias, cotangent):
    primals = tuple((a.astype(jnp.float32) for a in (frames, caption, attn_in, attn_out, cross_query, cross_keyval, cross_out, mlp_up, up_bias, mlp_down, down_bias, ada_weight, ada_bias, time_first, first_bias, time_second, second_bias)))
    result, pull = jax.vjp(lambda *p: forward(timesteps, cap_len, *p), *primals)
    grads = pull(cotangent.astype(jnp.float32))
    return (result.astype(jnp.bfloat16), grads[0], grads[1], grads[2], grads[3], grads[4], grads[5], grads[6], grads[7], grads[8], grads[9], grads[10], grads[11], grads[12], grads[13], grads[14], grads[15], grads[16])
```

```python
import functools
import math

import jax
import jax.numpy as jnp
from jax import lax
from jax.experimental import pallas as pl
from jax.experimental.pallas import tpu as pltpu
from jax.sharding import PartitionSpec as P

D = 768
HEAD = 64
PAIRS = 6
FF = 3072
EPSILON = 1e-06
NEGATIVE = -1e30
SCALE = 0.125
F32 = jnp.float32
BF16 = jnp.bfloat16
MIB = 1 << 20


def dot(a, b):
    return jnp.dot(a, b, preferred_element_type=F32)


def dot_nt(a, b):
    return lax.dot_general(a, b, (((1,), (1,)), ((), ())), preferred_element_type=F32)


def dot_tn(a, b):
    return lax.dot_general(a, b, (((0,), (0,)), ((), ())), preferred_element_type=F32)


def split_dot(x, w, contract=0):
    high = x.astype(BF16).astype(F32)
    both = jnp.concatenate([high, x - high], axis=0).astype(BF16)
    out = lax.dot_general(
        both, w, (((1,), (contract,)), ((), ())), preferred_element_type=F32
    )
    return out[: x.shape[0]] + out[x.shape[0] :]


def silu(v):
    return v * (1.0 / (1.0 + jnp.exp(-v)))


def silu_grad(v):
    s = 1.0 / (1.0 + jnp.exp(-v))
    return s * (1.0 + v * (1.0 - s))


def norm(v):
    mean = jnp.mean(v, axis=-1, keepdims=True)
    centred = v - mean
    spread = jnp.mean(centred * centred, axis=-1, keepdims=True)
    rstd = lax.rsqrt(spread + EPSILON)
    return centred * rstd, rstd


def norm_back(n, rstd, w):
    return (
        w - jnp.mean(w, axis=-1, keepdims=True) - n * jnp.mean(w * n, axis=-1, keepdims=True)
    ) * rstd


def colsum(v):
    return jnp.sum(v, axis=0, keepdims=True)


def cols(i):
    return slice(i * 128, (i + 1) * 128)


def head_masks():
    lane = lax.broadcasted_iota(jnp.int32, (1, 128), 1)
    first = (lane < HEAD).astype(F32)
    return first.astype(BF16), (1.0 - first).astype(BF16)


def stack_heads(block):
    first, second = head_masks()
    return jnp.concatenate([block * first, block * second], axis=0)


def unstack_t(both):
    rows = both.shape[1] // 2
    pair = jnp.concatenate([both[:HEAD, :rows], both[HEAD:, rows:]], axis=0)
    return pair.T


def params(mib):
    return pltpu.CompilerParams(vmem_limit_bytes=mib * MIB)


def vmem():
    return pl.BlockSpec(memory_space=pltpu.VMEM)


def smem():
    return pl.BlockSpec(memory_space=pltpu.SMEM)


def cost(flops, nbytes, trans=0):
    return pl.CostEstimate(flops=int(flops), bytes_accessed=int(nbytes), transcendentals=int(trans))


def sds(shape, dtype):
    return jax.ShapeDtypeStruct(shape, dtype)


def call(kernel, outs, args, mib, flops=0, name=None, in_specs=None):
    outs = list(outs)
    nbytes = sum(math.prod(o.shape) * o.dtype.itemsize for o in outs)
    nbytes += sum(math.prod(a.shape) * a.dtype.itemsize for a in args)
    return pl.pallas_call(
        kernel,
        out_shape=outs,
        in_specs=in_specs or [vmem()] * len(args),
        out_specs=[vmem()] * len(outs),
        compiler_params=params(mib),
        cost_estimate=cost(flops, nbytes),
        name=name,
    )(*args)


def mod_kernel(embed, t1, b1, t2, b2, w, b, pre_o, cond_o, mod_o, act):
    @pl.when(pl.program_id(0) == 0)
    def _():
        pre = split_dot(embed[...], t1[...]) + b1[...].astype(F32)
        cond = split_dot(silu(pre), t2[...]) + b2[...].astype(F32)
        pre_o[...] = pre
        cond_o[...] = cond
        act[...] = silu(cond)

    mod_o[...] = split_dot(act[...], w[...]) + b[...].astype(F32)


def modulation(embed, t1, b1, t2, b2, w, b):
    items = embed.shape[0]
    whole = lambda shape: pl.BlockSpec(shape, lambda i: (0, 0))
    return pl.pallas_call(
        mod_kernel,
        grid=(9,),
        out_shape=[sds((items, D), F32), sds((items, D), F32), sds((items, 9 * D), F32)],
        in_specs=[
            whole(embed.shape), whole(t1.shape), whole(b1.shape), whole(t2.shape), whole(b2.shape),
            pl.BlockSpec((D, D), lambda i: (0, i)),
            pl.BlockSpec((1, D), lambda i: (0, i)),
        ],
        out_specs=[whole((items, D)), whole((items, D)), pl.BlockSpec((items, D), lambda i: (0, i))],
        scratch_shapes=[pltpu.VMEM((items, D), F32)],
        compiler_params=params(24),
        cost_estimate=cost(2 * items * D * D * 20, w.size * 2),
        name="modulation",
    )(embed, t1, b1, t2, b2, w, b)


def mod_back_kernel(dmod, w, act, cond, pre, embed, t2, own_act, own_pre, own_embed,
                    g_ada, gb_ada, g_t2, gb_t2, g_t1, gb_t1, acc):
    step = pl.program_id(0)

    @pl.when(step == 0)
    def _():
        acc[...] = jnp.zeros_like(acc)

    part = dmod[...]
    acc[...] += split_dot(part, w[...], contract=1)
    g_ada[...] = outer_sum(own_act[...], part)
    gb_ada[...] = colsum(part)

    @pl.when(step == 8)
    def _():
        dcond = acc[...] * silu_grad(cond[...])
        g_t2[...] = outer_sum(own_pre[...], dcond)
        gb_t2[...] = colsum(dcond)
        dpre = split_dot(dcond, t2[...], contract=1) * silu_grad(pre[...])
        g_t1[...] = outer_sum(own_embed[...], dpre)
        gb_t1[...] = colsum(dpre)


def outer_sum(left_t, right):
    lh = left_t.astype(BF16)
    ll = (left_t - lh.astype(F32)).astype(BF16)
    rh = right.astype(BF16)
    rl = (right - rh.astype(F32)).astype(BF16)
    return dot(lh, rh) + dot(ll, rh) + dot(lh, rl)


def mod_back(dmod, w, act, cond, pre, embed, t2, own_act, own_pre, own_embed):
    items = dmod.shape[0]
    whole = lambda a: pl.BlockSpec(a.shape, lambda i: (0, 0))
    whole_s = lambda s: pl.BlockSpec(s, lambda i: (0, 0))
    m, m1 = own_act.shape[0], own_embed.shape[0]
    return pl.pallas_call(
        mod_back_kernel,
        grid=(9,),
        out_shape=[
            sds((m, 9 * D), F32), sds((1, 9 * D), F32), sds((m, D), F32), sds((1, D), F32),
            sds((m1, D), F32), sds((1, D), F32),
        ],
        in_specs=[
            pl.BlockSpec((items, D), lambda i: (0, i)),
            pl.BlockSpec((D, D), lambda i: (0, i)),
            whole(act), whole(cond), whole(pre), whole(embed), whole(t2),
            whole(own_act), whole(own_pre), whole(own_embed),
        ],
        out_specs=[
            pl.BlockSpec((m, D), lambda i: (0, i)), pl.BlockSpec((1, D), lambda i: (0, i)),
            whole_s((m, D)), whole_s((1, D)), whole_s((m1, D)), whole_s((1, D)),
        ],
        scratch_shapes=[pltpu.VMEM((items, D), F32)],
        compiler_params=params(24),
        cost_estimate=cost(2 * items * D * D * 20, w.size * 2 + m * 9 * D * 4),
        name="modulation_back",
    )(dmod, w, act, cond, pre, embed, t2, own_act, own_pre, own_embed)


def qkv_kernel(blocks, *refs):
    frames = refs[:blocks]
    mod, w, out, h1_o, h1 = refs[blocks:]
    span = frames[0].shape[0]
    own = 2 * span

    @pl.when(pl.program_id(0) == 0)
    def _():
        shift, scale = mod[0:1, 0:D], mod[0:1, D : 2 * D]
        for i in range(blocks):
            n, unused = norm(frames[i][...].astype(F32))
            h1[pl.ds(i * span, span), :] = (n * (1.0 + scale) + shift).astype(BF16)
        h1_o[...] = h1[0:own, :]

    factor = jnp.where(pl.program_id(0) == 0, SCALE, 1.0)

    @pl.loop(0, blocks * span // own)
    def _(i):
        rows = pl.ds(pl.multiple_of(i * own, own), own)
        out[0, rows, :] = (dot(h1[rows, :], w[...]) * factor).astype(BF16)


def qkv(blocks, mod, w):
    count = len(blocks)
    span = blocks[0].shape[0]
    total = count * span
    whole = lambda a: pl.BlockSpec(a.shape, lambda i: (0, 0))
    return pl.pallas_call(
        functools.partial(qkv_kernel, count),
        grid=(3,),
        out_shape=[sds((3, total, D), BF16), sds((2 * span, D), BF16)],
        in_specs=[whole(b) for b in blocks] + [whole(mod), pl.BlockSpec((D, D), lambda i: (0, i))],
        out_specs=[
            pl.BlockSpec((1, total, D), lambda i: (i, 0, 0)),
            pl.BlockSpec((2 * span, D), lambda i: (0, 0)),
        ],
        scratch_shapes=[pltpu.VMEM((total, D), BF16)],
        compiler_params=params(48),
        cost_estimate=cost(2 * total * D * 3 * D, total * D * 8 + w.size * 2),
        name="qkv",
    )(*blocks, mod, w)


def attend_kernel(q, k, v, o, lse):
    qm = stack_heads(q[0])
    scores = dot_nt(k[0], qm)
    peak = jnp.max(scores, axis=0, keepdims=True)
    weights = jnp.exp(scores - peak)
    total = jnp.sum(weights, axis=0, keepdims=True)
    both = dot(v[0].T, weights.astype(BF16)) * (1.0 / total)
    o[...] = unstack_t(both).astype(BF16)
    lse[0] = peak + jnp.log(total)


def attend(joined, own):
    total = joined.shape[1]
    return pl.pallas_call(
        attend_kernel,
        grid=(PAIRS,),
        out_shape=[sds((own, D), BF16), sds((PAIRS, 1, 2 * own), F32)],
        in_specs=[
            pl.BlockSpec((1, own, 128), lambda i: (0, 0, i)),
            pl.BlockSpec((1, total, 128), lambda i: (1, 0, i)),
            pl.BlockSpec((1, total, 128), lambda i: (2, 0, i)),
        ],
        out_specs=[
            pl.BlockSpec((own, 128), lambda i: (0, i)),
            pl.BlockSpec((1, 1, 2 * own), lambda i: (i, 0, 0)),
        ],
        compiler_params=params(56),
        cost_estimate=cost(16 * own * total * D, total * D * 4, 12 * own * total),
        name="attend",
    )(joined, joined, joined)


def attend_dq_kernel(q, k, v, do, lse, delta, dq):
    qm = stack_heads(q[0])
    dom = stack_heads(do[...])
    probs = jnp.exp(dot_nt(k[0], qm) - lse[0])
    grad = dot_nt(v[0], dom)
    ds = (probs * (grad - delta[0])).astype(BF16)
    dq[...] = (unstack_t(dot(k[0].T, ds)) * SCALE).astype(BF16)


def attend_dq(joined, do, lse, delta):
    own = do.shape[0]
    total = joined.shape[1]
    row = pl.BlockSpec((1, 1, 2 * own), lambda i: (i, 0, 0))
    return pl.pallas_call(
        attend_dq_kernel,
        grid=(PAIRS,),
        out_shape=[sds((own, D), BF16)],
        in_specs=[
            pl.BlockSpec((1, own, 128), lambda i: (0, 0, i)),
            pl.BlockSpec((1, total, 128), lambda i: (1, 0, i)),
            pl.BlockSpec((1, total, 128), lambda i: (2, 0, i)),
            pl.BlockSpec((own, 128), lambda i: (0, i)),
            row, row,
        ],
        out_specs=[pl.BlockSpec((own, 128), lambda i: (0, i))],
        compiler_params=params(56),
        cost_estimate=cost(24 * own * total * D, total * D * 4, 12 * own * total),
        name="attend_dq",
    )(joined, joined, joined, do, lse, delta)[0]


def attend_dkv_kernel(chunks, *refs):
    q, k, v = refs[:3]
    do = refs[3 : 3 + chunks]
    lse = refs[3 + chunks : 3 + 2 * chunks]
    delta = refs[3 + 2 * chunks : 3 + 3 * chunks]
    out = refs[-1]
    keys, values = k[0], v[0]
    own = keys.shape[0]
    dk = jnp.zeros((own, 128), F32)
    dv = jnp.zeros((own, 128), F32)
    for i in range(chunks):
        qm = stack_heads(q[0, i * own : (i + 1) * own, :])
        dom = stack_heads(do[i][...])
        probs = jnp.exp(dot_nt(keys, qm) - lse[i][0])
        dv += dot(probs.astype(BF16), dom)
        grad = dot_nt(values, dom)
        ds = (probs * (grad - delta[i][0])).astype(BF16)
        dk += dot(ds, qm)
    out[0] = dk.astype(BF16)
    out[1] = dv.astype(BF16)


def attend_dkv(joined, do, lse, delta):
    own = do[0].shape[0]
    chunks = len(do)
    total = joined.shape[1]
    row = pl.BlockSpec((1, 1, 2 * own), lambda i: (i, 0, 0))
    return pl.pallas_call(
        functools.partial(attend_dkv_kernel, chunks),
        grid=(PAIRS,),
        out_shape=[sds((2, own, D), BF16)],
        in_specs=[
            pl.BlockSpec((1, total, 128), lambda i: (0, 0, i)),
            pl.BlockSpec((1, own, 128), lambda i: (1, 0, i)),
            pl.BlockSpec((1, own, 128), lambda i: (2, 0, i)),
        ]
        + [pl.BlockSpec((own, 128), lambda i: (0, i))] * chunks
        + [row] * (2 * chunks),
        out_specs=[pl.BlockSpec((2, own, 128), lambda i: (0, 0, i))],
        compiler_params=params(56),
        cost_estimate=cost(32 * own * total * D, total * D * 4, 12 * own * total),
        name="attend_dkv",
    )(joined, joined, joined, *do, *lse, *delta)[0]


def caption_kernel(blocks, *refs):
    caps = refs[:blocks]
    w, cap_o, out = refs[blocks:]
    rows = caps[0].shape[0]
    for i in range(blocks):
        cap_o[i * rows : (i + 1) * rows, :] = caps[i][...]
    out[...] = dot(cap_o[...], w[...]).astype(BF16)


def middle_kernel(fa, fb, o, mod, wo, wq, kv2, offset, wc,
                  x1_o, x2_o, attn_o, attn2_o, h2_o, q2_o, h3_o, o2_o, p2_o):
    gate1, shift2, scale2, gate2, shift3, scale3 = (mod[0:1, i * D : (i + 1) * D] for i in range(2, 8))
    start = jnp.concatenate([fa[...], fb[...]], axis=0).astype(F32)
    attn = dot(o[...], wo[...])
    attn_o[...] = attn.astype(BF16)
    x1 = start + gate1 * attn
    x1_o[...] = x1
    n2, unused = norm(x1)
    h2 = (n2 * (1.0 + scale2) + shift2).astype(BF16)
    h2_o[...] = h2
    q2_o[...] = (dot(h2, wq[...]) * SCALE).astype(BF16)
    for i in range(PAIRS):
        qm = stack_heads(q2_o[:, cols(i)])
        scores = dot_nt(kv2[:, cols(i)], qm) + offset[...]
        peak = jnp.max(scores, axis=0, keepdims=True)
        weights = jnp.exp(scores - peak)
        probs = (weights * (1.0 / jnp.sum(weights, axis=0, keepdims=True))).astype(BF16)
        p2_o[i] = probs
        both = dot(kv2[:, D + i * 128 : D + (i + 1) * 128].T, probs)
        o2_o[:, cols(i)] = unstack_t(both).astype(BF16)
    attn2 = dot(o2_o[...], wc[...])
    attn2_o[...] = attn2.astype(BF16)
    x2 = x1 + gate2 * attn2
    x2_o[...] = x2
    n3, unused = norm(x2)
    h3_o[...] = (n3 * (1.0 + scale3) + shift3).astype(BF16)


def gelu_both(u):
    c = math.sqrt(2.0 / math.pi)
    square = u * u
    t = jnp.tanh(c * u * (1.0 + 0.044715 * square))
    half = 0.5 * (1.0 + t)
    slope = half + 0.5 * u * (1.0 - t * t) * (c * (1.0 + 3 * 0.044715 * square))
    return u * half, slope


def mlp_kernel(steps, h3, ca, cb, mod, x2, up, up_b, down, down_b,
               wide_o, narrow_o, out_o, dx2_o, sums_o, upb_o, low, dh3, dl):
    step = pl.program_id(0)
    gate3 = mod[0:1, 8 * D : 9 * D]

    @pl.when(step == 0)
    def _():
        dy = jnp.concatenate([ca[...], cb[...]], axis=0).astype(F32)
        dl[...] = (gate3 * dy).astype(BF16)
        low[...] = jnp.zeros_like(low)
        dh3[...] = jnp.zeros_like(dh3)

    upper = dot(h3[...], up[...]) + up_b[...].astype(F32)
    acted, slope = gelu_both(upper)
    acted = acted.astype(BF16)
    wide_o[0, 0] = acted
    low[...] += dot(acted, down[...])
    dupper = (slope * dot_nt(dl[...], down[...])).astype(BF16)
    wide_o[1, 0] = dupper
    upb_o[...] = colsum(dupper.astype(F32))
    dh3[...] += dot_nt(dupper, up[...])

    @pl.when(step == steps - 1)
    def _():
        dy = jnp.concatenate([ca[...], cb[...]], axis=0).astype(F32)
        scale3 = mod[0:1, 7 * D : 8 * D]
        lower = low[...] + down_b[...].astype(F32)
        value = x2[...]
        out_o[...] = (value + gate3 * lower).astype(BF16)
        narrow_o[0] = h3[...]
        narrow_o[1] = dl[...]
        n3, rstd = norm(value)
        back = dh3[...]
        sums_o[0:1, :] = colsum(back)
        sums_o[1:2, :] = colsum(n3 * back)
        sums_o[2:3, :] = colsum(lower * dy)
        sums_o[3:4, :] = colsum(dl[...].astype(F32))
        dx2_o[...] = dy + norm_back(n3, rstd, (1.0 + scale3) * back)


def mlp(h3, ca, cb, mod, x2, up, up_b, down, down_b):
    rows = h3.shape[0]
    steps = FF // D
    whole = lambda a: pl.BlockSpec(a.shape, lambda i: (0,) * len(a.shape))
    outs = [
        sds((2, steps, rows, D), BF16), sds((2, rows, D), BF16), sds((rows, D), BF16),
        sds((rows, D), F32), sds((4, D), F32), sds((1, FF), F32),
    ]
    return pl.pallas_call(
        functools.partial(mlp_kernel, steps),
        grid=(steps,),
        out_shape=outs,
        in_specs=[
            whole(h3), whole(ca), whole(cb), whole(mod), whole(x2),
            pl.BlockSpec((D, D), lambda i: (0, i)),
            pl.BlockSpec((1, D), lambda i: (0, i)),
            pl.BlockSpec((D, D), lambda i: (i, 0)),
            whole(down_b),
        ],
        out_specs=[pl.BlockSpec((2, 1, rows, D), lambda i: (0, i, 0, 0))]
        + [whole(o) for o in outs[1:5]]
        + [pl.BlockSpec((1, D), lambda i: (0, i))],
        scratch_shapes=[pltpu.VMEM((rows, D), F32), pltpu.VMEM((rows, D), F32), pltpu.VMEM((rows, D), BF16)],
        compiler_params=params(48),
        cost_estimate=cost(10 * rows * D * FF, 4 * D * FF + rows * D * 40, rows * FF),
        name="mlp",
    )(h3, ca, cb, mod, x2, up, up_b, down, down_b)


def back_kernel(dx2, mod, attn2, wc, p2, q2, kv2, wq, x1, attn, wo, o, h2, o2, h1, wkv,
                fac_o, dx1_o, do_o, delta_o, sums_o, dcap_o):
    gate1 = mod[0:1, 2 * D : 3 * D]
    scale2 = mod[0:1, 4 * D : 5 * D]
    gate2 = mod[0:1, 5 * D : 6 * D]
    dx2 = dx2[...]
    sums_o[2:3, :] = colsum(attn2[...].astype(F32) * dx2)
    da2 = (gate2 * dx2).astype(BF16)
    fac_o[3] = da2
    do2 = dot_nt(da2, wc[...]).astype(BF16)
    for i in range(PAIRS):
        qm = stack_heads(q2[:, cols(i)])
        dom = stack_heads(do2[:, cols(i)])
        keys, values = kv2[:, cols(i)], kv2[:, D + i * 128 : D + (i + 1) * 128]
        probs = p2[i]
        fac_o[5, :, cols(i)] = dot(probs, dom).astype(BF16)
        probs = probs.astype(F32)
        grad = dot_nt(values, dom)
        ds = (probs * (grad - colsum(probs * grad))).astype(BF16)
        fac_o[1, :, cols(i)] = (unstack_t(dot(keys.T, ds)) * SCALE).astype(BF16)
        fac_o[4, :, cols(i)] = dot(ds, qm).astype(BF16)
    fac_o[0] = h2[...]
    fac_o[2] = o2[...]
    dh2 = dot_nt(fac_o[1], wq[...])
    value = x1[...]
    n2, rstd = norm(value)
    sums_o[0:1, :] = colsum(dh2)
    sums_o[1:2, :] = colsum(n2 * dh2)
    dx1 = dx2 + norm_back(n2, rstd, (1.0 + scale2) * dh2)
    dx1_o[...] = dx1
    sums_o[3:4, :] = colsum(attn[...].astype(F32) * dx1)
    da = (gate1 * dx1).astype(BF16)
    fac_o[6] = da
    fac_o[7] = o[...]
    fac_o[8] = h1[...]
    do = dot_nt(da, wo[...]).astype(BF16)
    do_o[...] = do
    both = do.astype(F32) * o[...].astype(F32)
    rows = both.shape[0]
    for i in range(PAIRS):
        t = both[:, cols(i)].T
        delta_o[i, :, 0:rows] = colsum(t[:HEAD])
        delta_o[i, :, rows:] = colsum(t[HEAD:])
    dcap_o[...] = (
        dot_nt(fac_o[4], wkv[:, 0:D]) + dot_nt(fac_o[5], wkv[:, D : 2 * D])
    ).astype(BF16)


def last_kernel(dq, dkv, w, fa, fb, mod, dx1, own_o, other_o, sums_o):
    scale1 = mod[0:1, D : 2 * D]
    dh1 = dot_nt(dq[...], w[:, 0:D]) + dot_nt(dkv[0], w[:, D : 2 * D]) + dot_nt(dkv[1], w[:, 2 * D :])
    start = jnp.concatenate([fa[...], fb[...]], axis=0).astype(F32)
    n1, rstd = norm(start)
    sums_o[0:1, :] = colsum(dh1)
    sums_o[1:2, :] = colsum(n1 * dh1)
    grad = dx1[...] + norm_back(n1, rstd, (1.0 + scale1) * dh1)
    span = fa.shape[0]
    own_o[...] = grad[:span]
    other_o[...] = grad[span:].astype(BF16)


def pick_rows(info, x):
    source = lax.broadcasted_iota(jnp.int32, (D, D // 2), 0)
    column = lax.broadcasted_iota(jnp.int32, (D, D // 2), 1)
    block = sum((column >= 96 * i).astype(jnp.int32) for i in (1, 2, 3))
    wanted = 96 * jnp.bitwise_xor(info[1], 2 * block) + column - 96 * block
    choose = (source == wanted).astype(F32).astype(BF16)
    return dot(x, choose).astype(BF16)


def emit(first, info, tiles, send_o, keep_o):
    kept = 0
    sent = 0
    for r in range(4):
        block = tiles[jnp.bitwise_xor(info[0], r)]
        if r & first:
            send_o[sent] = block
            sent += 1
        else:
            keep_o[kept] = block
            kept += 1


def down_grad_kernel(info, wide, wide_p, narrow, narrow_p, send_o, keep_o, tiles):
    for e in range(4):
        owner = jnp.bitwise_xor(info[1], 2 * e)
        half = pl.multiple_of(lax.rem(owner, 2) * 384, 128)
        where = (0, lax.div(owner, 2), slice(None), pl.ds(half, 384))
        grad = dot_tn(wide[where], narrow[1]) + dot_tn(wide_p[where], narrow_p[1])
        for q in range(4):
            tiles[q, e] = grad[96 * q : 96 * (q + 1)].astype(BF16)
    emit(1, info, tiles, send_o, keep_o)


def put(tiles, q, grad):
    for e in range(4):
        tiles[q, e] = grad[96 * e : 96 * (e + 1)].astype(BF16)


def up_grad_kernel(info, wide, wide_p, narrow, narrow_p, send_o, keep_o, tiles):
    x, xp = pick_rows(info, narrow[0]), pick_rows(info, narrow_p[0])
    for q in range(4):
        put(tiles, q, dot_tn(x, wide[1, q]) + dot_tn(xp, wide_p[1, q]))
    emit(2, info, tiles, send_o, keep_o)


def cross_grad_kernel(info, cap, fac, fac_p, send_o, keep_o, tiles):
    def pair(x, y):
        return dot_tn(pick_rows(info, fac[x]), fac[y]) + dot_tn(pick_rows(info, fac_p[x]), fac_p[y])

    put(tiles, 0, pair(0, 1))
    put(tiles, 3, pair(2, 3))
    x = pick_rows(info, cap[...])
    rows = x.shape[0] // 4
    xp = jnp.concatenate([x[rows * i : rows * (i + 1)] for i in (1, 0, 3, 2)], axis=0)
    for q in (1, 2):
        put(tiles, q, dot_tn(x, fac[q + 3]) + dot_tn(xp, fac_p[q + 3]))
    emit(1, info, tiles, send_o, keep_o)


def attn_grad_kernel(info, fac, fac_p, dq, dq_p, dkv, dkv_p, send_o, keep_o, tiles):
    x, xp = pick_rows(info, fac[8]), pick_rows(info, fac_p[8])
    put(tiles, 0, dot_tn(x, dq[...]) + dot_tn(xp, dq_p[...]))
    for q in (1, 2):
        put(tiles, q, dot_tn(x, dkv[q - 1]) + dot_tn(xp, dkv_p[q - 1]))
    put(tiles, 3, dot_tn(pick_rows(info, fac[7]), fac[6]) + dot_tn(pick_rows(info, fac_p[7]), fac_p[6]))
    emit(2, info, tiles, send_o, keep_o)


def grad_call(kernel, info, args, name):
    outs = [sds((2, 4, 96, D), BF16)] * 2
    nbytes = sum(a.size * 2 for a in args) + 4 * 4 * 96 * D * 2
    return pl.pallas_call(
        kernel,
        out_shape=outs,
        in_specs=[smem()] + [vmem()] * len(args),
        out_specs=[vmem()] * 2,
        scratch_shapes=[pltpu.VMEM((4, 4, 96, D), BF16)],
        compiler_params=params(48),
        cost_estimate=cost(2 * 512 * 1536 * D, nbytes),
        name=name,
    )(info, *args)


def add_first_kernel(keep, recv, keep_o, send_o):
    keep_o[...] = (keep[0].astype(F32) + recv[0].astype(F32)).astype(BF16)
    send_o[...] = (keep[1].astype(F32) + recv[1].astype(F32)).astype(BF16)


def add_second_kernel(ka, ra, kb, rb, keep_o, s1_o, s2_o, s3_o):
    for g, (keep, recv) in enumerate(((ka, ra), (kb, rb))):
        for e, out in enumerate((keep_o, s1_o, s2_o, s3_o)):
            out[g] = (keep[e].astype(F32) + recv[e].astype(F32)).astype(BF16)


def add_third_kernel(k, r1, r2, r3, out):
    out[...] = (
        k[...].astype(F32) + r1[...].astype(F32) + r2[...].astype(F32) + r3[...].astype(F32)
    ).astype(BF16)


def swap(x, axis, size, k):
    return lax.ppermute(x, axis, [(i, i ^ k) for i in range(size)])


def reduce_pair(first, second, finish_kernel, outs, info, name):
    ra = swap(first[0], "band", 4, 1)
    rb = swap(second[0], "band", 4, 2)
    half = sds((4, 96, D), BF16)
    ka, sa = call(add_first_kernel, [half, half], [first[1], ra], 24, name=name + "_add1x")
    kb, sb = call(add_first_kernel, [half, half], [second[1], rb], 24, name=name + "_add1y")
    ra = swap(sa, "band", 4, 2)
    rb = swap(sb, "band", 4, 1)
    both = sds((2, 96, D), BF16)
    keep, s1, s2, s3 = call(add_second_kernel, [both] * 4, [ka, ra, kb, rb], 24, name=name + "_add2")
    r1, r2, r3 = swap(s1, "seq", 8, 2), swap(s2, "seq", 8, 4), swap(s3, "seq", 8, 6)
    done = call(add_third_kernel, [both], [keep, r1, r2, r3], 24, name=name + "_add3")[0]
    others = [swap(done, "band", 4, t) for t in (1, 2, 3)]
    args = [info, done, *others]
    return call(finish_kernel, outs, args, 24, name=name + "_finish", in_specs=[smem()] + [vmem()] * 4)


def mlp_finish_kernel(info, t0, t1, t2, t3, down_o, up_o):
    for r, tile in enumerate((t0, t1, t2, t3)):
        q = jnp.bitwise_xor(info[0], r)
        down_o[pl.ds(pl.multiple_of(96 * q, 96), 96), :] = tile[0].astype(F32)
        up_o[:, pl.ds(pl.multiple_of(D * q, D), D)] = tile[1].astype(F32)


def attn_finish_kernel(info, t0, t1, t2, t3, cq_o, ckv_o, co_o, in_o, out_o, *unused):
    for r, tile in enumerate((t0, t1, t2, t3)):
        q = jnp.bitwise_xor(info[0], r)

        @pl.when(q == 0)
        def _():
            cq_o[...] = tile[0].astype(F32)
            in_o[:, 0:D] = tile[1].astype(F32)

        @pl.when(q == 1)
        def _():
            ckv_o[:, 0:D] = tile[0].astype(F32)
            in_o[:, D : 2 * D] = tile[1].astype(F32)

        @pl.when(q == 2)
        def _():
            ckv_o[:, D:] = tile[0].astype(F32)
            in_o[:, 2 * D :] = tile[1].astype(F32)

        @pl.when(q == 3)
        def _():
            co_o[...] = tile[0].astype(F32)
            out_o[...] = tile[1].astype(F32)


def plain_reduce(x, y, owners):
    grad = lax.psum_scatter(dot_tn(x, y).astype(BF16), "seq", scatter_dimension=0, tiled=True)
    return lax.psum(grad, "band").astype(F32)


def on_device(bands, seqs, frames, caption, timesteps, cap_len, attn_in, attn_out, cross_query,
              cross_keyval, cross_out, mlp_up, up_bias, mlp_down, down_bias, ada_weight, ada_bias,
              time_first, first_bias, time_second, second_bias, cotangent):
    span = frames.shape[1]
    own = 2 * span
    cap_rows = caption.shape[1]
    items = timesteps.shape[0]
    halves = seqs // 2
    band = lax.axis_index("band")
    seq = lax.axis_index("seq")
    half = (seq >= halves).astype(jnp.int32)
    item = 2 * band + half
    info = jnp.stack([band, seq]).astype(jnp.int32)

    def mine(x):
        return jnp.where(half == 0, x[0], x[1])

    def theirs(x):
        return jnp.where(half == 0, x[1], x[0])

    def whole_item(x):
        same, other = mine(x), theirs(x)
        block = {0: same}
        for k in range(2, seqs, 2):
            block[k] = swap(same if k < halves else other, "seq", seqs, k)
        block[halves] = block[halves] if halves % 2 == 0 else swap(other, "seq", seqs, halves)
        for k in range(0, seqs, 2):
            block[k + 1] = swap(block[k], "seq", seqs, 1)
        order = [k for i in range(halves) for k in (i, i + halves)]
        return [block[k] for k in order], order

    blocks, order = whole_item(frames)
    cot_own = mine(cotangent)
    cot_other = swap(theirs(cotangent), "seq", seqs, halves)
    caps, unused = whole_item(caption)

    steps = jnp.take(timesteps, jnp.bitwise_xor(jnp.arange(items), item))
    width = time_first.shape[0] // 2
    freq = jnp.exp(-math.log(10000.0) * jnp.arange(width, dtype=F32) / width)
    angle = steps.astype(F32)[:, None] * freq[None, :]
    embed = jnp.concatenate([jnp.cos(angle), jnp.sin(angle)], axis=1)
    row = lambda v: v.reshape(1, -1)
    pre, cond, mod = modulation(
        embed, time_first, row(first_bias), time_second, row(second_bias), ada_weight, row(ada_bias)
    )

    joined, h1 = qkv(blocks, mod, attn_in)
    mixed, lse = attend(joined, own)

    cap_total = seqs * cap_rows
    cap_all, kv2 = call(
        functools.partial(caption_kernel, seqs),
        [sds((cap_total, D), BF16), sds((cap_total, 2 * D), BF16)],
        [*caps, cross_keyval], 24, flops=4 * cap_total * D * D, name="caption_keyval",
    )
    token = jnp.concatenate([jnp.bitwise_xor(seq, k) * cap_rows + jnp.arange(cap_rows) for k in order])
    length = lax.dynamic_index_in_dim(cap_len, item, keepdims=False)
    offset = jnp.where(token < length, 0.0, NEGATIVE).astype(F32)[:, None]

    wide = sds((own, D), F32)
    thin = sds((own, D), BF16)
    x1, x2, attn, attn2, h2, q2, h3, o2, p2 = call(
        middle_kernel,
        [wide, wide, thin, thin, thin, thin, thin, thin, sds((PAIRS, cap_total, 2 * own), BF16)],
        [blocks[0], blocks[1], mixed, mod, attn_out, cross_query, kv2, offset, cross_out],
        48, flops=2 * own * D * D * 3 + 16 * own * cap_total * D, name="middle",
    )

    big, small, out, dx2, sums3, sums_up = mlp(
        h3, cot_own, cot_other, mod, x2, mlp_up, row(up_bias), mlp_down, row(down_bias)
    )
    out_back = swap(out[span:], "seq", seqs, halves)

    fast = bands == 4 and seqs == 8
    if fast:
        big_p, small_p = swap(big, "seq", seqs, 1), swap(small, "seq", seqs, 1)

    fac, dx1, do, delta, sums2, dcap = call(
        back_kernel,
        [sds((9, own, D), BF16), wide, thin, sds((PAIRS, 1, 2 * own), F32), sds((4, D), F32),
         sds((cap_total, D), BF16)],
        [dx2, mod, attn2, cross_out, p2, q2, kv2, cross_query, x1, attn, attn_out, mixed, h2, o2, h1,
         cross_keyval],
        56, flops=2 * own * D * D * 4 + 40 * own * cap_total * D, name="back",
    )

    stats = jnp.concatenate([lse, delta], axis=1)
    got, got_stats = {0: do}, {0: stats}
    for k in range(2, halves, 2):
        got[k], got_stats[k] = swap(do, "seq", seqs, k), swap(stats, "seq", seqs, k)
    for k in range(0, halves, 2):
        got[k + 1], got_stats[k + 1] = swap(got[k], "seq", seqs, 1), swap(got_stats[k], "seq", seqs, 1)

    dq = attend_dq(joined, do, lse, delta)

    if fast:
        down_g = grad_call(down_grad_kernel, info, [big, big_p, small, small_p], "down_grad")
        up_g = grad_call(up_grad_kernel, info, [big, big_p, small, small_p], "up_grad")
        g_down, g_up = reduce_pair(
            down_g, up_g, mlp_finish_kernel, [sds((384, D), F32), sds((96, FF), F32)], info, "mlp"
        )
        fac_p = swap(fac, "seq", seqs, 1)
        cross_g = grad_call(cross_grad_kernel, info, [cap_all, fac, fac_p], "cross_grad")

    dkv = attend_dkv(
        joined,
        [got[k] for k in range(halves)],
        [got_stats[k][:, 0:1] for k in range(halves)],
        [got_stats[k][:, 1:2] for k in range(halves)],
    )
    grad_own, grad_other, sums1 = call(
        last_kernel,
        [sds((span, D), F32), sds((span, D), BF16), sds((2, D), F32)],
        [dq, dkv, attn_in, blocks[0], blocks[1], mod, dx1],
        48, flops=6 * own * D * D, name="last",
    )
    grad_back = swap(grad_other, "seq", seqs, halves).astype(F32)

    def place(kept, received):
        return jnp.where(half == 0, jnp.stack([kept, received]), jnp.stack([received, kept]))

    out = place(out[:span], out_back)
    grad_frames = place(grad_own, grad_back)

    if fast:
        dq_p, dkv_p = swap(dq, "seq", seqs, 1), swap(dkv, "seq", seqs, 1)
        attn_g = grad_call(attn_grad_kernel, info, [fac, fac_p, dq, dq_p, dkv, dkv_p], "attn_grad")
        one = sds((96, D), F32)
        g_cq, g_ckv, g_co, g_in, g_out = reduce_pair(
            cross_g, attn_g, attn_finish_kernel,
            [one, sds((96, 2 * D), F32), one, sds((96, 3 * D), F32), one], info, "attn",
        )
    else:
        acted = jnp.concatenate([big[0, i] for i in range(FF // D)], axis=1)
        dupper = jnp.concatenate([big[1, i] for i in range(FF // D)], axis=1)
        g_down = plain_reduce(acted, small[1], seqs)
        g_up = plain_reduce(h3, dupper, seqs)
        g_cq = plain_reduce(h2, fac[1], seqs)
        g_ckv = plain_reduce(cap_all, jnp.concatenate([fac[4], fac[5]], axis=1), seqs)
        g_co = plain_reduce(o2, fac[3], seqs)
        g_out = plain_reduce(mixed, fac[6], seqs)
        g_in = plain_reduce(h1, jnp.concatenate([dq, dkv[0], dkv[1]], axis=1), seqs)

    dcap = {k: dcap[i * cap_rows : (i + 1) * cap_rows] for i, k in enumerate(order)}
    odd = swap(jnp.stack([dcap[k] for k in range(1, seqs, 2)]), "seq", seqs, 1)
    even = {k: dcap[k].astype(F32) + odd[k // 2].astype(F32) for k in range(0, seqs, 2)}
    same, other = even[0], 0.0
    for k in range(2, seqs, 2):
        part = swap(even[k].astype(BF16), "seq", seqs, k).astype(F32)
        if k < halves:
            same = same + part
        else:
            other = other + part
    grad_caption = place(same, other)

    def spread(rows, biases):
        packed = rows if biases is None else jnp.concatenate([rows, biases])
        k = 1
        while k < halves:
            packed = packed + swap(packed, "seq", seqs, k)
            k *= 2
        away = swap(packed, "seq", seqs, halves)
        n = rows.shape[0]
        both = jnp.stack([packed[:n], away[:n]])
        if biases is None:
            return [both] + [swap(both, "band", bands, t) for t in range(1, bands)], None
        flat = jnp.concatenate([both.reshape(2 * n, D), packed[n:] + away[n:]])
        all_flat = [flat] + [swap(flat, "band", bands, t) for t in range(1, bands)]
        return [f[: 2 * n].reshape(2, n, D) for f in all_flat], sum(f[2 * n :] for f in all_flat)

    late, unused = spread(sums1, None)
    early, bias_sums = spread(
        jnp.concatenate([sums2[3:4], sums2[0:3], sums3[0:3]]),
        jnp.concatenate([sums3[3:4], sums_up.reshape(FF // D, D)]),
    )
    dmod = jnp.concatenate(
        [jnp.concatenate(late, axis=0), jnp.concatenate(early, axis=0)], axis=1
    ).reshape(items, 9 * D)

    act, act_pre = silu(cond), silu(pre)

    def own_rows(v):
        size = v.shape[1] // seqs
        return lax.dynamic_slice_in_dim(v, seq * size, size, axis=1)

    g_ada, gb_ada, g_t2, gb_t2, g_t1, gb_t1 = mod_back(
        dmod, ada_weight, act, cond, pre, embed, time_second,
        own_rows(act).T, own_rows(act_pre).T, own_rows(embed).T,
    )
    gb_down = own_rows(bias_sums[0:1])
    gb_up = own_rows(bias_sums[1:].reshape(1, FF))
    flat = lambda v: v.reshape(-1)
    return (
        out, grad_frames, grad_caption, g_in, g_out, g_cq, g_ckv, g_co, g_up, flat(gb_up), g_down,
        flat(gb_down), g_ada, flat(own_rows(gb_ada)), g_t1, flat(own_rows(gb_t1)), g_t2,
        flat(own_rows(gb_t2)),
    )


def solution(mesh):
    split = P("band", "seq", None)
    rows, flat = P("seq", None), P("seq")
    return jax.shard_map(
        functools.partial(on_device, mesh.shape["band"], mesh.shape["seq"]),
        mesh=mesh,
        in_specs=(split, split) + (P(),) * 17 + (split,),
        out_specs=(split, split, split, rows, rows, rows, rows, rows, rows, flat, rows, flat, rows, flat,
                   rows, flat, rows, flat),
        check_vma=False,
    )
```

```python
import functools
import math

import jax
import jax.numpy as jnp
from jax import lax
from jax.experimental import pallas as pl
from jax.experimental.pallas import tpu as pltpu
from jax.sharding import PartitionSpec as P

D = 768
HEAD = 64
PAIRS = 6
FF = 3072
EPSILON = 1e-06
NEGATIVE = -1e30
SCALE = 0.125
F32 = jnp.float32
BF16 = jnp.bfloat16
MIB = 1 << 20
MODMIB = 10


def dot(a, b):
    return jnp.dot(a, b, preferred_element_type=F32)


def dot_nt(a, b):
    return lax.dot_general(a, b, (((1,), (1,)), ((), ())), preferred_element_type=F32)


def dot_tn(a, b):
    return lax.dot_general(a, b, (((0,), (0,)), ((), ())), preferred_element_type=F32)


def split_dot(x, w, contract=0):
    high = x.astype(BF16).astype(F32)
    both = jnp.concatenate([high, x - high], axis=0).astype(BF16)
    out = lax.dot_general(
        both, w, (((1,), (contract,)), ((), ())), preferred_element_type=F32
    )
    return out[: x.shape[0]] + out[x.shape[0] :]


def silu(v):
    return v * (1.0 / (1.0 + jnp.exp(-v)))


def silu_grad(v):
    s = 1.0 / (1.0 + jnp.exp(-v))
    return s * (1.0 + v * (1.0 - s))


def norm(v):
    mean = jnp.mean(v, axis=-1, keepdims=True)
    centred = v - mean
    spread = jnp.mean(centred * centred, axis=-1, keepdims=True)
    rstd = lax.rsqrt(spread + EPSILON)
    return centred * rstd, rstd


def norm_back(n, rstd, w):
    return (
        w - jnp.mean(w, axis=-1, keepdims=True) - n * jnp.mean(w * n, axis=-1, keepdims=True)
    ) * rstd


def colsum(v):
    return jnp.sum(v, axis=0, keepdims=True)


def cols(i):
    return slice(i * 128, (i + 1) * 128)


def head_masks():
    lane = lax.broadcasted_iota(jnp.int32, (1, 128), 1)
    first = (lane < HEAD).astype(F32)
    return first.astype(BF16), (1.0 - first).astype(BF16)


def stack_heads(block):
    first, second = head_masks()
    return jnp.concatenate([block * first, block * second], axis=0)


def unstack_t(both):
    rows = both.shape[1] // 2
    pair = jnp.concatenate([both[:HEAD, :rows], both[HEAD:, rows:]], axis=0)
    return pair.T


def sds(shape, dtype):
    return jax.ShapeDtypeStruct(shape, dtype)


def vmem():
    return pl.BlockSpec(memory_space=pltpu.VMEM)


def smem():
    return pl.BlockSpec(memory_space=pltpu.SMEM)


def whole(a):
    return pl.BlockSpec(a.shape, lambda *i: (0,) * len(a.shape))


class Chain:
    def __init__(self):
        self.token = None

    def __call__(self, kernel, outs, args, mib, name, grid=None, in_specs=None, out_specs=None, scratch=()):
        outs = list(outs)
        in_specs = list(in_specs or [vmem()] * len(args))
        out_specs = list(out_specs or [vmem()] * len(outs))
        count = len(args)
        body = kernel
        if self.token is not None:
            args = [*args, self.token]
            in_specs.append(pl.BlockSpec(memory_space=pl.ANY))
            body = lambda *refs: kernel(*refs[:count], *refs[count + 1 :])
        results = pl.pallas_call(
            body,
            **({} if grid is None else {"grid": grid}),
            out_shape=outs,
            in_specs=in_specs,
            out_specs=out_specs,
            scratch_shapes=list(scratch),
            compiler_params=pltpu.CompilerParams(vmem_limit_bytes=mib * MIB),
            cost_estimate=pl.CostEstimate(flops=1000, bytes_accessed=1000, transcendentals=0),
            name=name,
        )(*args)
        self.token = min(results, key=lambda r: r.size * r.dtype.itemsize)
        return results

    def after(self, x):
        self.token = x


def room(mib, frames):
    return min(56, mib * max(1, frames // 1024))


def pick_kernel(info, *refs):
    half = info[2]
    parts, (mine_o, theirs_o, sems) = refs[:-3], refs[-3:]
    copies = []
    at = 0
    for x in parts:
        rows = pl.ds(at, x.shape[1])
        for source, out in ((half, mine_o), (1 - half, theirs_o)):
            copies.append(pltpu.make_async_copy(x.at[source], out.at[rows], sems.at[len(copies)]))
        at += x.shape[1]
    for copy in copies:
        copy.start()
    for copy in copies:
        copy.wait()


def pick(chain, info, *parts):
    out = sds((sum(x.shape[1] for x in parts), D), BF16)
    anywhere = pl.BlockSpec(memory_space=pl.ANY)
    return chain(
        pick_kernel, [out, out], [info, *parts], 4, "pick", in_specs=[smem()] + [anywhere] * len(parts),
        out_specs=[anywhere] * 2, scratch=[pltpu.SemaphoreType.DMA((2 * len(parts),))],
    )


def stack_kernel(*refs):
    for i, ref in enumerate(refs[:-1]):
        refs[-1][i] = ref[...]


def stack(chain, arrays, name):
    out = sds((len(arrays),) + arrays[0].shape, arrays[0].dtype)
    return chain(stack_kernel, [out], arrays, 4, name)[0]


def place_kernel(info, *refs):
    count = len(refs) // 3
    for i in range(count):
        kept, received, out = refs[2 * i], refs[2 * i + 1], refs[2 * count + i]
        out[info[2]] = kept[...].astype(out.dtype)
        out[1 - info[2]] = received[...].reshape(kept.shape).astype(out.dtype)


def place(chain, info, pairs, dtypes, name):
    args, specs = [info], [smem()]
    for kept, received in pairs:
        args.append(kept)
        specs.append(whole(kept))
        if isinstance(received, tuple):
            args.append(received[0])
            specs.append(pl.BlockSpec((1,) + kept.shape, functools.partial(lambda at, i: (at, 0, 0), received[1])))
        else:
            args.append(received)
            specs.append(whole(received))
    outs = [sds((2,) + kept.shape, dtype) for (kept, unused), dtype in zip(pairs, dtypes)]
    return chain(
        place_kernel, outs, args, 8, name, grid=(1,), in_specs=specs, out_specs=[whole(o) for o in outs]
    )


def mod_kernel(embed, t1, b1, t2, b2, w, b, both_o, mod_o, act):
    @pl.when(pl.program_id(0) == 0)
    def _():
        pre = split_dot(embed[...], t1[...]) + b1[...].astype(F32)
        cond = split_dot(silu(pre), t2[...]) + b2[...].astype(F32)
        both_o[0] = pre
        both_o[1] = cond
        act[...] = silu(cond)

    mod_o[...] = split_dot(act[...], w[...]) + b[...].astype(F32)


def modulation(chain, embed, t1, b1, t2, b2, w, b):
    items = embed.shape[0]
    outs = [sds((2, items, D), F32), sds((items, 9 * D), F32)]
    return chain(
        mod_kernel, outs, [embed, t1, b1, t2, b2, w, b], MODMIB, "modulation", grid=(9,),
        in_specs=[whole(v) for v in (embed, t1, b1, t2, b2)]
        + [pl.BlockSpec((D, D), lambda i: (0, i)), pl.BlockSpec((1, D), lambda i: (0, i))],
        out_specs=[whole(outs[0]), pl.BlockSpec((items, D), lambda i: (0, i))],
        scratch=[pltpu.VMEM((items, D), F32)],
    )


def outer_sum(left_t, right):
    lh = left_t.astype(BF16)
    ll = (left_t - lh.astype(F32)).astype(BF16)
    rh = right.astype(BF16)
    rl = (right - rh.astype(F32)).astype(BF16)
    return dot(lh, rh) + dot(ll, rh) + dot(lh, rl)


def own_rows_t(info, size, v):
    row = lax.broadcasted_iota(jnp.int32, (size, v.shape[1]), 0)
    column = lax.broadcasted_iota(jnp.int32, (size, v.shape[1]), 1)
    choose = (column == row + size * info[1]).astype(F32).astype(BF16)
    high = v.astype(BF16)
    rest = (v - high.astype(F32)).astype(BF16)
    return dot_nt(choose, high) + dot_nt(choose, rest)


def mod_back_kernel(bands, info, *refs):
    sums = refs[:bands]
    w, both, embed, t2, g_ada, gb_ada, g_t2, gb_t2, g_t1, gb_t1, gb_o, acc, dmod, own_act = refs[bands:]
    step = pl.program_id(0)

    @pl.when(step == 0)
    def _():
        acc[...] = jnp.zeros_like(acc)
        own_act[...] = own_rows_t(info, own_act.shape[0], silu(both[1]))
        bias = jnp.zeros(gb_o.shape, F32)
        for t in range(bands):
            held = sums[t][sums[t].shape[0] - 32 :, :].astype(F32)
            for u in range(2):
                r = 2 * t + u
                for p in range(9):
                    dmod[p, r : r + 1, :] = held[16 * u + p : 16 * u + p + 1]
                bias += held[16 * u + 9 : 16 * u + 14]
        gb_o[...] = bias

    part = dmod[step]
    acc[...] += split_dot(part, w[...], contract=1)
    g_ada[...] = outer_sum(own_act[...], part)
    gb_ada[...] = colsum(part)

    @pl.when(step == 8)
    def _():
        dcond = acc[...] * silu_grad(both[1])
        g_t2[...] = outer_sum(own_rows_t(info, g_t2.shape[0], silu(both[0])), dcond)
        gb_t2[...] = colsum(dcond)
        dpre = split_dot(dcond, t2[...], contract=1) * silu_grad(both[0])
        g_t1[...] = outer_sum(own_rows_t(info, g_t1.shape[0], embed[...]), dpre)
        gb_t1[...] = colsum(dpre)


def mod_back(chain, info, sums, w, both, embed, t2, seqs):
    bands = len(sums)
    items = 2 * bands
    m, m1 = D // seqs, embed.shape[1] // seqs
    outs = [
        sds((m, 9 * D), F32), sds((1, 9 * D), F32), sds((m, D), F32), sds((1, D), F32),
        sds((m1, D), F32), sds((1, D), F32), sds((5, D), F32),
    ]
    return chain(
        functools.partial(mod_back_kernel, bands), outs,
        [info, *sums, w, both, embed, t2], MODMIB, "modulation_back", grid=(9,),
        in_specs=[smem()] + [whole(v) for v in sums]
        + [pl.BlockSpec((D, D), lambda i: (0, i)), whole(both), whole(embed), whole(t2)],
        out_specs=[pl.BlockSpec((m, D), lambda i: (0, i)), pl.BlockSpec((1, D), lambda i: (0, i))]
        + [whole(o) for o in outs[2:]],
        scratch=[
            pltpu.VMEM((items, D), F32), pltpu.VMEM((9, items, D), F32), pltpu.VMEM((m, items), F32)
        ],
    )


def block_refs(order, even, odd):
    return [(odd if k % 2 else even).at[k // 2] for k in order]


def qkv_kernel(order, span, even, odd, mod, w, out, h1_o, h1):
    frames = block_refs(order, even, odd)
    blocks = len(order)
    own = 2 * span

    @pl.when(pl.program_id(0) == 0)
    def _():
        shift, scale = mod[0:1, 0:D], mod[0:1, D : 2 * D]
        for i in range(blocks):
            n, unused = norm(frames[i][0:span, :].astype(F32))
            h1[pl.ds(i * span, span), :] = (n * (1.0 + scale) + shift).astype(BF16)
        h1_o[...] = h1[0:own, :]

    factor = jnp.where(pl.program_id(0) == 0, SCALE, 1.0)

    @pl.loop(0, blocks * span // own)
    def _(i):
        rows = pl.ds(pl.multiple_of(i * own, own), own)
        out[0, rows, :] = (dot(h1[rows, :], w[...]) * factor).astype(BF16)


def qkv(chain, blocks, order, span, mod, w):
    total = len(order) * span
    outs = [sds((3, total, D), BF16), sds((2 * span, D), BF16)]
    args = [blocks[0][0], blocks[2][0], mod]
    return chain(
        functools.partial(qkv_kernel, order, span), outs, [*args, w], room(16, total), "qkv", grid=(3,),
        in_specs=[whole(v) for v in args] + [pl.BlockSpec((D, D), lambda i: (0, i))],
        out_specs=[pl.BlockSpec((1, total, D), lambda i: (i, 0, 0)), whole(outs[1])],
        scratch=[pltpu.VMEM((total, D), BF16)],
    )


def attend_kernel(q, k, v, o, lse):
    qm = stack_heads(q[0])
    scores = dot_nt(k[0], qm)
    peak = jnp.max(scores, axis=0, keepdims=True)
    weights = jnp.exp(scores - peak)
    total = jnp.sum(weights, axis=0, keepdims=True)
    both = dot(v[0].T, weights.astype(BF16)) * (1.0 / total)
    o[...] = unstack_t(both).astype(BF16)
    lse[0] = peak + jnp.log(total)


def part_spec(part, rows):
    return pl.BlockSpec((1, rows, 128), lambda i: (part, 0, i))


def attend(chain, joined, own):
    total = joined.shape[1]
    return chain(
        attend_kernel, [sds((own, D), BF16), sds((PAIRS, 1, 2 * own), F32)], [joined] * 3, room(8, total),
        "attend", grid=(PAIRS,),
        in_specs=[part_spec(0, own), part_spec(1, total), part_spec(2, total)],
        out_specs=[
            pl.BlockSpec((own, 128), lambda i: (0, i)),
            pl.BlockSpec((1, 1, 2 * own), lambda i: (i, 0, 0)),
        ],
    )


def two_terms(rows):
    high = rows.astype(BF16).astype(F32)
    return jnp.concatenate([high, rows - high], axis=0).astype(BF16)


def read_stats(block):
    own = block.shape[0] - 16
    held = block[own:, :].astype(F32)

    def line(at):
        rows = held[at : at + 4] + held[at + 4 : at + 8]
        return jnp.concatenate([rows[i : i + 1] for i in range(4)], axis=1)

    return line(0), line(8)


def attend_dq_kernel(q, k, v, do, dq):
    own = do.shape[0] - 16
    qm = stack_heads(q[0])
    dom = stack_heads(do[0:own, :])
    lse, delta = read_stats(do)
    probs = jnp.exp(dot_nt(k[0], qm) - lse)
    grad = dot_nt(v[0], dom)
    ds = (probs * (grad - delta)).astype(BF16)
    dq[...] = (unstack_t(dot(k[0].T, ds)) * SCALE).astype(BF16)


def attend_dq(chain, joined, do):
    own = do.shape[0] - 16
    total = joined.shape[1]
    return chain(
        attend_dq_kernel, [sds((own, D), BF16)], [joined, joined, joined, do], room(8, total),
        "attend_dq", grid=(PAIRS,),
        in_specs=[
            part_spec(0, own), part_spec(1, total), part_spec(2, total),
            pl.BlockSpec((own + 16, 128), lambda i: (0, i)),
        ],
        out_specs=[pl.BlockSpec((own, 128), lambda i: (0, i))],
    )[0]


def attend_dkv_kernel(chunks, dq, q, k, v, *refs):
    do, out = refs[:chunks], refs[-1]
    keys, values = k[0], v[0]
    own = keys.shape[0]
    dk = jnp.zeros((own, 128), F32)
    dv = jnp.zeros((own, 128), F32)
    for i in range(chunks):
        block = do[i][0] if len(do[i].shape) == 3 else do[i][...]
        qm = stack_heads(q[0, i * own : (i + 1) * own, :])
        dom = stack_heads(block[0:own, :])
        lse, delta = read_stats(block)
        probs = jnp.exp(dot_nt(keys, qm) - lse)
        dv += dot(probs.astype(BF16), dom)
        grad = dot_nt(values, dom)
        ds = (probs * (grad - delta)).astype(BF16)
        dk += dot(ds, qm)
    out[0] = dq[...]
    out[1] = dk.astype(BF16)
    out[2] = dv.astype(BF16)


def attend_dkv(chain, dq, joined, do):
    own = dq.shape[0]
    specs, arrays = [], []
    for entry in do:
        if isinstance(entry, tuple):
            arrays.append(entry[0])
            specs.append(pl.BlockSpec((1, own + 16, 128), functools.partial(lambda at, i: (at, 0, i), entry[1])))
        else:
            arrays.append(entry)
            specs.append(pl.BlockSpec((own + 16, 128), lambda i: (0, i)))
    return chain(
        functools.partial(attend_dkv_kernel, len(do)), [sds((3, own, D), BF16)],
        [dq, joined, joined, joined, *arrays], room(8, joined.shape[1]), "attend_dkv", grid=(PAIRS,),
        in_specs=[pl.BlockSpec((own, 128), lambda i: (0, i))]
        + [part_spec(0, joined.shape[1]), part_spec(1, own), part_spec(2, own)]
        + specs,
        out_specs=[pl.BlockSpec((3, own, 128), lambda i: (0, 0, i))],
    )[0]


def start_rows(fa, fb, span):
    return jnp.concatenate([fa[0:span, :], fb[0:span, :]], axis=0).astype(F32)


def gelu_both(u):
    c = math.sqrt(2.0 / math.pi)
    square = u * u
    t = jnp.tanh(c * u * (1.0 + 0.044715 * square))
    half = 0.5 * (1.0 + t)
    slope = half + 0.5 * u * (1.0 - t * t) * (c * (1.0 + 3 * 0.044715 * square))
    return u * half, slope


STEPS = FF // D


def fetch(pairs, sems):
    copies = [pltpu.make_async_copy(a, b, sems.at[i]) for i, (a, b) in enumerate(pairs)]
    for copy in copies:
        copy.start()
    return copies


def trunk_kernel(span, order, *refs):
    count = len(order)
    info, cap_len, *blocks = refs[: 2 + count]
    (o, lse, h1, mod, ca, cb, up_b, down_b, wo_h, wq_h, wkv_h, wc_h, up_h, down_h,
     big_o, out_o, away_o, cap_o, fac_o, dx1_o, do_o, sums_o,
     wo, wq, wkv, wc, up, down, sems, kv2, q2, p2, x1, x2, low, dh3, offset) = refs[2 + count :]
    own = 2 * span
    slot = lambda i: slice(i * own, (i + 1) * own)
    cap_rows = blocks[0].shape[0] - span

    pairs = [(wkv_h, wkv), (wo_h, wo), (wq_h, wq), (wc_h, wc)]
    for i in range(STEPS):
        piece = pl.ds(i * D, D)
        pairs += [(up_h.at[:, piece], up.at[i]), (down_h.at[piece, :], down.at[i])]
    copies = fetch(pairs, sems)

    gate1, shift2, scale2, gate2, shift3, scale3, gate3 = (
        mod[0:1, i * D : (i + 1) * D] for i in range(2, 9)
    )

    length = cap_len[2 * info[0] + info[2]]
    for i, k in enumerate(order):
        here = slice(i * cap_rows, (i + 1) * cap_rows)
        cap_o[here, :] = blocks[i][span:, :]
        first = jnp.bitwise_xor(info[1], k) * cap_rows
        token = first + lax.broadcasted_iota(jnp.int32, (cap_rows, 128), 0)
        offset[here, :] = jnp.where(token < length, 0.0, NEGATIVE)
    copies[0].wait()
    kv2[...] = dot(cap_o[...], wkv[...]).astype(BF16)

    copies[1].wait()
    attn = dot(o[...], wo[...])
    x1[...] = start_rows(blocks[0], blocks[1], span) + gate1 * attn
    attn = attn.astype(BF16)
    n2, unused = norm(x1[...])
    h2 = (n2 * (1.0 + scale2) + shift2).astype(BF16)
    fac_o[slot(0), :] = h2
    copies[2].wait()
    q2[...] = (dot(h2, wq[...]) * SCALE).astype(BF16)
    for i in range(PAIRS):
        qm = stack_heads(q2[:, cols(i)])
        scores = dot_nt(kv2[:, cols(i)], qm) + offset[:, 0:1]
        peak = jnp.max(scores, axis=0, keepdims=True)
        weights = jnp.exp(scores - peak)
        probs = (weights * (1.0 / jnp.sum(weights, axis=0, keepdims=True))).astype(BF16)
        p2[i] = probs
        both = dot(kv2[:, D + i * 128 : D + (i + 1) * 128].T, probs)
        fac_o[slot(2), cols(i)] = unstack_t(both).astype(BF16)
    copies[3].wait()
    attn2 = dot(fac_o[slot(2), :], wc[...])
    x2[...] = x1[...] + gate2 * attn2
    attn2 = attn2.astype(BF16)

    n3, unused = norm(x2[...])
    big_o[2 * STEPS] = (n3 * (1.0 + scale3) + shift3).astype(BF16)
    dy = jnp.concatenate([ca[...], cb[...]], axis=0).astype(F32)
    big_o[2 * STEPS + 1] = (gate3 * dy).astype(BF16)
    for i in range(STEPS):
        copies[4 + 2 * i].wait()
        copies[5 + 2 * i].wait()
        piece = slice(i * D, (i + 1) * D)
        acted, slope = gelu_both(dot(big_o[2 * STEPS], up[i]) + up_b[:, piece].astype(F32))
        acted = acted.astype(BF16)
        big_o[i] = acted
        dupper = (slope * dot_nt(big_o[2 * STEPS + 1], down[i])).astype(BF16)
        big_o[STEPS + i] = dupper
        sums_o[8 + i : 9 + i, :] = colsum(dupper.astype(F32))
        if i:
            low[...] += dot(acted, down[i])
            dh3[...] += dot_nt(dupper, up[i])
        else:
            low[...] = dot(acted, down[i])
            dh3[...] = dot_nt(dupper, up[i])
    lower = low[...] + down_b[...].astype(F32)
    value = x2[...]
    result = (value + gate3 * lower).astype(BF16)
    out_o[...] = result[:span]
    away_o[...] = result[span:]
    dy = jnp.concatenate([ca[...], cb[...]], axis=0).astype(F32)
    n3, rstd = norm(value)
    back = dh3[...]
    sums_o[4:5, :] = colsum(back)
    sums_o[5:6, :] = colsum(n3 * back)
    sums_o[6:7, :] = colsum(lower * dy)
    sums_o[7:8, :] = colsum(big_o[2 * STEPS + 1].astype(F32))
    sums_o[12:16, :] = jnp.zeros((4, D), F32)
    dx2 = dy + norm_back(n3, rstd, (1.0 + scale3) * back)

    sums_o[3:4, :] = colsum(attn2.astype(F32) * dx2)
    da2 = (gate2 * dx2).astype(BF16)
    fac_o[slot(3), :] = da2
    do2 = dot_nt(da2, wc[...]).astype(BF16)
    for i in range(PAIRS):
        qm = stack_heads(q2[:, cols(i)])
        dom = stack_heads(do2[:, cols(i)])
        keys, values = kv2[:, cols(i)], kv2[:, D + i * 128 : D + (i + 1) * 128]
        probs = p2[i]
        fac_o[slot(5), cols(i)] = dot(probs, dom).astype(BF16)
        probs = probs.astype(F32)
        grad = dot_nt(values, dom)
        ds = (probs * (grad - colsum(probs * grad))).astype(BF16)
        fac_o[slot(1), cols(i)] = (unstack_t(dot(keys.T, ds)) * SCALE).astype(BF16)
        fac_o[slot(4), cols(i)] = dot(ds, qm).astype(BF16)
    dh2 = dot_nt(fac_o[slot(1), :], wq[...])
    n2, rstd = norm(x1[...])
    sums_o[1:2, :] = colsum(dh2)
    sums_o[2:3, :] = colsum(n2 * dh2)
    dx1 = dx2 + norm_back(n2, rstd, (1.0 + scale2) * dh2)
    dx1_o[...] = dx1
    sums_o[0:1, :] = colsum(attn.astype(F32) * dx1)

    da = (gate1 * dx1).astype(BF16)
    fac_o[slot(6), :] = da
    fac_o[slot(7), :] = o[...]
    fac_o[slot(8), :] = h1[...]
    do = dot_nt(da, wo[...]).astype(BF16)
    do_o[0:own, :] = do
    both = do.astype(F32) * o[...].astype(F32)
    for i in range(PAIRS):
        t = both[:, cols(i)].T
        delta = [colsum(t[:HEAD]), colsum(t[HEAD:])]
        delta = [d[:, 128 * j : 128 * (j + 1)] for d in delta for j in range(own // 128)]
        sums = [lse[i][:, 128 * j : 128 * (j + 1)] for j in range(2 * own // 128)]
        held = [two_terms(jnp.concatenate(rows, axis=0)) for rows in (sums, delta)]
        do_o[own:, cols(i)] = jnp.concatenate(held, axis=0)
    dcap = (dot_nt(fac_o[slot(4), :], wkv[:, 0:D]) + dot_nt(fac_o[slot(5), :], wkv[:, D : 2 * D])).astype(BF16)
    cap_total = dcap.shape[0]
    fac_o[9 * own : 9 * own + cap_total, :] = dcap
    fac_o[9 * own + cap_total :, :] = sums_o[...].astype(BF16)


def trunk(chain, info, cap_len, blocks, order, span, o, lse, h1, mod, ca, cb, up_b, down_b, *weights):
    own = 2 * span
    cap_total = len(blocks) * (blocks[0][0].shape[1] - span)
    thin, wide = sds((own, D), BF16), sds((own, D), F32)
    half = sds((span, D), BF16)
    outs = [
        sds((2 * STEPS + 2, own, D), BF16), half, half, sds((cap_total, D), BF16),
        sds((9 * own + cap_total + 16, D), BF16), wide, sds((own + 16, D), BF16), sds((16, D), F32),
    ]
    stacks = [blocks[0][0], blocks[2][0]]
    here = [*stacks, o, lse, h1, mod, ca, cb, up_b, down_b]
    square = pltpu.VMEM((D, D), BF16)

    def kernel(info, cap_len, even, odd, *refs):
        trunk_kernel(span, order, info, cap_len, *block_refs(order, even, odd), *refs)

    return chain(
        kernel, outs, [info, cap_len, *here, *weights], 44, "trunk",
        in_specs=[smem()] * 2 + [vmem()] * len(here) + [pl.BlockSpec(memory_space=pl.ANY)] * len(weights),
        scratch=[
            square, square, pltpu.VMEM((D, 2 * D), BF16), square,
            pltpu.VMEM((STEPS, D, D), BF16), pltpu.VMEM((STEPS, D, D), BF16),
            pltpu.SemaphoreType.DMA((4 + 2 * STEPS,)),
            pltpu.VMEM((cap_total, 2 * D), BF16), pltpu.VMEM((own, D), BF16),
            pltpu.VMEM((PAIRS, cap_total, 2 * own), BF16),
        ]
        + [pltpu.VMEM((own, D), F32)] * 4
        + [pltpu.VMEM((cap_total, 128), F32)],
    )


def last_kernel(even, dqkv, w, mod, dx1, away, own_o, back_o, sums_o):
    scale1 = mod[0:1, D : 2 * D]
    dh1 = sum(dot_nt(dqkv[i], w[:, i * D : (i + 1) * D]) for i in range(3))
    span = own_o.shape[0]
    start = start_rows(even.at[0], even.at[even.shape[0] // 2], span)
    n1, rstd = norm(start)
    sums_o[0:1, :] = colsum(dh1)
    sums_o[1:2, :] = colsum(n1 * dh1)
    sums_o[2:8, :] = jnp.zeros((6, D), F32)
    grad = dx1[...] + norm_back(n1, rstd, (1.0 + scale1) * dh1)
    own_o[...] = grad[:span]
    back_o[0] = grad[span:].astype(BF16)
    back_o[1] = away[...]


def pick_rows(info, x):
    source = lax.broadcasted_iota(jnp.int32, (D, D // 2), 0)
    column = lax.broadcasted_iota(jnp.int32, (D, D // 2), 1)
    block = sum((column >= 96 * i).astype(jnp.int32) for i in (1, 2, 3))
    wanted = 96 * jnp.bitwise_xor(info[1], 2 * block) + column - 96 * block
    choose = (source == wanted).astype(F32).astype(BF16)
    return dot(x, choose).astype(BF16)


def emit(first, info, tiles, blocks, send_o, keep_o):
    place = {True: 0, False: 0}
    for r in range(4):
        sent = bool(r & first)
        (send_o if sent else keep_o)[place[sent]] = tiles[jnp.bitwise_xor(info[0], r), blocks]
        place[sent] += 1


def down_grad_kernel(info, fac, fac_p, send_o, keep_o, tiles):
    for e in range(4):
        owner = jnp.bitwise_xor(info[1], 2 * e)
        half = pl.multiple_of(lax.rem(owner, 2) * 384, 128)
        where = (lax.div(owner, 2), slice(None), pl.ds(half, 384))
        grad = dot_tn(fac[where], fac[9]) + dot_tn(fac_p[where], fac_p[9])
        for q in range(4):
            tiles[q, e] = grad[96 * q : 96 * (q + 1)].astype(BF16)
    emit(1, info, tiles, slice(0, 4), send_o, keep_o)


def up_grad_kernel(info, fac, fac_p, send_o, keep_o, tiles):
    x, xp = pick_rows(info, fac[8]), pick_rows(info, fac_p[8])
    for q in range(4):
        grad = dot_tn(x, fac[4 + q]) + dot_tn(xp, fac_p[4 + q])
        for e in range(4):
            tiles[q, e] = grad[96 * e : 96 * (e + 1)].astype(BF16)
    emit(2, info, tiles, slice(0, 4), send_o, keep_o)


def put(tiles, q, grad):
    for e in range(4):
        tiles[q, e] = grad[96 * e : 96 * (e + 1)].astype(BF16)


def emit_both(info, tiles, sx, kx, sy, ky):
    emit(1, info, tiles, slice(0, 2), sx, kx)
    emit(2, info, tiles, slice(2, 4), sy, ky)


def cross_grad_kernel(info, cap, fac, fac_p, sx, kx, sy, ky, tiles):
    own = (fac.shape[0] - cap.shape[0] - 16) // 9

    def slot(ref, i):
        return ref[i * own : (i + 1) * own, :]

    def pair(x, y):
        left, left_p = pick_rows(info, slot(fac, x)), pick_rows(info, slot(fac_p, x))
        return dot_tn(left, slot(fac, y)) + dot_tn(left_p, slot(fac_p, y))

    put(tiles, 0, pair(0, 1))
    x = pick_rows(info, cap[...])
    rows = x.shape[0] // 4
    xp = jnp.concatenate([x[rows * i : rows * (i + 1)] for i in (1, 0, 3, 2)], axis=0)
    for q in (1, 2):
        put(tiles, q, dot_tn(x, slot(fac, q + 3)) + dot_tn(xp, slot(fac_p, q + 3)))
    put(tiles, 3, pair(2, 3))
    emit_both(info, tiles, sx, kx, sy, ky)


def attn_grad_kernel(info, da, o, h1, da_p, o_p, h1_p, dqkv, dqkv_p, sx, kx, sy, ky, tiles):
    x, xp = pick_rows(info, h1[...]), pick_rows(info, h1_p[...])
    for i in range(3):
        put(tiles, i, dot_tn(x, dqkv[i]) + dot_tn(xp, dqkv_p[i]))
    x, xp = pick_rows(info, o[...]), pick_rows(info, o_p[...])
    put(tiles, 3, dot_tn(x, da[...]) + dot_tn(xp, da_p[...]))
    emit_both(info, tiles, sx, kx, sy, ky)


def grad_call(chain, kernel, info, args, name, shape, outs, in_specs=None):
    return chain(
        kernel, [sds(o, BF16) for o in outs], [info, *args], 20, name, grid=(1,) if in_specs else None,
        in_specs=[smem()] + (in_specs or [vmem()] * len(args)),
        scratch=[pltpu.VMEM(shape, BF16)],
    )


def total(*refs):
    return sum(r.astype(F32) for r in refs).astype(BF16)


def add_first_kernel(keep, recv, keep_o, send_o):
    keep_o[...] = total(keep[0], recv[0])
    send_o[...] = total(keep[1], recv[1])


def add_both_kernel(kx, rx, ky, ry, kx_o, sx_o, ky_o, sy_o):
    add_first_kernel(kx, rx, kx_o, sx_o)
    add_first_kernel(ky, ry, ky_o, sy_o)


def sum_rows(early, early_p, late, late_p):
    first = late[0:2, :] + late_p[0:2, :]
    both = early[0:12, :].astype(F32) + early_p[0:12, :].astype(F32)
    return jnp.concatenate([first, both, jnp.zeros((2, D), F32)], axis=0).astype(BF16)


def mlp_second_kernel(ka, ra, kb, rb, fac, fac_p, late, late_p, keep_o, send_o):
    for g, (keep, recv) in enumerate(((ka, ra), (kb, rb))):
        for e in range(4):
            (send_o if e % 2 else keep_o)[e // 2, 96 * g : 96 * (g + 1), :] = total(keep[e], recv[e])
    rows = sum_rows(fac, fac_p, late, late_p)
    for ref in (keep_o, send_o):
        for i in range(2):
            ref[i, 192:208, :] = rows


def mlp_third_kernel(keep, recv, keep_o, send_o):
    keep_o[...] = total(keep[0], recv[0])
    send_o[0:192, :] = total(keep[1, 0:192, :], recv[1, 0:192, :])
    send_o[192:208, :] = total(keep[0, 192:208, :], recv[0, 192:208, :])


def mlp_fourth_kernel(keep, recv, out):
    out[0:192, :] = total(keep[0:192, :], recv[0:192, :])
    out[192:208, :] = keep[192:208, :]
    out[208:224, :] = recv[192:208, :]


def order_place(k):
    return 2 * (k % 4) + k // 4


def second_kernel(kx, rx, ky, ry, *refs):
    caption, (keep_o, send_o) = refs[:-2], refs[-2:]
    for e in range(4):
        out = send_o if e % 2 else keep_o
        keep, recv = ((kx, rx), (ky, ry))[e // 2]
        out[e // 2, 0:96, :] = total(keep[e % 2], recv[e % 2])
        if caption:
            dcap, dcap_p = caption
            rows = dcap.shape[0] // 8
            at, at_p = (rows * order_place(2 * e + i) for i in range(2))
            out[e // 2, 96:, :] = total(dcap[at : at + rows, :], dcap_p[at_p : at_p + rows, :])


def third_kernel(keep, recv, keep_o, send_o):
    keep_o[...] = total(keep[0], recv[0])
    send_o[...] = total(keep[1], recv[1])


def fourth_kernel(keep, recv, out):
    out[...] = total(keep[...], recv[...])


def cross_fourth_kernel(keep, recv, out, same_o, away_o):
    out[...] = total(keep[0:96, :], recv[0:96, :])
    same_o[...] = keep[96:, :].astype(F32)
    away_o[...] = recv[96:, :].astype(F32)


def swap(x, axis, size, k):
    return lax.ppermute(x, axis, [(i, i ^ k) for i in range(size)])


def over_x(x):
    return swap(x, "band", 4, 1)


def over_y(x):
    return swap(x, "band", 4, 2)


def to_band(x):
    return [x] + [swap(x, "band", 4, t) for t in (1, 2, 3)]


def mlp_finish_kernel(info, t0, t1, t2, t3, down_o, up_o):
    for r, tile in enumerate((t0, t1, t2, t3)):
        q = jnp.bitwise_xor(info[0], r)
        down_o[pl.ds(pl.multiple_of(96 * q, 96), 96), :] = tile[0:96, :].astype(F32)
        up_o[:, pl.ds(pl.multiple_of(D * q, D), D)] = tile[96:192, :].astype(F32)


def cross_finish_kernel(info, t0, t1, t2, t3, cq_o, ckv_o, co_o, tiles):
    for r, tile in enumerate((t0, t1, t2, t3)):
        tiles[jnp.bitwise_xor(info[0], r)] = tile[...]
    cq_o[...] = tiles[0].astype(F32)
    ckv_o[:, 0:D] = tiles[1].astype(F32)
    ckv_o[:, D:] = tiles[2].astype(F32)
    co_o[...] = tiles[3].astype(F32)


def attn_finish_kernel(info, t0, t1, t2, t3, in_o, out_o, tiles):
    for r, tile in enumerate((t0, t1, t2, t3)):
        tiles[jnp.bitwise_xor(info[0], r)] = tile[...]
    for i in range(3):
        in_o[:, i * D : (i + 1) * D] = tiles[i].astype(F32)
    out_o[...] = tiles[3].astype(F32)


def finish(chain, kernel, info, tiles, widths, name, scratch=()):
    outs = [sds(w, F32) for w in widths]
    return chain(
        kernel, outs, [info, *tiles], 12, name, grid=(1,), in_specs=[smem()] + [whole(t) for t in tiles],
        out_specs=[whole(o) for o in outs], scratch=scratch,
    )


def plain_reduce(x, y, owners):
    grad = lax.psum_scatter(dot_tn(x, y).astype(BF16), "seq", scatter_dimension=0, tiled=True)
    return lax.psum(grad, "band").astype(F32)


def on_device(bands, seqs, frames, caption, timesteps, cap_len, attn_in, attn_out, cross_query,
              cross_keyval, cross_out, mlp_up, up_bias, mlp_down, down_bias, ada_weight, ada_bias,
              time_first, first_bias, time_second, second_bias, cotangent):
    span = frames.shape[1]
    own = 2 * span
    cap_rows = caption.shape[1]
    items = timesteps.shape[0]
    halves = seqs // 2
    band = lax.axis_index("band")
    seq = lax.axis_index("seq")
    half = (seq >= halves).astype(jnp.int32)
    item = 2 * band + half
    info = jnp.stack([band, seq, half]).astype(jnp.int32)

    chain = Chain()

    order = [k for i in range(halves) for k in (i, i + halves)]
    same, other = pick(chain, info, frames, caption)
    even = [same] + [swap(same if k < halves else other, "seq", seqs, k) for k in range(2, seqs, 2)]

    steps = jnp.take(timesteps, jnp.bitwise_xor(jnp.arange(items), item))
    width = time_first.shape[0] // 2
    freq = jnp.exp(-math.log(10000.0) * jnp.arange(width, dtype=F32) / width)
    angle = steps.astype(F32)[:, None] * freq[None, :]
    embed = jnp.concatenate([jnp.cos(angle), jnp.sin(angle)], axis=1)
    row = lambda v: v.reshape(1, -1)
    pre_cond, mod = modulation(
        chain, embed, time_first, row(first_bias), time_second, row(second_bias), ada_weight, row(ada_bias)
    )
    cot_own, cot_other = pick(chain, info, cotangent)
    cot_other = swap(cot_other, "seq", seqs, halves)

    even = stack(chain, even, "blocks")
    odd = swap(even, "seq", seqs, 1)
    blocks = [(odd if k % 2 else even, k // 2) for k in order]
    joined, h1 = qkv(chain, blocks, order, span, mod, attn_in)
    mixed, lse = attend(chain, joined, own)

    cap_total = seqs * cap_rows
    big, out, out_back, cap_all, fac, dx1, do, early = trunk(
        chain, info, cap_len, blocks, order, span, mixed, lse, h1, mod, cot_own, cot_other, row(up_bias),
        row(down_bias), attn_out, cross_query, cross_keyval, cross_out, mlp_up, mlp_down,
    )
    fast = bands == 4 and seqs == 8
    if fast:
        big_p, fac_p = swap(big, "seq", seqs, 1), swap(fac, "seq", seqs, 1)
    got = [do] + [swap(do, "seq", seqs, k) for k in range(2, halves, 2)]
    dq = attend_dq(chain, joined, do)
    if fast:
        whole_tiles, pieces, halved = (4, 4, 96, D), [(2, 4, 96, D)] * 2, [(2, 2, 96, D)] * 4
        args = [big, big_p]
        sa, ka = grad_call(chain, down_grad_kernel, info, args, "down_grad", whole_tiles, pieces)
        ra = over_x(sa)
        sb, kb = grad_call(chain, up_grad_kernel, info, args, "up_grad", whole_tiles, pieces)
        rb = over_y(sb)
    got = stack(chain, got, "do_blocks")
    got_p = swap(got, "seq", seqs, 1)
    if fast:
        cx, ckx, cy, cky = grad_call(
            chain, cross_grad_kernel, info, [cap_all, fac, fac_p], "cross_grad", whole_tiles, halved
        )
        crx, cry = over_x(cx), over_y(cy)

    do_blocks = [(array, i) for i in range(halves // 2) for array in (got, got_p)]
    dqkv = attend_dkv(chain, dq, joined, do_blocks)
    first_two = pl.BlockSpec((seqs // 2, span + cap_rows, D), lambda i: (0, 0, 0))
    grad_own, back, late = chain(
        last_kernel,
        [sds((span, D), F32), sds((2, span, D), BF16), sds((8, D), F32)],
        [even, dqkv, attn_in, mod, dx1, out_back],
        12, "last", grid=(1,),
        in_specs=[first_two, vmem(), vmem(), vmem(), vmem(), vmem()],
    )
    back = swap(back, "seq", seqs, halves)

    if fast:
        dqkv_p, late_p = swap(dqkv, "seq", seqs, 1), swap(late, "seq", seqs, 1)
        half = sds((4, 96, D), BF16)
        ka, sa, kb, sb = chain(add_both_kernel, [half] * 4, [ka, ra, kb, rb], 4, "mlp_add1")
        ra, rb = over_y(sa), over_x(sb)
        slots = [pl.BlockSpec((own, D), functools.partial(lambda at, *i: (at, 0), at)) for at in (6, 7, 8)]
        tx, tkx, ty, tky = grad_call(
            chain, attn_grad_kernel, info, [fac] * 3 + [fac_p] * 3 + [dqkv, dqkv_p], "attn_grad",
            whole_tiles, halved, in_specs=slots * 2 + [whole(dqkv)] * 2,
        )
        trx, try_ = over_x(tx), over_y(ty)
        grad_frames, out = place(
            chain, info, [(grad_own, (back, 0)), (out, (back, 1))], [F32, BF16], "place_frames"
        )
        quarter = sds((2, 96, D), BF16)
        ckx, cx, cky, cy = chain(add_both_kernel, [quarter] * 4, [ckx, crx, cky, cry], 4, "cross_add1")
        crx, cry = over_y(cx), over_x(cy)
        cap_at, sum_at = 9 * own // cap_total, (9 * own + cap_total) // 16
        cap_spec = pl.BlockSpec((cap_total, D), lambda *i: (cap_at, 0))
        sum_spec = pl.BlockSpec((16, D), lambda *i: (sum_at, 0))
        both = sds((2, 208, D), BF16)
        keep, send = chain(
            mlp_second_kernel, [both] * 2, [ka, ra, kb, rb, fac, fac_p, late, late_p], 4, "mlp_add2",
            grid=(1,), in_specs=[vmem()] * 4 + [sum_spec] * 2 + [vmem()] * 2,
        )
        recv = swap(send, "seq", seqs, 2)
        tkx, tx, tky, ty = chain(add_both_kernel, [quarter] * 4, [tkx, trx, tky, try_], 4, "attn_add1")
        trx, try_ = over_y(tx), over_x(ty)
        keep, send = chain(mlp_third_kernel, [sds((208, D), BF16)] * 2, [keep, recv], 4, "mlp_z1")
        recv = swap(send, "seq", seqs, 4)
        rows = 96 + cap_rows
        c_keep, c_send = chain(
            second_kernel, [sds((2, rows, D), BF16)] * 2, [ckx, crx, cky, cry, fac, fac_p], 4, "cross_add2",
            grid=(1,), in_specs=[vmem()] * 4 + [cap_spec] * 2,
        )
        c_recv = swap(c_send, "seq", seqs, 2)
        t_keep, t_send = chain(second_kernel, [quarter] * 2, [tkx, trx, tky, try_], 4, "attn_add2")
        t_recv = swap(t_send, "seq", seqs, 2)
        a_all = to_band(
            chain(mlp_fourth_kernel, [sds((224, D), BF16)], [keep, recv], 4, "mlp_z2")[0]
        )
        c_keep, c_send = chain(third_kernel, [sds((rows, D), BF16)] * 2, [c_keep, c_recv], 4, "cross_z1")
        c_recv = swap(c_send, "seq", seqs, 4)
        t_keep, t_send = chain(third_kernel, [sds((96, D), BF16)] * 2, [t_keep, t_recv], 4, "attn_z1")
        t_recv = swap(t_send, "seq", seqs, 4)
        c_done, cap_same, cap_away = chain(
            cross_fourth_kernel, [sds((96, D), BF16)] + [sds((cap_rows, D), F32)] * 2, [c_keep, c_recv], 4,
            "cross_z2",
        )
        c_all = to_band(c_done)
        t_all = to_band(chain(fourth_kernel, [sds((96, D), BF16)], [t_keep, t_recv], 4, "attn_z2")[0])
        sums = a_all
        g_down, g_up = finish(
            chain, mlp_finish_kernel, info, a_all, [(384, D), (96, FF)], "mlp_finish"
        )
    else:
        grad_frames, out = place(
            chain, info, [(grad_own, (back, 0)), (out, (back, 1))], [F32, BF16], "place_frames"
        )
        dcap = fac[9 * own : 9 * own + cap_total].reshape(seqs, cap_rows, D)
        place_of = jnp.asarray([order.index(k) for k in range(seqs)])
        dcap = dcap[place_of[jnp.bitwise_xor(seq, jnp.arange(seqs))]].reshape(cap_total, D)
        dcap = jnp.where(half == 0, jnp.stack([dcap, 0 * dcap]), jnp.stack([0 * dcap, dcap]))
        grad_caption = lax.psum_scatter(dcap, "seq", scatter_dimension=1, tiled=True).astype(F32)
        rows = jnp.concatenate([late[0:2], early[0:12], jnp.zeros((2, D), F32)])
        for k in range(1, halves):
            if k & (k - 1) == 0:
                rows = rows + swap(rows, "seq", seqs, k)
        rows = jnp.concatenate([rows, swap(rows, "seq", seqs, halves)]).astype(BF16)
        sums = [rows] + [swap(rows, "band", bands, t) for t in range(1, bands)]

    g_ada, gb_ada, g_t2, gb_t2, g_t1, gb_t1, gb_mlp = mod_back(
        chain, info, sums, ada_weight, pre_cond, embed, time_second, seqs
    )

    if fast:
        grad_caption = place(chain, info, [(cap_same, cap_away)], [F32], "place_caption")[0]
        tiles = [pltpu.VMEM((4, 96, D), BF16)]
        g_cq, g_ckv, g_co = finish(
            chain, cross_finish_kernel, info, c_all, [(96, D), (96, 2 * D), (96, D)], "cross_finish", tiles
        )
        g_in, g_out = finish(
            chain, attn_finish_kernel, info, t_all, [(96, 3 * D), (96, D)], "attn_finish", tiles
        )
    else:
        slot = lambda i: fac[i * own : (i + 1) * own]
        acted = jnp.concatenate([big[i] for i in range(FF // D)], axis=1)
        dupper = jnp.concatenate([big[FF // D + i] for i in range(FF // D)], axis=1)
        g_down = plain_reduce(acted, big[-1], seqs)
        g_up = plain_reduce(big[-2], dupper, seqs)
        g_cq = plain_reduce(slot(0), slot(1), seqs)
        g_ckv = plain_reduce(cap_all, jnp.concatenate([slot(4), slot(5)], axis=1), seqs)
        g_co = plain_reduce(slot(2), slot(3), seqs)
        g_out = plain_reduce(mixed, slot(6), seqs)
        g_in = plain_reduce(h1, jnp.concatenate([dqkv[0], dqkv[1], dqkv[2]], axis=1), seqs)

    def own_rows(v):
        size = v.size // seqs
        return lax.dynamic_slice_in_dim(v.reshape(-1), seq * size, size)

    return (
        out, grad_frames, grad_caption, g_in, g_out, g_cq, g_ckv, g_co, g_up, own_rows(gb_mlp[1:]), g_down,
        own_rows(gb_mlp[0]), g_ada, own_rows(gb_ada), g_t1, own_rows(gb_t1), g_t2, own_rows(gb_t2),
    )


def solution(mesh):
    split = P("band", "seq", None)
    rows, flat = P("seq", None), P("seq")
    return jax.shard_map(
        functools.partial(on_device, mesh.shape["band"], mesh.shape["seq"]),
        mesh=mesh,
        in_specs=(split, split) + (P(),) * 17 + (split,),
        out_specs=(split, split, split, rows, rows, rows, rows, rows, rows, flat, rows, flat, rows, flat,
                   rows, flat, rows, flat),
        check_vma=False,
    )
```

```python
import functools
import math

import jax
import jax.numpy as jnp
from jax import lax
from jax.experimental import pallas as pl
from jax.experimental.pallas import tpu as pltpu
from jax.sharding import PartitionSpec as P

D = 768
HEAD = 64
PAIRS = 6
FF = 3072
EPSILON = 1e-06
NEGATIVE = -1e30
SCALE = 0.125
F32 = jnp.float32
BF16 = jnp.bfloat16
MIB = 1 << 20
MODMIB = 10
COST = 1000000
FWD = 26
BWD = 16


def dot(a, b):
    return jnp.dot(a, b, preferred_element_type=F32)


def dot_nt(a, b):
    return lax.dot_general(a, b, (((1,), (1,)), ((), ())), preferred_element_type=F32)


def dot_tn(a, b):
    return lax.dot_general(a, b, (((0,), (0,)), ((), ())), preferred_element_type=F32)


def split_dot(x, w, contract=0):
    high = x.astype(BF16).astype(F32)
    both = jnp.concatenate([high, x - high], axis=0).astype(BF16)
    out = lax.dot_general(
        both, w, (((1,), (contract,)), ((), ())), preferred_element_type=F32
    )
    return out[: x.shape[0]] + out[x.shape[0] :]


def silu(v):
    return v * (1.0 / (1.0 + jnp.exp(-v)))


def silu_grad(v):
    s = 1.0 / (1.0 + jnp.exp(-v))
    return s * (1.0 + v * (1.0 - s))


def norm(v):
    mean = jnp.mean(v, axis=-1, keepdims=True)
    centred = v - mean
    spread = jnp.mean(centred * centred, axis=-1, keepdims=True)
    rstd = lax.rsqrt(spread + EPSILON)
    return centred * rstd, rstd


def norm_back(n, rstd, w):
    return (
        w - jnp.mean(w, axis=-1, keepdims=True) - n * jnp.mean(w * n, axis=-1, keepdims=True)
    ) * rstd


def colsum(v):
    return jnp.sum(v, axis=0, keepdims=True)


def cols(i):
    return slice(i * 128, (i + 1) * 128)


def head_masks():
    lane = lax.broadcasted_iota(jnp.int32, (1, 128), 1)
    first = (lane < HEAD).astype(F32)
    return first.astype(BF16), (1.0 - first).astype(BF16)


def stack_heads(block):
    first, second = head_masks()
    return jnp.concatenate([block * first, block * second], axis=0)


def unstack_t(both):
    rows = both.shape[1] // 2
    pair = jnp.concatenate([both[:HEAD, :rows], both[HEAD:, rows:]], axis=0)
    return pair.T


def sds(shape, dtype):
    return jax.ShapeDtypeStruct(shape, dtype)


def vmem():
    return pl.BlockSpec(memory_space=pltpu.VMEM)


def smem():
    return pl.BlockSpec(memory_space=pltpu.SMEM)


def whole(a):
    return pl.BlockSpec(a.shape, lambda *i: (0,) * len(a.shape))


class Chain:
    def __init__(self):
        self.token = None

    def __call__(self, kernel, outs, args, mib, name, grid=None, in_specs=None, out_specs=None, scratch=()):
        outs = list(outs)
        in_specs = list(in_specs or [vmem()] * len(args))
        out_specs = list(out_specs or [vmem()] * len(outs))
        count = len(args)
        body = kernel
        if self.token is not None:
            args = [*args, self.token]
            in_specs.append(pl.BlockSpec(memory_space=pl.ANY))
            body = lambda *refs: kernel(*refs[:count], *refs[count + 1 :])
        results = pl.pallas_call(
            body,
            **({} if grid is None else {"grid": grid}),
            out_shape=outs,
            in_specs=in_specs,
            out_specs=out_specs,
            scratch_shapes=list(scratch),
            compiler_params=pltpu.CompilerParams(vmem_limit_bytes=mib * MIB),
            cost_estimate=pl.CostEstimate(flops=1000, bytes_accessed=COST, transcendentals=0),
            name=name,
        )(*args)
        self.token = min(results, key=lambda r: r.size * r.dtype.itemsize)
        return results

    def after(self, x):
        self.token = x


def room(mib, frames):
    return min(56, mib * max(1, frames // 1024))


def pick_kernel(info, *refs):
    half = info[2]
    parts, (mine_o, theirs_o, sems) = refs[:-3], refs[-3:]
    copies = []
    at = 0
    for x in parts:
        rows = pl.ds(at, x.shape[1])
        for source, out in ((half, mine_o), (1 - half, theirs_o)):
            copies.append(pltpu.make_async_copy(x.at[source], out.at[rows], sems.at[len(copies)]))
        at += x.shape[1]
    for copy in copies:
        copy.start()
    for copy in copies:
        copy.wait()


def pick(chain, info, *parts):
    out = sds((sum(x.shape[1] for x in parts), D), BF16)
    anywhere = pl.BlockSpec(memory_space=pl.ANY)
    return chain(
        pick_kernel, [out, out], [info, *parts], 4, "pick", in_specs=[smem()] + [anywhere] * len(parts),
        out_specs=[anywhere] * 2, scratch=[pltpu.SemaphoreType.DMA((2 * len(parts),))],
    )


def stack_kernel(*refs):
    for i, ref in enumerate(refs[:-1]):
        refs[-1][i] = ref[...]


def stack(chain, arrays, name):
    out = sds((len(arrays),) + arrays[0].shape, arrays[0].dtype)
    return chain(stack_kernel, [out], arrays, 4, name)[0]


def place_kernel(info, *refs):
    count = len(refs) // 3
    for i in range(count):
        kept, received, out = refs[2 * i], refs[2 * i + 1], refs[2 * count + i]
        out[info[2]] = kept[...].astype(out.dtype)
        out[1 - info[2]] = received[...].reshape(kept.shape).astype(out.dtype)


def place(chain, info, pairs, dtypes, name):
    args, specs = [info], [smem()]
    for kept, received in pairs:
        args.append(kept)
        specs.append(whole(kept))
        if isinstance(received, tuple):
            args.append(received[0])
            specs.append(pl.BlockSpec((1,) + kept.shape, functools.partial(lambda at, i: (at, 0, 0), received[1])))
        else:
            args.append(received)
            specs.append(whole(received))
    outs = [sds((2,) + kept.shape, dtype) for (kept, unused), dtype in zip(pairs, dtypes)]
    return chain(
        place_kernel, outs, args, 8, name, grid=(1,), in_specs=specs, out_specs=[whole(o) for o in outs]
    )


def mod_kernel(embed, t1, b1, t2, b2, w, b, both_o, mod_o, act):
    @pl.when(pl.program_id(0) == 0)
    def _():
        pre = split_dot(embed[...], t1[...]) + b1[...].astype(F32)
        cond = split_dot(silu(pre), t2[...]) + b2[...].astype(F32)
        both_o[0] = pre
        both_o[1] = cond
        act[...] = silu(cond)

    mod_o[...] = split_dot(act[...], w[...]) + b[...].astype(F32)


def modulation(chain, embed, t1, b1, t2, b2, w, b):
    items = embed.shape[0]
    outs = [sds((2, items, D), F32), sds((items, 9 * D), F32)]
    return chain(
        mod_kernel, outs, [embed, t1, b1, t2, b2, w, b], MODMIB, "modulation", grid=(9,),
        in_specs=[whole(v) for v in (embed, t1, b1, t2, b2)]
        + [pl.BlockSpec((D, D), lambda i: (0, i)), pl.BlockSpec((1, D), lambda i: (0, i))],
        out_specs=[whole(outs[0]), pl.BlockSpec((items, D), lambda i: (0, i))],
        scratch=[pltpu.VMEM((items, D), F32)],
    )


def outer_sum(left_t, right):
    lh = left_t.astype(BF16)
    ll = (left_t - lh.astype(F32)).astype(BF16)
    rh = right.astype(BF16)
    rl = (right - rh.astype(F32)).astype(BF16)
    return dot(lh, rh) + dot(ll, rh) + dot(lh, rl)


def own_rows_t(info, size, v):
    row = lax.broadcasted_iota(jnp.int32, (size, v.shape[1]), 0)
    column = lax.broadcasted_iota(jnp.int32, (size, v.shape[1]), 1)
    choose = (column == row + size * info[1]).astype(F32).astype(BF16)
    high = v.astype(BF16)
    rest = (v - high.astype(F32)).astype(BF16)
    return dot_nt(choose, high) + dot_nt(choose, rest)


def mod_back_kernel(bands, seqs, info, *refs):
    sums = refs[:bands]
    (both, embed, t2, w_h, g_ada_h, gb_ada, g_t2, gb_t2, g_t1, gb_t1, gb_down, gb_up,
     w, g_ada, sems, acc, dmod, all_bias) = refs[bands:]
    pieces = [pl.ds(i * D, D) for i in range(9)]
    copies = fetch([(w_h.at[:, piece], w.at[i]) for i, piece in enumerate(pieces)], sems)
    own_act = own_rows_t(info, D // seqs, silu(both[1]))
    bias = jnp.zeros((5, D), F32)
    for t in range(bands):
        held = sums[t][sums[t].shape[0] - 32 :, :].astype(F32)
        for u in range(2):
            r = 2 * t + u
            for p in range(9):
                dmod[p, r : r + 1, :] = held[16 * u + p : 16 * u + p + 1]
            bias += held[16 * u + 9 : 16 * u + 14]
    stores = []
    for i, piece in enumerate(pieces):
        part = dmod[i]
        g_ada[i] = outer_sum(own_act, part)
        stores.append(pltpu.make_async_copy(g_ada.at[i], g_ada_h.at[:, piece], sems.at[9 + i]))
        stores[-1].start()
        all_bias[:, i * D : (i + 1) * D] = jnp.broadcast_to(colsum(part), (8, D))
        copies[i].wait()
        term = split_dot(part, w[i], contract=1)
        if i:
            acc[...] += term
        else:
            acc[...] = term

    def own_part(row):
        size = row.shape[1] // seqs
        rows = jnp.broadcast_to(row, (8, row.shape[1]))
        return pltpu.roll(rows, row.shape[1] - info[1] * size, 1)[0:1, 0:size]

    size = 9 * D // seqs
    gb_ada[...] = pltpu.roll(all_bias[...], 9 * D - info[1] * size, 1)[0:1, 0:size]
    gb_down[...] = own_part(bias[0:1])
    gb_up[...] = own_part(jnp.concatenate([bias[1 + i : 2 + i] for i in range(4)], axis=1))
    dcond = acc[...] * silu_grad(both[1])
    g_t2[...] = outer_sum(own_rows_t(info, D // seqs, silu(both[0])), dcond)
    gb_t2[...] = own_part(colsum(dcond))
    dpre = split_dot(dcond, t2[...], contract=1) * silu_grad(both[0])
    g_t1[...] = outer_sum(own_rows_t(info, g_t1.shape[0], embed[...]), dpre)
    gb_t1[...] = own_part(colsum(dpre))
    for store in stores:
        store.wait()


def mod_back(chain, info, sums, w, both, embed, t2, seqs):
    bands = len(sums)
    items = 2 * bands
    m = D // seqs
    line = lambda n: sds((1, n // seqs), F32)
    outs = [
        sds((m, 9 * D), F32), line(9 * D), sds((m, D), F32), line(D), sds((embed.shape[1] // seqs, D), F32),
        line(D), line(D), line(FF),
    ]
    anywhere = pl.BlockSpec(memory_space=pl.ANY)
    here = [*sums, both, embed, t2]
    return chain(
        functools.partial(mod_back_kernel, bands, seqs), outs, [info, *here, w], 20, "modulation_back",
        grid=(1,), in_specs=[smem()] + [whole(v) for v in here] + [anywhere],
        out_specs=[anywhere] + [whole(o) for o in outs[1:]],
        scratch=[
            pltpu.VMEM((9, D, D), BF16), pltpu.VMEM((9, m, D), F32), pltpu.SemaphoreType.DMA((18,)),
            pltpu.VMEM((items, D), F32), pltpu.VMEM((9, items, D), F32), pltpu.VMEM((8, 9 * D), F32),
        ],
    )


def block_refs(order, even, odd):
    return [(odd if k % 2 else even).at[k // 2] for k in order]


def qkv_kernel(order, span, even, odd, mod, w, out, h1_o, h1):
    frames = block_refs(order, even, odd)
    blocks = len(order)
    own = 2 * span

    @pl.when(pl.program_id(0) == 0)
    def _():
        shift, scale = mod[0:1, 0:D], mod[0:1, D : 2 * D]
        for i in range(blocks):
            n, unused = norm(frames[i][0:span, :].astype(F32))
            h1[pl.ds(i * span, span), :] = (n * (1.0 + scale) + shift).astype(BF16)
        h1_o[...] = h1[0:own, :]

    factor = jnp.where(pl.program_id(0) == 0, SCALE, 1.0)

    @pl.loop(0, blocks * span // own)
    def _(i):
        rows = pl.ds(pl.multiple_of(i * own, own), own)
        out[0, rows, :] = (dot(h1[rows, :], w[...]) * factor).astype(BF16)


def qkv(chain, blocks, order, span, mod, w):
    total = len(order) * span
    outs = [sds((3, total, D), BF16), sds((2 * span, D), BF16)]
    args = [blocks[0][0], blocks[2][0], mod]
    return chain(
        functools.partial(qkv_kernel, order, span), outs, [*args, w], room(16, total), "qkv", grid=(3,),
        in_specs=[whole(v) for v in args] + [pl.BlockSpec((D, D), lambda i: (0, i))],
        out_specs=[pl.BlockSpec((1, total, D), lambda i: (i, 0, 0)), whole(outs[1])],
        scratch=[pltpu.VMEM((total, D), BF16)],
    )


def attend_kernel(q, k, v, o, lse):
    qm = stack_heads(q[0])
    scores = dot_nt(k[0], qm)
    peak = jnp.max(scores, axis=0, keepdims=True)
    weights = jnp.exp(scores - peak)
    total = jnp.sum(weights, axis=0, keepdims=True)
    both = dot(v[0].T, weights.astype(BF16)) * (1.0 / total)
    o[...] = unstack_t(both).astype(BF16)
    lse[0] = peak + jnp.log(total)


def part_spec(part, rows):
    return pl.BlockSpec((1, rows, 128), lambda i: (part, 0, i))


def attend(chain, joined, own):
    total = joined.shape[1]
    return chain(
        attend_kernel, [sds((own, D), BF16), sds((PAIRS, 1, 2 * own), F32)], [joined] * 3, room(8, total),
        "attend", grid=(PAIRS,),
        in_specs=[part_spec(0, own), part_spec(1, total), part_spec(2, total)],
        out_specs=[
            pl.BlockSpec((own, 128), lambda i: (0, i)),
            pl.BlockSpec((1, 1, 2 * own), lambda i: (i, 0, 0)),
        ],
    )


def two_terms(rows):
    high = rows.astype(BF16).astype(F32)
    return jnp.concatenate([high, rows - high], axis=0).astype(BF16)


def read_stats(block):
    own = block.shape[0] - 16
    held = block[own:, :].astype(F32)

    def line(at):
        rows = held[at : at + 4] + held[at + 4 : at + 8]
        return jnp.concatenate([rows[i : i + 1] for i in range(4)], axis=1)

    return line(0), line(8)


def attend_dq_kernel(q, k, v, do, dq):
    own = do.shape[0] - 16
    qm = stack_heads(q[0])
    dom = stack_heads(do[0:own, :])
    lse, delta = read_stats(do)
    probs = jnp.exp(dot_nt(k[0], qm) - lse)
    grad = dot_nt(v[0], dom)
    ds = (probs * (grad - delta)).astype(BF16)
    dq[...] = (unstack_t(dot(k[0].T, ds)) * SCALE).astype(BF16)


def attend_dq(chain, joined, do):
    own = do.shape[0] - 16
    total = joined.shape[1]
    return chain(
        attend_dq_kernel, [sds((own, D), BF16)], [joined, joined, joined, do], room(8, total),
        "attend_dq", grid=(PAIRS,),
        in_specs=[
            part_spec(0, own), part_spec(1, total), part_spec(2, total),
            pl.BlockSpec((own + 16, 128), lambda i: (0, i)),
        ],
        out_specs=[pl.BlockSpec((own, 128), lambda i: (0, i))],
    )[0]


def attend_dkv_kernel(chunks, dq, q, k, v, *refs):
    do, out = refs[:chunks], refs[-1]
    keys, values = k[0], v[0]
    own = keys.shape[0]
    dk = jnp.zeros((own, 128), F32)
    dv = jnp.zeros((own, 128), F32)
    for i in range(chunks):
        qm = stack_heads(q[0, i * own : (i + 1) * own, :])
        block = do[i][...]
        dom = stack_heads(block[0:own, :])
        lse, delta = read_stats(block)
        probs = jnp.exp(dot_nt(keys, qm) - lse)
        dv += dot(probs.astype(BF16), dom)
        grad = dot_nt(values, dom)
        ds = (probs * (grad - delta)).astype(BF16)
        dk += dot(ds, qm)
    lanes = pl.ds(pl.multiple_of(128 * pl.program_id(0), 128), 128)
    out[0:own, lanes] = dq[...]
    out[own : 2 * own, lanes] = dk.astype(BF16)
    out[2 * own : 3 * own, lanes] = dv.astype(BF16)


def last_kernel(chunks, *refs):
    first, even, w, mod, dx1, away, out, own_o, back_o, part = refs[4 + chunks :]
    attend_dkv_kernel(chunks, *refs[: 4 + chunks], part)
    own = part.shape[0] // 3
    half = part.shape[1]

    @pl.when(pl.program_id(0) == PAIRS // 2 - 1)
    def _():
        out[0 : 3 * own, 0:half] = first[...]
        out[0 : 3 * own, half:] = part[...]
        scale1 = mod[0:1, D : 2 * D]
        dh1 = sum(dot_nt(out[i * own : (i + 1) * own, :], w[:, i * D : (i + 1) * D]) for i in range(3))
        span = own_o.shape[0]
        n1, rstd = norm(start_rows(even.at[0], even.at[even.shape[0] // 2], span))
        sums = jnp.concatenate([colsum(dh1), colsum(n1 * dh1), jnp.zeros((14, D), F32)], axis=0)
        out[3 * own :, :] = sums.astype(BF16)
        grad = dx1[...] + norm_back(n1, rstd, (1.0 + scale1) * dh1)
        own_o[...] = grad[:span]
        back_o[0] = grad[span:].astype(BF16)
        back_o[1] = away[...]


def attend_dkv(chain, dq, joined, do, half, rest=()):
    own = dq.shape[0]
    span = own // 2
    shift = half * (PAIRS // 2)
    pair = lambda part, rows: pl.BlockSpec((1, rows, 128), lambda i: (part, 0, i + shift))
    specs = [
        pl.BlockSpec((own + 16, 128), functools.partial(lambda at, i: (at, i + shift), at)) for unused, at in do
    ]
    outs = [sds((3 * own, D // 2), BF16)]
    kernel = attend_dkv_kernel
    scratch = []
    if rest:
        outs = [sds((3 * own + 16, D), BF16), sds((span, D), F32), sds((2, span, D), BF16)]
        kernel = last_kernel
        scratch = [pltpu.VMEM((3 * own, D // 2), BF16)]
    return chain(
        functools.partial(kernel, len(do)), outs,
        [dq, joined, joined, joined, *(array for array, unused in do), *rest],
        room(8, joined.shape[1]) + (16 if rest else 0), "attend_dkv", grid=(PAIRS // 2,),
        in_specs=[pl.BlockSpec((own, 128), lambda i: (0, i + shift))]
        + [pair(0, joined.shape[1]), pair(1, own), pair(2, own)]
        + specs + [whole(v) for v in rest],
        out_specs=[whole(o) for o in outs], scratch=scratch,
    )


def start_rows(fa, fb, span):
    return jnp.concatenate([fa[0:span, :], fb[0:span, :]], axis=0).astype(F32)


def gelu_both(u):
    c = math.sqrt(2.0 / math.pi)
    square = u * u
    t = jnp.tanh(c * u * (1.0 + 0.044715 * square))
    half = 0.5 * (1.0 + t)
    slope = half + 0.5 * u * (1.0 - t * t) * (c * (1.0 + 3 * 0.044715 * square))
    return u * half, slope


STEPS = FF // D


def fetch(pairs, sems):
    copies = [pltpu.make_async_copy(a, b, sems.at[i]) for i, (a, b) in enumerate(pairs)]
    for copy in copies:
        copy.start()
    return copies


def forward_kernel(span, order, *refs):
    count = len(order)
    info, cap_len, *blocks = refs[: 2 + count]
    (o, h1, mod, ca, cb, up_b, down_b, wo_h, wq_h, wkv_h, wc_h, up_h, down_h,
     big_o, out_o, away_o, cap_o, h2_o, o2_o, x1, dx2_o, attn_o, attn2_o, sums_o, kv2, q2, p2,
     wo, wq, wkv, wc, up, down, sems, x2, low, dh3, offset) = refs[2 + count :]
    cap_rows = blocks[0].shape[0] - span

    pairs = [(wkv_h, wkv), (wo_h, wo), (wq_h, wq), (wc_h, wc)]
    for i in range(STEPS):
        piece = pl.ds(i * D, D)
        pairs += [(up_h.at[:, piece], up.at[i]), (down_h.at[piece, :], down.at[i])]
    copies = fetch(pairs, sems)
    big_o[2 * STEPS + 2] = o[...]
    big_o[2 * STEPS + 3] = h1[...]

    gate1, shift2, scale2, gate2, shift3, scale3, gate3 = (
        mod[0:1, i * D : (i + 1) * D] for i in range(2, 9)
    )

    length = cap_len[2 * info[0] + info[2]]
    for i, k in enumerate(order):
        here = slice(i * cap_rows, (i + 1) * cap_rows)
        cap_o[here, :] = blocks[i][span:, :]
        first = jnp.bitwise_xor(info[1], k) * cap_rows
        token = first + lax.broadcasted_iota(jnp.int32, (cap_rows, 128), 0)
        offset[here, :] = jnp.where(token < length, 0.0, NEGATIVE)
    copies[0].wait()
    kv2[...] = dot(cap_o[...], wkv[...]).astype(BF16)

    copies[1].wait()
    attn = dot(o[...], wo[...])
    x1[...] = start_rows(blocks[0], blocks[1], span) + gate1 * attn
    attn_o[...] = attn.astype(BF16)
    n2, unused = norm(x1[...])
    h2 = (n2 * (1.0 + scale2) + shift2).astype(BF16)
    h2_o[...] = h2
    copies[2].wait()
    q2[...] = (dot(h2, wq[...]) * SCALE).astype(BF16)
    for i in range(PAIRS):
        qm = stack_heads(q2[:, cols(i)])
        scores = dot_nt(kv2[:, cols(i)], qm) + offset[:, 0:1]
        peak = jnp.max(scores, axis=0, keepdims=True)
        weights = jnp.exp(scores - peak)
        probs = (weights * (1.0 / jnp.sum(weights, axis=0, keepdims=True))).astype(BF16)
        p2[i] = probs
        both = dot(kv2[:, D + i * 128 : D + (i + 1) * 128].T, probs)
        o2_o[:, cols(i)] = unstack_t(both).astype(BF16)
    copies[3].wait()
    attn2 = dot(o2_o[...], wc[...])
    x2[...] = x1[...] + gate2 * attn2
    attn2_o[...] = attn2.astype(BF16)

    n3, unused = norm(x2[...])
    big_o[2 * STEPS] = (n3 * (1.0 + scale3) + shift3).astype(BF16)
    dy = jnp.concatenate([ca[...], cb[...]], axis=0).astype(F32)
    big_o[2 * STEPS + 1] = (gate3 * dy).astype(BF16)
    for i in range(STEPS):
        copies[4 + 2 * i].wait()
        copies[5 + 2 * i].wait()
        piece = slice(i * D, (i + 1) * D)
        acted, slope = gelu_both(dot(big_o[2 * STEPS], up[i]) + up_b[:, piece].astype(F32))
        acted = acted.astype(BF16)
        big_o[i] = acted
        dupper = (slope * dot_nt(big_o[2 * STEPS + 1], down[i])).astype(BF16)
        big_o[STEPS + i] = dupper
        sums_o[8 + i : 9 + i, :] = colsum(dupper.astype(F32))
        if i:
            low[...] += dot(acted, down[i])
            dh3[...] += dot_nt(dupper, up[i])
        else:
            low[...] = dot(acted, down[i])
            dh3[...] = dot_nt(dupper, up[i])
    lower = low[...] + down_b[...].astype(F32)
    value = x2[...]
    result = (value + gate3 * lower).astype(BF16)
    out_o[...] = result[:span]
    away_o[...] = result[span:]
    dy = jnp.concatenate([ca[...], cb[...]], axis=0).astype(F32)
    n3, rstd = norm(value)
    back = dh3[...]
    sums_o[0:4, :] = jnp.zeros((4, D), F32)
    sums_o[4:5, :] = colsum(back)
    sums_o[5:6, :] = colsum(n3 * back)
    sums_o[6:7, :] = colsum(lower * dy)
    sums_o[7:8, :] = colsum(big_o[2 * STEPS + 1].astype(F32))
    sums_o[12:16, :] = jnp.zeros((4, D), F32)
    dx2_o[...] = dy + norm_back(n3, rstd, (1.0 + scale3) * back)


def backward_kernel(dx2_r, mod, attn2, kv2, q2, p2, x1, attn, o, lse, h2, o2, sums3,
                    wc_h, wq_h, wo_h, wkv_h, fac_o, dx1_o, do_o, sums_o, wc, wq, wo, wkv, sems):
    copies = fetch([(wc_h, wc), (wq_h, wq), (wo_h, wo), (wkv_h, wkv)], sems)
    own = o.shape[0]
    slot = lambda i: slice(i * own, (i + 1) * own)
    gate1, scale2, gate2 = (mod[0:1, i * D : (i + 1) * D] for i in (2, 4, 5))
    sums_o[...] = sums3[...]
    fac_o[slot(0), :] = h2[...]
    fac_o[slot(2), :] = o2[...]
    dx2 = dx2_r[...]
    sums_o[3:4, :] = colsum(attn2[...].astype(F32) * dx2)
    da2 = (gate2 * dx2).astype(BF16)
    fac_o[slot(3), :] = da2
    copies[0].wait()
    do2 = dot_nt(da2, wc[...]).astype(BF16)
    for i in range(PAIRS):
        qm = stack_heads(q2[:, cols(i)])
        dom = stack_heads(do2[:, cols(i)])
        keys, values = kv2[:, cols(i)], kv2[:, D + i * 128 : D + (i + 1) * 128]
        probs = p2[i]
        fac_o[slot(5), cols(i)] = dot(probs, dom).astype(BF16)
        probs = probs.astype(F32)
        grad = dot_nt(values, dom)
        ds = (probs * (grad - colsum(probs * grad))).astype(BF16)
        fac_o[slot(1), cols(i)] = (unstack_t(dot(keys.T, ds)) * SCALE).astype(BF16)
        fac_o[slot(4), cols(i)] = dot(ds, qm).astype(BF16)
    copies[1].wait()
    dh2 = dot_nt(fac_o[slot(1), :], wq[...])
    n2, rstd = norm(x1[...])
    sums_o[1:2, :] = colsum(dh2)
    sums_o[2:3, :] = colsum(n2 * dh2)
    dx1 = dx2 + norm_back(n2, rstd, (1.0 + scale2) * dh2)
    dx1_o[...] = dx1
    sums_o[0:1, :] = colsum(attn[...].astype(F32) * dx1)

    da = (gate1 * dx1).astype(BF16)
    fac_o[slot(6), :] = da
    copies[2].wait()
    do = dot_nt(da, wo[...]).astype(BF16)
    do_o[0:own, :] = do
    both = do.astype(F32) * o[...].astype(F32)
    for i in range(PAIRS):
        t = both[:, cols(i)].T
        delta = [colsum(t[:HEAD]), colsum(t[HEAD:])]
        delta = [d[:, 128 * j : 128 * (j + 1)] for d in delta for j in range(own // 128)]
        sums = [lse[i][:, 128 * j : 128 * (j + 1)] for j in range(2 * own // 128)]
        held = [two_terms(jnp.concatenate(rows, axis=0)) for rows in (sums, delta)]
        do_o[own:, cols(i)] = jnp.concatenate(held, axis=0)
    copies[3].wait()
    dcap = (dot_nt(fac_o[slot(4), :], wkv[:, 0:D]) + dot_nt(fac_o[slot(5), :], wkv[:, D : 2 * D])).astype(BF16)
    cap_total = dcap.shape[0]
    fac_o[7 * own : 7 * own + cap_total, :] = dcap
    fac_o[7 * own + cap_total : 7 * own + cap_total + 16, :] = sums_o[...].astype(BF16)
    at = do_place(own, cap_total) * (own + 16)
    fac_o[7 * own + cap_total + 16 : at, :] = jnp.zeros((at - 7 * own - cap_total - 16, D), BF16)
    fac_o[at:, :] = do_o[...]


def forward(chain, info, cap_len, blocks, order, span, o, h1, mod, ca, cb, up_b, down_b, *weights):
    own = 2 * span
    cap_total = len(blocks) * (blocks[0][0].shape[1] - span)
    thin, wide = sds((own, D), BF16), sds((own, D), F32)
    half = sds((span, D), BF16)
    outs = [
        sds((2 * STEPS + 4, own, D), BF16), half, half, sds((cap_total, D), BF16), thin, thin, wide, wide,
        thin, thin, sds((16, D), F32), sds((cap_total, 2 * D), BF16), thin,
        sds((PAIRS, cap_total, 2 * own), BF16),
    ]
    here = [blocks[0][0], blocks[2][0], o, h1, mod, ca, cb, up_b, down_b]
    square = pltpu.VMEM((D, D), BF16)

    def kernel(info, cap_len, even, odd, *refs):
        forward_kernel(span, order, info, cap_len, *block_refs(order, even, odd), *refs)

    return chain(
        kernel, outs, [info, cap_len, *here, *weights], FWD, "forward",
        in_specs=[smem()] * 2 + [vmem()] * len(here) + [pl.BlockSpec(memory_space=pl.ANY)] * len(weights),
        scratch=[
            square, square, pltpu.VMEM((D, 2 * D), BF16), square,
            pltpu.VMEM((STEPS, D, D), BF16), pltpu.VMEM((STEPS, D, D), BF16),
            pltpu.SemaphoreType.DMA((4 + 2 * STEPS,)),
        ]
        + [pltpu.VMEM((own, D), F32)] * 3
        + [pltpu.VMEM((cap_total, 128), F32)],
    )


def do_place(own, cap_total):
    return -(-(7 * own + cap_total + 16) // (own + 16))


def backward(chain, here, weights):
    own = here[0].shape[0]
    cap_total = here[3].shape[0]
    outs = [
        sds(((do_place(own, cap_total) + 1) * (own + 16), D), BF16), sds((own, D), F32),
        sds((own + 16, D), BF16),
        sds((16, D), F32),
    ]
    square = pltpu.VMEM((D, D), BF16)
    return chain(
        backward_kernel, outs, [*here, *weights], BWD, "backward",
        in_specs=[vmem()] * len(here) + [pl.BlockSpec(memory_space=pl.ANY)] * len(weights),
        scratch=[square, square, square, pltpu.VMEM((D, 2 * D), BF16), pltpu.SemaphoreType.DMA((4,))],
    )


def pick_rows(info, x):
    source = lax.broadcasted_iota(jnp.int32, (D, D // 2), 0)
    column = lax.broadcasted_iota(jnp.int32, (D, D // 2), 1)
    block = sum((column >= 96 * i).astype(jnp.int32) for i in (1, 2, 3))
    wanted = 96 * jnp.bitwise_xor(info[1], 2 * block) + column - 96 * block
    choose = (source == wanted).astype(F32).astype(BF16)
    return dot(x, choose).astype(BF16)


def emit(first, info, tiles, blocks, send_o, keep_o):
    place = {True: 0, False: 0}
    for r in range(4):
        sent = bool(r & first)
        (send_o if sent else keep_o)[place[sent]] = tiles[jnp.bitwise_xor(info[0], r), blocks]
        place[sent] += 1


def down_grad_kernel(info, fac, fac_p, send_o, keep_o, tiles):
    for e in range(4):
        owner = jnp.bitwise_xor(info[1], 2 * e)
        half = pl.multiple_of(lax.rem(owner, 2) * 384, 128)
        where = (lax.div(owner, 2), slice(None), pl.ds(half, 384))
        grad = dot_tn(fac[where], fac[2 * STEPS + 1]) + dot_tn(fac_p[where], fac_p[9])
        for q in range(4):
            tiles[q, e] = grad[96 * q : 96 * (q + 1)].astype(BF16)
    emit(1, info, tiles, slice(0, 4), send_o, keep_o)


def up_grad_kernel(info, fac, fac_p, send_o, keep_o, tiles):
    x, xp = pick_rows(info, fac[8]), pick_rows(info, fac_p[8])
    for q in range(4):
        grad = dot_tn(x, fac[4 + q]) + dot_tn(xp, fac_p[4 + q])
        for e in range(4):
            tiles[q, e] = grad[96 * e : 96 * (e + 1)].astype(BF16)
    emit(2, info, tiles, slice(0, 4), send_o, keep_o)


def put(tiles, q, grad):
    for e in range(4):
        tiles[q, e] = grad[96 * e : 96 * (e + 1)].astype(BF16)


def emit_both(info, tiles, sx, kx, sy, ky):
    emit(1, info, tiles, slice(0, 2), sx, kx)
    emit(2, info, tiles, slice(2, 4), sy, ky)


def cross_grad_kernel(own, info, cap, fac, fac_p, sx, kx, sy, ky, tiles):
    def slot(ref, i):
        return ref[i * own : (i + 1) * own, :]

    def pair(x, y):
        left, left_p = pick_rows(info, slot(fac, x)), pick_rows(info, slot(fac_p, x))
        return dot_tn(left, slot(fac, y)) + dot_tn(left_p, slot(fac_p, y))

    put(tiles, 0, pair(0, 1))
    x = pick_rows(info, cap[...])
    rows = cap.shape[0] // 4
    xp = jnp.concatenate([x[rows * i : rows * (i + 1)] for i in (1, 0, 3, 2)], axis=0)
    for q in (1, 2):
        put(tiles, q, dot_tn(x, slot(fac, q + 3)) + dot_tn(xp, slot(fac_p, q + 3)))
    put(tiles, 3, pair(2, 3))
    emit_both(info, tiles, sx, kx, sy, ky)


def attn_grad_kernel(info, da, o, h1, da_p, o_p, h1_p, dqkv, dqkv_p, sx, kx, sy, ky, tiles):
    own = da.shape[0]
    x, xp = pick_rows(info, h1[0]), pick_rows(info, h1_p[0])
    for i in range(3):
        slot = slice(i * own, (i + 1) * own)
        put(tiles, i, dot_tn(x, dqkv[slot, :]) + dot_tn(xp, dqkv_p[slot, :]))
    x, xp = pick_rows(info, o[0]), pick_rows(info, o_p[0])
    put(tiles, 3, dot_tn(x, da[...]) + dot_tn(xp, da_p[...]))
    emit_both(info, tiles, sx, kx, sy, ky)


def grad_call(chain, kernel, info, args, name, shape, outs, in_specs=None):
    return chain(
        kernel, [sds(o, BF16) for o in outs], [info, *args], 20, name, grid=(1,) if in_specs else None,
        in_specs=[smem()] + (in_specs or [vmem()] * len(args)),
        scratch=[pltpu.VMEM(shape, BF16)],
    )


def total(*refs):
    return sum(r.astype(F32) for r in refs).astype(BF16)


def add_first_kernel(keep, recv, keep_o, send_o):
    keep_o[...] = total(keep[0], recv[0])
    send_o[...] = total(keep[1], recv[1])


def add_both_kernel(kx, rx, ky, ry, kx_o, sx_o, ky_o, sy_o):
    add_first_kernel(kx, rx, kx_o, sx_o)
    add_first_kernel(ky, ry, ky_o, sy_o)


def sum_rows(early, early_p, late, late_p):
    first = late[0:2, :].astype(F32) + late_p[0:2, :].astype(F32)
    both = early[0:12, :].astype(F32) + early_p[0:12, :].astype(F32)
    return jnp.concatenate([first, both, jnp.zeros((2, D), F32)], axis=0).astype(BF16)


def mlp_second_kernel(ka, ra, kb, rb, fac, fac_p, late, late_p, keep_o, send_o):
    for g, (keep, recv) in enumerate(((ka, ra), (kb, rb))):
        for e in range(4):
            (send_o if e % 2 else keep_o)[e // 2, 96 * g : 96 * (g + 1), :] = total(keep[e], recv[e])
    rows = sum_rows(fac, fac_p, late, late_p)
    for ref in (keep_o, send_o):
        for i in range(2):
            ref[i, 192:208, :] = rows


def mlp_third_kernel(keep, recv, keep_o, send_o):
    keep_o[...] = total(keep[0], recv[0])
    send_o[0:192, :] = total(keep[1, 0:192, :], recv[1, 0:192, :])
    send_o[192:208, :] = total(keep[0, 192:208, :], recv[0, 192:208, :])


def mlp_fourth_kernel(keep, recv, out):
    out[0:192, :] = total(keep[0:192, :], recv[0:192, :])
    out[192:208, :] = keep[192:208, :]
    out[208:224, :] = recv[192:208, :]


def order_place(k):
    return 2 * (k % 4) + k // 4


def second_kernel(kx, rx, ky, ry, *refs):
    caption, (keep_o, send_o) = refs[:-2], refs[-2:]
    for e in range(4):
        out = send_o if e % 2 else keep_o
        keep, recv = ((kx, rx), (ky, ry))[e // 2]
        out[e // 2, 0:96, :] = total(keep[e % 2], recv[e % 2])
        if caption:
            dcap, dcap_p = caption
            rows = dcap.shape[0] // 8
            at, at_p = (rows * order_place(2 * e + i) for i in range(2))
            out[e // 2, 96:, :] = total(dcap[at : at + rows, :], dcap_p[at_p : at_p + rows, :])


def third_kernel(keep, recv, keep_o, send_o):
    keep_o[...] = total(keep[0], recv[0])
    send_o[...] = total(keep[1], recv[1])


def fourth_kernel(keep, recv, c_keep, c_recv, out, same_o, away_o):
    out[0:96, :] = total(keep[...], recv[...])
    out[96:, :] = total(c_keep[0:96, :], c_recv[0:96, :])
    same_o[...] = c_keep[96:, :].astype(F32)
    away_o[...] = c_recv[96:, :].astype(F32)


def swap(x, axis, size, k):
    return lax.ppermute(x, axis, [(i, i ^ k) for i in range(size)])


def over_x(x):
    return swap(x, "band", 4, 1)


def over_y(x):
    return swap(x, "band", 4, 2)


def to_band(x):
    return [x] + [swap(x, "band", 4, t) for t in (1, 2, 3)]


def mlp_finish_kernel(info, t0, t1, t2, t3, down_o, up_o):
    for r, tile in enumerate((t0, t1, t2, t3)):
        q = jnp.bitwise_xor(info[0], r)
        down_o[pl.ds(pl.multiple_of(96 * q, 96), 96), :] = tile[0:96, :].astype(F32)
        up_o[:, pl.ds(pl.multiple_of(D * q, D), D)] = tile[96:192, :].astype(F32)


def last_finish_kernel(info, t0, t1, t2, t3, in_o, out_o, cq_o, ckv_o, co_o, tiles):
    for r, tile in enumerate((t0, t1, t2, t3)):
        tiles[jnp.bitwise_xor(info[0], r)] = tile[...]
    for i in range(3):
        in_o[:, i * D : (i + 1) * D] = tiles[i, 0:96, :].astype(F32)
    out_o[...] = tiles[3, 0:96, :].astype(F32)
    cq_o[...] = tiles[0, 96:, :].astype(F32)
    ckv_o[:, 0:D] = tiles[1, 96:, :].astype(F32)
    ckv_o[:, D:] = tiles[2, 96:, :].astype(F32)
    co_o[...] = tiles[3, 96:, :].astype(F32)


def finish(chain, kernel, info, tiles, widths, name, scratch=(), held=()):
    outs = [sds(w, F32) for w in widths] + [sds(h.shape, h.dtype) for h in held]
    tiles = [*tiles, *held]
    return chain(
        kernel, outs, [info, *tiles], 12, name, grid=(1,), in_specs=[smem()] + [whole(t) for t in tiles],
        out_specs=[whole(o) for o in outs], scratch=scratch,
    )


def plain_reduce(x, y, owners):
    grad = lax.psum_scatter(dot_tn(x, y).astype(BF16), "seq", scatter_dimension=0, tiled=True)
    return lax.psum(grad, "band").astype(F32)


def on_device(bands, seqs, frames, caption, timesteps, cap_len, attn_in, attn_out, cross_query,
              cross_keyval, cross_out, mlp_up, up_bias, mlp_down, down_bias, ada_weight, ada_bias,
              time_first, first_bias, time_second, second_bias, cotangent):
    span = frames.shape[1]
    own = 2 * span
    cap_rows = caption.shape[1]
    items = timesteps.shape[0]
    halves = seqs // 2
    band = lax.axis_index("band")
    seq = lax.axis_index("seq")
    half = (seq >= halves).astype(jnp.int32)
    item = 2 * band + half
    info = jnp.stack([band, seq, half]).astype(jnp.int32)

    chain = Chain()

    order = [k for i in range(halves) for k in (i, i + halves)]
    same, other = pick(chain, info, frames, caption)
    even = [same] + [swap(same if k < halves else other, "seq", seqs, k) for k in range(2, seqs, 2)]

    steps = jnp.take(timesteps, jnp.bitwise_xor(jnp.arange(items), item))
    width = time_first.shape[0] // 2
    freq = jnp.exp(-math.log(10000.0) * jnp.arange(width, dtype=F32) / width)
    angle = steps.astype(F32)[:, None] * freq[None, :]
    embed = jnp.concatenate([jnp.cos(angle), jnp.sin(angle)], axis=1)
    row = lambda v: v.reshape(1, -1)
    pre_cond, mod = modulation(
        chain, embed, time_first, row(first_bias), time_second, row(second_bias), ada_weight, row(ada_bias)
    )
    cot_own, cot_other = pick(chain, info, cotangent)
    cot_other = swap(cot_other, "seq", seqs, halves)

    even = stack(chain, even, "blocks")
    odd = swap(even, "seq", seqs, 1)
    blocks = [(odd if k % 2 else even, k // 2) for k in order]
    joined, h1 = qkv(chain, blocks, order, span, mod, attn_in)
    mixed, lse = attend(chain, joined, own)

    cap_total = seqs * cap_rows
    (big, out, out_back, cap_all, h2, o2, x1, dx2, attn, attn2, sums3, kv2, q2, p2) = forward(
        chain, info, cap_len, blocks, order, span, mixed, h1, mod, cot_own, cot_other, row(up_bias),
        row(down_bias), attn_out, cross_query, cross_keyval, cross_out, mlp_up, mlp_down,
    )
    fast = bands == 4 and seqs == 8
    if fast:
        big_p = swap(big, "seq", seqs, 1)
    fac, dx1, do, early = backward(
        chain, [dx2, mod, attn2, kv2, q2, p2, x1, attn, mixed, lse, h2, o2, sums3],
        [cross_out, cross_query, attn_out, cross_keyval],
    )
    if fast:
        fac_p = swap(fac, "seq", seqs, 1)
    got = {k: (swap(do, "seq", seqs, k), 0) for k in range(2 if fast else 1, halves)}
    got[0] = (do, 0)
    if fast:
        got[1] = (fac_p, do_place(own, cap_total))
        whole_tiles, pieces, halved = (4, 4, 96, D), [(2, 4, 96, D)] * 2, [(2, 2, 96, D)] * 4
        args = [big, big_p]
        sa, ka = grad_call(chain, down_grad_kernel, info, args, "down_grad", whole_tiles, pieces)
        ra = over_x(sa)
        sb, kb = grad_call(chain, up_grad_kernel, info, args, "up_grad", whole_tiles, pieces)
        rb = over_y(sb)
        cx, ckx, cy, cky = grad_call(
            chain, functools.partial(cross_grad_kernel, own), info, [cap_all, fac, fac_p], "cross_grad",
            whole_tiles, halved,
        )
        crx, cry = over_x(cx), over_y(cy)
    dq = attend_dq(chain, joined, do)
    do_blocks = [got[k] for k in range(halves)]
    dkv_first = attend_dkv(chain, dq, joined, do_blocks, 0)[0]
    dqkv, grad_own, back = attend_dkv(
        chain, dq, joined, do_blocks, 1, [dkv_first, even, attn_in, mod, dx1, out_back]
    )
    back = swap(back, "seq", seqs, halves)
    if fast:
        dqkv_p = swap(dqkv, "seq", seqs, 1)
        half, quarter, tile = sds((4, 96, D), BF16), sds((2, 96, D), BF16), sds((96, D), BF16)
        ka, sa = chain(add_first_kernel, [half] * 2, [ka, ra], 4, "down_add1")
        ra = over_y(sa)
        kb, sb = chain(add_first_kernel, [half] * 2, [kb, rb], 4, "up_add1")
        rb = over_x(sb)
        slots = [pl.BlockSpec((own, D), lambda *i: (6, 0))] + [
            pl.BlockSpec((1, own, D), functools.partial(lambda at, *i: (at, 0, 0), at))
            for at in (2 * STEPS + 2, 2 * STEPS + 3)
        ]
        tx, tkx, ty, tky = grad_call(
            chain, attn_grad_kernel, info, [fac, big, big, fac_p, big_p, big_p, dqkv, dqkv_p], "attn_grad",
            whole_tiles, halved, in_specs=slots * 2 + [whole(dqkv)] * 2,
        )
        trx, try_ = over_x(tx), over_y(ty)
        grad_frames, out = place(
            chain, info, [(grad_own, (back, 0)), (out, (back, 1))], [F32, BF16], "place_frames"
        )
        cap_at, sum_at, late_at = 7 * own // cap_total, (7 * own + cap_total) // 16, 3 * own // 16
        cap_spec = pl.BlockSpec((cap_total, D), lambda *i: (cap_at, 0))
        sum_spec = pl.BlockSpec((16, D), lambda *i: (sum_at, 0))
        late_spec = pl.BlockSpec((16, D), lambda *i: (late_at, 0))
        ckx, cx, cky, cy = chain(add_both_kernel, [quarter] * 4, [ckx, crx, cky, cry], 4, "cross_add1")
        crx, cry = over_y(cx), over_x(cy)
        keep, send = chain(
            mlp_second_kernel, [sds((2, 208, D), BF16)] * 2, [ka, ra, kb, rb, fac, fac_p, dqkv, dqkv_p], 4,
            "mlp_add2", grid=(1,), in_specs=[vmem()] * 4 + [sum_spec] * 2 + [late_spec] * 2,
        )
        recv = swap(send, "seq", seqs, 2)
        tkx, tx, tky, ty = chain(add_both_kernel, [quarter] * 4, [tkx, trx, tky, try_], 4, "attn_add1")
        trx, try_ = over_y(tx), over_x(ty)
        keep, send = chain(mlp_third_kernel, [sds((208, D), BF16)] * 2, [keep, recv], 4, "mlp_z1")
        recv = swap(send, "seq", seqs, 4)
        rows = 96 + cap_rows
        c_keep, c_send = chain(
            second_kernel, [sds((2, rows, D), BF16)] * 2, [ckx, crx, cky, cry, fac, fac_p], 4, "cross_add2",
            grid=(1,), in_specs=[vmem()] * 4 + [cap_spec] * 2,
        )
        c_recv = swap(c_send, "seq", seqs, 2)
        t_keep, t_send = chain(second_kernel, [quarter] * 2, [tkx, trx, tky, try_], 4, "attn_add2")
        t_recv = swap(t_send, "seq", seqs, 2)
        a_all = to_band(chain(mlp_fourth_kernel, [sds((224, D), BF16)], [keep, recv], 4, "mlp_z2")[0])
        c_keep, c_send = chain(third_kernel, [sds((rows, D), BF16)] * 2, [c_keep, c_recv], 4, "cross_z1")
        c_recv = swap(c_send, "seq", seqs, 4)
        t_keep, t_send = chain(third_kernel, [tile] * 2, [t_keep, t_recv], 4, "attn_z1")
        t_recv = swap(t_send, "seq", seqs, 4)
        t_done, cap_same, cap_away = chain(
            fourth_kernel, [sds((192, D), BF16)] + [sds((cap_rows, D), F32)] * 2,
            [t_keep, t_recv, c_keep, c_recv], 4, "other_z2",
        )
        t_all = to_band(t_done)
        g_down, g_up = finish(chain, mlp_finish_kernel, info, a_all, [(384, D), (96, FF)], "mlp_finish")
        grad_caption = place(chain, info, [(cap_same, cap_away)], [F32], "place_caption")[0]
        sums = a_all
    else:
        grad_frames, out = place(
            chain, info, [(grad_own, (back, 0)), (out, (back, 1))], [F32, BF16], "place_frames"
        )
        dcap = fac[7 * own : 7 * own + cap_total].reshape(seqs, cap_rows, D)
        place_of = jnp.asarray([order.index(k) for k in range(seqs)])
        dcap = dcap[place_of[jnp.bitwise_xor(seq, jnp.arange(seqs))]].reshape(cap_total, D)
        dcap = jnp.where(half == 0, jnp.stack([dcap, 0 * dcap]), jnp.stack([0 * dcap, dcap]))
        grad_caption = lax.psum_scatter(dcap, "seq", scatter_dimension=1, tiled=True).astype(F32)
        rows = jnp.concatenate([dqkv[3 * own : 3 * own + 2].astype(F32), early[0:12], jnp.zeros((2, D), F32)])
        for k in range(1, halves):
            if k & (k - 1) == 0:
                rows = rows + swap(rows, "seq", seqs, k)
        rows = jnp.concatenate([rows, swap(rows, "seq", seqs, halves)]).astype(BF16)
        sums = [rows] + [swap(rows, "band", bands, t) for t in range(1, bands)]

    g_ada, gb_ada, g_t2, gb_t2, g_t1, gb_t1, gb_down, gb_up = mod_back(
        chain, info, sums, ada_weight, pre_cond, embed, time_second, seqs
    )

    if fast:
        g_in, g_out, g_cq, g_ckv, g_co = finish(
            chain, last_finish_kernel, info, t_all, [(96, 3 * D), (96, D), (96, D), (96, 2 * D), (96, D)],
            "last_finish", [pltpu.VMEM((4, 192, D), BF16)],
        )
    else:
        slot = lambda i: fac[i * own : (i + 1) * own]
        acted = jnp.concatenate([big[i] for i in range(FF // D)], axis=1)
        dupper = jnp.concatenate([big[FF // D + i] for i in range(FF // D)], axis=1)
        g_down = plain_reduce(acted, big[2 * STEPS + 1], seqs)
        g_up = plain_reduce(big[2 * STEPS], dupper, seqs)
        g_cq = plain_reduce(slot(0), slot(1), seqs)
        g_ckv = plain_reduce(cap_all, jnp.concatenate([slot(4), slot(5)], axis=1), seqs)
        g_co = plain_reduce(slot(2), slot(3), seqs)
        g_out = plain_reduce(mixed, slot(6), seqs)
        g_in = plain_reduce(h1, jnp.concatenate([dqkv[i * own : (i + 1) * own] for i in range(3)], axis=1), seqs)

    flat = lambda v: v.reshape(-1)
    return (
        out, grad_frames, grad_caption, g_in, g_out, g_cq, g_ckv, g_co, g_up, flat(gb_up), g_down,
        flat(gb_down), g_ada, flat(gb_ada), g_t1, flat(gb_t1), g_t2, flat(gb_t2),
    )


def solution(mesh):
    split = P("band", "seq", None)
    rows, flat = P("seq", None), P("seq")
    return jax.shard_map(
        functools.partial(on_device, mesh.shape["band"], mesh.shape["seq"]),
        mesh=mesh,
        in_specs=(split, split) + (P(),) * 17 + (split,),
        out_specs=(split, split, split, rows, rows, rows, rows, rows, rows, flat, rows, flat, rows, flat,
                   rows, flat, rows, flat),
        check_vma=False,
    )
```

```python
import functools
import math

import jax
import jax.numpy as jnp
from jax import lax
from jax.experimental import pallas as pl
from jax.experimental.pallas import tpu as pltpu
from jax.sharding import PartitionSpec as P

D = 768
HEAD = 64
PAIRS = 6
FF = 3072
EPSILON = 1e-06
NEGATIVE = -1e30
SCALE = 0.125
F32 = jnp.float32
BF16 = jnp.bfloat16
MIB = 1 << 20
MODMIB = 4
COST = 1000000
FWD = 19
BWD = 9


def dot(a, b):
    return jnp.dot(a, b, preferred_element_type=F32)


def dot_nt(a, b):
    return lax.dot_general(a, b, (((1,), (1,)), ((), ())), preferred_element_type=F32)


def dot_tn(a, b):
    return lax.dot_general(a, b, (((0,), (0,)), ((), ())), preferred_element_type=F32)


def split_dot(x, w, contract=0):
    high = x.astype(BF16).astype(F32)
    both = jnp.concatenate([high, x - high], axis=0).astype(BF16)
    out = lax.dot_general(
        both, w, (((1,), (contract,)), ((), ())), preferred_element_type=F32
    )
    return out[: x.shape[0]] + out[x.shape[0] :]


def silu(v):
    return v * (1.0 / (1.0 + jnp.exp(-v)))


def silu_grad(v):
    s = 1.0 / (1.0 + jnp.exp(-v))
    return s * (1.0 + v * (1.0 - s))


def norm(v):
    mean = jnp.mean(v, axis=-1, keepdims=True)
    centred = v - mean
    spread = jnp.mean(centred * centred, axis=-1, keepdims=True)
    rstd = lax.rsqrt(spread + EPSILON)
    return centred * rstd, rstd


def norm_back(n, rstd, w):
    return (
        w - jnp.mean(w, axis=-1, keepdims=True) - n * jnp.mean(w * n, axis=-1, keepdims=True)
    ) * rstd


def colsum(v):
    return jnp.sum(v, axis=0, keepdims=True)


def cols(i):
    return slice(i * 128, (i + 1) * 128)


def head_masks():
    lane = lax.broadcasted_iota(jnp.int32, (1, 128), 1)
    first = (lane < HEAD).astype(F32)
    return first.astype(BF16), (1.0 - first).astype(BF16)


def stack_heads(block):
    first, second = head_masks()
    return jnp.concatenate([block * first, block * second], axis=0)


def unstack_t(both):
    rows = both.shape[1] // 2
    pair = jnp.concatenate([both[:HEAD, :rows], both[HEAD:, rows:]], axis=0)
    return pair.T


def sds(shape, dtype):
    return jax.ShapeDtypeStruct(shape, dtype)


def vmem():
    return pl.BlockSpec(memory_space=pltpu.VMEM)


def smem():
    return pl.BlockSpec(memory_space=pltpu.SMEM)


def whole(a):
    return pl.BlockSpec(a.shape, lambda *i: (0,) * len(a.shape))


class Chain:
    def __init__(self):
        self.token = None

    def __call__(self, kernel, outs, args, mib, name, grid=None, in_specs=None, out_specs=None, scratch=()):
        outs = list(outs)
        in_specs = list(in_specs or [vmem()] * len(args))
        out_specs = list(out_specs or [vmem()] * len(outs))
        count = len(args)
        body = kernel
        if self.token is not None:
            args = [*args, self.token]
            in_specs.append(pl.BlockSpec(memory_space=pl.ANY))
            body = lambda *refs: kernel(*refs[:count], *refs[count + 1 :])
        results = pl.pallas_call(
            body,
            **({} if grid is None else {"grid": grid}),
            out_shape=outs,
            in_specs=in_specs,
            out_specs=out_specs,
            scratch_shapes=list(scratch),
            compiler_params=pltpu.CompilerParams(vmem_limit_bytes=mib * MIB),
            cost_estimate=pl.CostEstimate(flops=1000, bytes_accessed=COST, transcendentals=0),
            name=name,
        )(*args)
        self.token = min(results, key=lambda r: r.size * r.dtype.itemsize)
        return results

    def after(self, x):
        self.token = x


def room(mib, frames):
    return min(56, mib * max(1, frames // 1024))


def pick_kernel(info, *refs):
    half = info[2]
    parts, (mine_o, theirs_o, sems) = refs[:-3], refs[-3:]
    copies = []
    at = 0
    for x in parts:
        rows = pl.ds(at, x.shape[1])
        for source, out in ((half, mine_o), (1 - half, theirs_o)):
            copies.append(pltpu.make_async_copy(x.at[source], out.at[rows], sems.at[len(copies)]))
        at += x.shape[1]
    for copy in copies:
        copy.start()
    for copy in copies:
        copy.wait()


def pick(chain, info, *parts):
    out = sds((sum(x.shape[1] for x in parts), D), BF16)
    anywhere = pl.BlockSpec(memory_space=pl.ANY)
    return chain(
        pick_kernel, [out, out], [info, *parts], 4, "pick", in_specs=[smem()] + [anywhere] * len(parts),
        out_specs=[anywhere] * 2, scratch=[pltpu.SemaphoreType.DMA((2 * len(parts),))],
    )


def stack_kernel(*refs):
    for i, ref in enumerate(refs[:-1]):
        refs[-1][i] = ref[...]


def stack(chain, arrays, name):
    out = sds((len(arrays),) + arrays[0].shape, arrays[0].dtype)
    return chain(stack_kernel, [out], arrays, 4, name)[0]


def place_kernel(info, *refs):
    count = len(refs) // 3
    for i in range(count):
        kept, received, out = refs[2 * i], refs[2 * i + 1], refs[2 * count + i]
        out[info[2]] = kept[...].astype(out.dtype)
        out[1 - info[2]] = received[...].reshape(kept.shape).astype(out.dtype)


def place(chain, info, pairs, dtypes, name):
    args, specs = [info], [smem()]
    for kept, received in pairs:
        args.append(kept)
        specs.append(whole(kept))
        if isinstance(received, tuple):
            args.append(received[0])
            specs.append(pl.BlockSpec((1,) + kept.shape, functools.partial(lambda at, i: (at, 0, 0), received[1])))
        else:
            args.append(received)
            specs.append(whole(received))
    outs = [sds((2,) + kept.shape, dtype) for (kept, unused), dtype in zip(pairs, dtypes)]
    return chain(
        place_kernel, outs, args, 4, name, grid=(1,), in_specs=specs, out_specs=[whole(o) for o in outs]
    )


def mod_kernel(embed, t1, b1, t2, b2, w, b, both_o, mod_o, act):
    @pl.when(pl.program_id(0) == 0)
    def _():
        pre = split_dot(embed[...], t1[...]) + b1[...].astype(F32)
        cond = split_dot(silu(pre), t2[...]) + b2[...].astype(F32)
        both_o[0] = pre
        both_o[1] = cond
        act[...] = silu(cond)

    mod_o[...] = split_dot(act[...], w[...]) + b[...].astype(F32)


def modulation(chain, embed, t1, b1, t2, b2, w, b):
    items = embed.shape[0]
    outs = [sds((2, items, D), F32), sds((items, 9 * D), F32)]
    return chain(
        mod_kernel, outs, [embed, t1, b1, t2, b2, w, b], MODMIB, "modulation", grid=(9,),
        in_specs=[whole(v) for v in (embed, t1, b1, t2, b2)]
        + [pl.BlockSpec((D, D), lambda i: (0, i)), pl.BlockSpec((1, D), lambda i: (0, i))],
        out_specs=[whole(outs[0]), pl.BlockSpec((items, D), lambda i: (0, i))],
        scratch=[pltpu.VMEM((items, D), F32)],
    )


def outer_sum(left_t, right):
    lh = left_t.astype(BF16)
    ll = (left_t - lh.astype(F32)).astype(BF16)
    rh = right.astype(BF16)
    rl = (right - rh.astype(F32)).astype(BF16)
    return dot(lh, rh) + dot(ll, rh) + dot(lh, rl)


def own_rows_t(info, size, v):
    row = lax.broadcasted_iota(jnp.int32, (size, v.shape[1]), 0)
    column = lax.broadcasted_iota(jnp.int32, (size, v.shape[1]), 1)
    choose = (column == row + size * info[1]).astype(F32).astype(BF16)
    high = v.astype(BF16)
    rest = (v - high.astype(F32)).astype(BF16)
    return dot_nt(choose, high) + dot_nt(choose, rest)


def mod_back_kernel(bands, seqs, info, *refs):
    sums = refs[:bands]
    (both, embed, t2, w_h, g_ada_h, gb_ada, g_t2, gb_t2, g_t1, gb_t1, gb_down, gb_up,
     w, g_ada, sems, acc, dmod, all_bias) = refs[bands:]
    pieces = [pl.ds(i * D, D) for i in range(9)]
    copies = fetch([(w_h.at[:, piece], w.at[i]) for i, piece in enumerate(pieces)], sems)
    own_act = own_rows_t(info, D // seqs, silu(both[1]))
    bias = jnp.zeros((5, D), F32)
    for t in range(bands):
        held = sums[t][sums[t].shape[0] - 32 :, :].astype(F32)
        for u in range(2):
            r = 2 * t + u
            for p in range(9):
                dmod[p, r : r + 1, :] = held[16 * u + p : 16 * u + p + 1]
            bias += held[16 * u + 9 : 16 * u + 14]
    stores = []
    for i, piece in enumerate(pieces):
        part = dmod[i]
        g_ada[i] = outer_sum(own_act, part)
        stores.append(pltpu.make_async_copy(g_ada.at[i], g_ada_h.at[:, piece], sems.at[9 + i]))
        stores[-1].start()
        all_bias[:, i * D : (i + 1) * D] = jnp.broadcast_to(colsum(part), (8, D))
        copies[i].wait()
        term = split_dot(part, w[i], contract=1)
        if i:
            acc[...] += term
        else:
            acc[...] = term

    def own_part(row):
        size = row.shape[1] // seqs
        rows = jnp.broadcast_to(row, (8, row.shape[1]))
        return pltpu.roll(rows, row.shape[1] - info[1] * size, 1)[0:1, 0:size]

    size = 9 * D // seqs
    gb_ada[...] = pltpu.roll(all_bias[...], 9 * D - info[1] * size, 1)[0:1, 0:size]
    gb_down[...] = own_part(bias[0:1])
    gb_up[...] = own_part(jnp.concatenate([bias[1 + i : 2 + i] for i in range(4)], axis=1))
    dcond = acc[...] * silu_grad(both[1])
    g_t2[...] = outer_sum(own_rows_t(info, D // seqs, silu(both[0])), dcond)
    gb_t2[...] = own_part(colsum(dcond))
    dpre = split_dot(dcond, t2[...], contract=1) * silu_grad(both[0])
    g_t1[...] = outer_sum(own_rows_t(info, g_t1.shape[0], embed[...]), dpre)
    gb_t1[...] = own_part(colsum(dpre))
    for store in stores:
        store.wait()


def mod_back(chain, info, sums, w, both, embed, t2, seqs):
    bands = len(sums)
    items = 2 * bands
    m = D // seqs
    line = lambda n: sds((1, n // seqs), F32)
    outs = [
        sds((m, 9 * D), F32), line(9 * D), sds((m, D), F32), line(D), sds((embed.shape[1] // seqs, D), F32),
        line(D), line(D), line(FF),
    ]
    anywhere = pl.BlockSpec(memory_space=pl.ANY)
    here = [*sums, both, embed, t2]
    return chain(
        functools.partial(mod_back_kernel, bands, seqs), outs, [info, *here, w], 15, "modulation_back",
        grid=(1,), in_specs=[smem()] + [whole(v) for v in here] + [anywhere],
        out_specs=[anywhere] + [whole(o) for o in outs[1:]],
        scratch=[
            pltpu.VMEM((9, D, D), BF16), pltpu.VMEM((9, m, D), F32), pltpu.SemaphoreType.DMA((18,)),
            pltpu.VMEM((items, D), F32), pltpu.VMEM((9, items, D), F32), pltpu.VMEM((8, 9 * D), F32),
        ],
    )


def block_refs(order, even, odd):
    return [(odd if k % 2 else even).at[k // 2] for k in order]


def qkv_kernel(order, span, even, odd, mod, w, out, h1_o, h1):
    frames = block_refs(order, even, odd)
    blocks = len(order)
    own = 2 * span

    @pl.when(pl.program_id(0) == 0)
    def _():
        shift, scale = mod[0:1, 0:D], mod[0:1, D : 2 * D]
        for i in range(blocks):
            n, unused = norm(frames[i][0:span, :].astype(F32))
            h1[pl.ds(i * span, span), :] = (n * (1.0 + scale) + shift).astype(BF16)
        h1_o[...] = h1[0:own, :]

    factor = jnp.where(pl.program_id(0) == 0, SCALE, 1.0)

    @pl.loop(0, blocks * span // own)
    def _(i):
        rows = pl.ds(pl.multiple_of(i * own, own), own)
        out[0, rows, :] = (dot(h1[rows, :], w[...]) * factor).astype(BF16)


def qkv(chain, blocks, order, span, mod, w):
    total = len(order) * span
    outs = [sds((3, total, D), BF16), sds((2 * span, D), BF16)]
    args = [blocks[0][0], blocks[2][0], mod]
    return chain(
        functools.partial(qkv_kernel, order, span), outs, [*args, w], room(16, total), "qkv", grid=(3,),
        in_specs=[whole(v) for v in args] + [pl.BlockSpec((D, D), lambda i: (0, i))],
        out_specs=[pl.BlockSpec((1, total, D), lambda i: (i, 0, 0)), whole(outs[1])],
        scratch=[pltpu.VMEM((total, D), BF16)],
    )


def attend_kernel(q, k, v, o, lse):
    qm = stack_heads(q[0])
    scores = dot_nt(k[0], qm)
    peak = jnp.max(scores, axis=0, keepdims=True)
    weights = jnp.exp(scores - peak)
    total = jnp.sum(weights, axis=0, keepdims=True)
    both = dot(v[0].T, weights.astype(BF16)) * (1.0 / total)
    o[...] = unstack_t(both).astype(BF16)
    lse[0] = peak + jnp.log(total)


def part_spec(part, rows):
    return pl.BlockSpec((1, rows, 128), lambda i: (part, 0, i))


def attend(chain, joined, own):
    total = joined.shape[1]
    return chain(
        attend_kernel, [sds((own, D), BF16), sds((PAIRS, 1, 2 * own), F32)], [joined] * 3, room(8, total),
        "attend", grid=(PAIRS,),
        in_specs=[part_spec(0, own), part_spec(1, total), part_spec(2, total)],
        out_specs=[
            pl.BlockSpec((own, 128), lambda i: (0, i)),
            pl.BlockSpec((1, 1, 2 * own), lambda i: (i, 0, 0)),
        ],
    )


def qkv_attend_kernel(order, span, even, odd, mod, w, out_h, h1_o, o, lse, h1, joined, sems):
    own = 2 * span
    total = joined.shape[1]
    shift, scale = mod[0:1, 0:D], mod[0:1, D : 2 * D]
    for i, block in enumerate(block_refs(order, even, odd)):
        n, unused = norm(block[0:span, :].astype(F32))
        h1[pl.ds(i * span, span), :] = (n * (1.0 + scale) + shift).astype(BF16)
    h1_o[...] = h1[0:own, :]
    stores = []
    for part in (1, 2, 0):
        piece = w[:, part * D : (part + 1) * D]
        for i in range(total // own):
            rows = slice(i * own, (i + 1) * own)
            value = dot(h1[rows, :], piece)
            joined[part, rows, :] = ((value * SCALE) if part == 0 else value).astype(BF16)
        stores.append(pltpu.make_async_copy(joined.at[part], out_h.at[part], sems.at[part]))
        stores[-1].start()
    for i in range(PAIRS):
        qm = stack_heads(joined[0, 0:own, cols(i)])
        scores = dot_nt(joined[1, :, cols(i)], qm)
        peak = jnp.max(scores, axis=0, keepdims=True)
        weights = jnp.exp(scores - peak)
        sums = jnp.sum(weights, axis=0, keepdims=True)
        both = dot(joined[2, :, cols(i)].T, weights.astype(BF16)) * (1.0 / sums)
        o[:, cols(i)] = unstack_t(both).astype(BF16)
        lse[i] = peak + jnp.log(sums)
    for store in stores:
        store.wait()


def qkv_attend(chain, blocks, order, span, mod, w):
    total, own = len(order) * span, 2 * span
    if total > 1024:
        joined, h1 = qkv(chain, blocks, order, span, mod, w)
        mixed, lse = attend(chain, joined, own)
        return joined, h1, mixed, lse
    outs = [
        sds((3, total, D), BF16), sds((own, D), BF16), sds((own, D), BF16), sds((PAIRS, 1, 2 * own), F32)
    ]
    return chain(
        functools.partial(qkv_attend_kernel, order, span), outs, [blocks[0][0], blocks[2][0], mod, w], 10,
        "qkv_attend", out_specs=[pl.BlockSpec(memory_space=pl.ANY)] + [vmem()] * 3,
        scratch=[
            pltpu.VMEM((total, D), BF16), pltpu.VMEM((3, total, D), BF16), pltpu.SemaphoreType.DMA((3,))
        ],
    )


def two_terms(rows):
    high = rows.astype(BF16).astype(F32)
    return jnp.concatenate([high, rows - high], axis=0).astype(BF16)


def read_stats(block):
    own = block.shape[0] - 16
    held = block[own:, :].astype(F32)

    def line(at):
        rows = held[at : at + 4] + held[at + 4 : at + 8]
        return jnp.concatenate([rows[i : i + 1] for i in range(4)], axis=1)

    return line(0), line(8)


def attend_dq_kernel(q, k, v, do, dq):
    own = do.shape[0] - 16
    qm = stack_heads(q[0])
    dom = stack_heads(do[0:own, :])
    lse, delta = read_stats(do)
    probs = jnp.exp(dot_nt(k[0], qm) - lse)
    grad = dot_nt(v[0], dom)
    ds = (probs * (grad - delta)).astype(BF16)
    dq[...] = (unstack_t(dot(k[0].T, ds)) * SCALE).astype(BF16)


def attend_dq(chain, joined, do):
    own = do.shape[0] - 16
    total = joined.shape[1]
    return chain(
        attend_dq_kernel, [sds((own, D), BF16)], [joined, joined, joined, do], room(5, total),
        "attend_dq", grid=(PAIRS,),
        in_specs=[
            part_spec(0, own), part_spec(1, total), part_spec(2, total),
            pl.BlockSpec((own + 16, 128), lambda i: (0, i)),
        ],
        out_specs=[pl.BlockSpec((own, 128), lambda i: (0, i))],
    )[0]


def attend_dkv_kernel(chunks, dq, q, k, v, *refs):
    do, out = refs[:chunks], refs[-1]
    keys, values = k[0], v[0]
    own = keys.shape[0]
    dk = jnp.zeros((own, 128), F32)
    dv = jnp.zeros((own, 128), F32)
    for i in range(chunks):
        qm = stack_heads(q[0, i * own : (i + 1) * own, :])
        block = do[i][...]
        dom = stack_heads(block[0:own, :])
        lse, delta = read_stats(block)
        probs = jnp.exp(dot_nt(keys, qm) - lse)
        dv += dot(probs.astype(BF16), dom)
        grad = dot_nt(values, dom)
        ds = (probs * (grad - delta)).astype(BF16)
        dk += dot(ds, qm)
    lanes = pl.ds(pl.multiple_of(128 * pl.program_id(0), 128), 128)
    out[0:own, lanes] = dq[...]
    out[own : 2 * own, lanes] = dk.astype(BF16)
    out[2 * own : 3 * own, lanes] = dv.astype(BF16)


def last_kernel(chunks, *refs):
    first, even, w, mod, dx1, away, out, own_o, back_o, part = refs[4 + chunks :]
    attend_dkv_kernel(chunks, *refs[: 4 + chunks], part)
    own = part.shape[0] // 3
    half = part.shape[1]

    @pl.when(pl.program_id(0) == PAIRS // 2 - 1)
    def _():
        out[0 : 3 * own, 0:half] = first[...]
        out[0 : 3 * own, half:] = part[...]
        scale1 = mod[0:1, D : 2 * D]
        dh1 = sum(dot_nt(out[i * own : (i + 1) * own, :], w[:, i * D : (i + 1) * D]) for i in range(3))
        span = own_o.shape[0]
        n1, rstd = norm(start_rows(even.at[0], even.at[even.shape[0] // 2], span))
        sums = jnp.concatenate([colsum(dh1), colsum(n1 * dh1), jnp.zeros((14, D), F32)], axis=0)
        out[3 * own :, :] = sums.astype(BF16)
        grad = dx1[...] + norm_back(n1, rstd, (1.0 + scale1) * dh1)
        own_o[...] = grad[:span]
        back_o[0] = grad[span:].astype(BF16)
        back_o[1] = away[...]


def attend_dkv(chain, dq, joined, do, half, rest=()):
    own = dq.shape[0]
    span = own // 2
    shift = half * (PAIRS // 2)
    pair = lambda part, rows: pl.BlockSpec((1, rows, 128), lambda i: (part, 0, i + shift))
    specs = [
        pl.BlockSpec((own + 16, 128), functools.partial(lambda at, i: (at, i + shift), at)) for unused, at in do
    ]
    outs = [sds((3 * own, D // 2), BF16)]
    kernel = attend_dkv_kernel
    scratch = []
    if rest:
        outs = [sds((3 * own + 16, D), BF16), sds((span, D), F32), sds((2, span, D), BF16)]
        kernel = last_kernel
        scratch = [pltpu.VMEM((3 * own, D // 2), BF16)]
    return chain(
        functools.partial(kernel, len(do)), outs,
        [dq, joined, joined, joined, *(array for array, unused in do), *rest],
        room(4, joined.shape[1]) + (3 if rest else 0), "attend_dkv", grid=(PAIRS // 2,),
        in_specs=[pl.BlockSpec((own, 128), lambda i: (0, i + shift))]
        + [pair(0, joined.shape[1]), pair(1, own), pair(2, own)]
        + specs + [whole(v) for v in rest],
        out_specs=[whole(o) for o in outs], scratch=scratch,
    )


def start_rows(fa, fb, span):
    return jnp.concatenate([fa[0:span, :], fb[0:span, :]], axis=0).astype(F32)


def gelu_both(u):
    c = math.sqrt(2.0 / math.pi)
    square = u * u
    t = jnp.tanh(c * u * (1.0 + 0.044715 * square))
    half = 0.5 * (1.0 + t)
    slope = half + 0.5 * u * (1.0 - t * t) * (c * (1.0 + 3 * 0.044715 * square))
    return u * half, slope


STEPS = FF // D


def fetch(pairs, sems):
    copies = [pltpu.make_async_copy(a, b, sems.at[i]) for i, (a, b) in enumerate(pairs)]
    for copy in copies:
        copy.start()
    return copies


def forward_kernel(span, order, *refs):
    count = len(order)
    info, cap_len, *blocks = refs[: 2 + count]
    (o, h1, mod, ca, cb, up_b, down_b, wo_h, wq_h, wkv_h, wc_h, up_h, down_h,
     big_o, out_o, away_o, cap_o, h2_o, o2_o, x1, dx2_o, attn_o, attn2_o, sums_o, kv2, q2, p2,
     wo, wq, wkv, wc, up, down, sems, x2, low, dh3, offset) = refs[2 + count :]
    cap_rows = blocks[0].shape[0] - span

    pairs = [(wo_h, wo), (wkv_h, wkv), (wq_h, wq), (wc_h, wc)]
    for i in range(STEPS):
        piece = pl.ds(i * D, D)
        pairs += [(up_h.at[:, piece], up.at[i]), (down_h.at[piece, :], down.at[i])]
    copies = fetch(pairs, sems)
    big_o[2 * STEPS + 2] = o[...]
    big_o[2 * STEPS + 3] = h1[...]

    gate1, shift2, scale2, gate2, shift3, scale3, gate3 = (
        mod[0:1, i * D : (i + 1) * D] for i in range(2, 9)
    )

    length = cap_len[2 * info[0] + info[2]]
    for i, k in enumerate(order):
        here = slice(i * cap_rows, (i + 1) * cap_rows)
        cap_o[here, :] = blocks[i][span:, :]
        first = jnp.bitwise_xor(info[1], k) * cap_rows
        token = first + lax.broadcasted_iota(jnp.int32, (cap_rows, 128), 0)
        offset[here, :] = jnp.where(token < length, 0.0, NEGATIVE)
    dy = jnp.concatenate([ca[...], cb[...]], axis=0).astype(F32)
    big_o[2 * STEPS + 1] = (gate3 * dy).astype(BF16)

    copies[0].wait()
    attn = dot(o[...], wo[...])
    x1[...] = start_rows(blocks[0], blocks[1], span) + gate1 * attn
    attn_o[...] = attn.astype(BF16)
    n2, unused = norm(x1[...])
    h2 = (n2 * (1.0 + scale2) + shift2).astype(BF16)
    h2_o[...] = h2
    copies[1].wait()
    kv2[...] = dot(cap_o[...], wkv[...]).astype(BF16)
    copies[2].wait()
    q2[...] = (dot(h2, wq[...]) * SCALE).astype(BF16)
    for i in range(PAIRS):
        qm = stack_heads(q2[:, cols(i)])
        scores = dot_nt(kv2[:, cols(i)], qm) + offset[:, 0:1]
        peak = jnp.max(scores, axis=0, keepdims=True)
        weights = jnp.exp(scores - peak)
        probs = (weights * (1.0 / jnp.sum(weights, axis=0, keepdims=True))).astype(BF16)
        p2[i] = probs
        both = dot(kv2[:, D + i * 128 : D + (i + 1) * 128].T, probs)
        o2_o[:, cols(i)] = unstack_t(both).astype(BF16)
    copies[3].wait()
    attn2 = dot(o2_o[...], wc[...])
    x2[...] = x1[...] + gate2 * attn2
    attn2_o[...] = attn2.astype(BF16)

    n3, unused = norm(x2[...])
    big_o[2 * STEPS] = (n3 * (1.0 + scale3) + shift3).astype(BF16)
    for i in range(STEPS):
        copies[4 + 2 * i].wait()
        copies[5 + 2 * i].wait()
        piece = slice(i * D, (i + 1) * D)
        acted, slope = gelu_both(dot(big_o[2 * STEPS], up[i]) + up_b[:, piece].astype(F32))
        acted = acted.astype(BF16)
        big_o[i] = acted
        dupper = (slope * dot_nt(big_o[2 * STEPS + 1], down[i])).astype(BF16)
        big_o[STEPS + i] = dupper
        sums_o[8 + i : 9 + i, :] = colsum(dupper.astype(F32))
        if i:
            low[...] += dot(acted, down[i])
            dh3[...] += dot_nt(dupper, up[i])
        else:
            low[...] = dot(acted, down[i])
            dh3[...] = dot_nt(dupper, up[i])
    lower = low[...] + down_b[...].astype(F32)
    value = x2[...]
    result = (value + gate3 * lower).astype(BF16)
    out_o[...] = result[:span]
    away_o[...] = result[span:]
    dy = jnp.concatenate([ca[...], cb[...]], axis=0).astype(F32)
    n3, rstd = norm(value)
    back = dh3[...]
    sums_o[0:4, :] = jnp.zeros((4, D), F32)
    sums_o[4:5, :] = colsum(back)
    sums_o[5:6, :] = colsum(n3 * back)
    sums_o[6:7, :] = colsum(lower * dy)
    sums_o[7:8, :] = colsum(big_o[2 * STEPS + 1].astype(F32))
    sums_o[12:16, :] = jnp.zeros((4, D), F32)
    dx2_o[...] = dy + norm_back(n3, rstd, (1.0 + scale3) * back)


def backward_kernel(dx2_r, mod, attn2, kv2, q2, p2, x1, attn, o, lse, h2, o2, sums3,
                    wc_h, wq_h, wo_h, fac_o, dx1_o, do_o, sums_o, wc, wq, wo, sems):
    copies = fetch([(wc_h, wc), (wq_h, wq), (wo_h, wo)], sems)
    own = o.shape[0]
    slot = lambda i: slice(i * own, (i + 1) * own)
    gate1, scale2, gate2 = (mod[0:1, i * D : (i + 1) * D] for i in (2, 4, 5))
    sums_o[...] = sums3[...]
    fac_o[slot(0), :] = h2[...]
    fac_o[slot(2), :] = o2[...]
    dx2 = dx2_r[...]
    sums_o[3:4, :] = colsum(attn2[...].astype(F32) * dx2)
    da2 = (gate2 * dx2).astype(BF16)
    fac_o[slot(3), :] = da2
    copies[0].wait()
    do2 = dot_nt(da2, wc[...]).astype(BF16)
    for i in range(PAIRS):
        qm = stack_heads(q2[:, cols(i)])
        dom = stack_heads(do2[:, cols(i)])
        keys, values = kv2[:, cols(i)], kv2[:, D + i * 128 : D + (i + 1) * 128]
        probs = p2[i]
        fac_o[slot(5), cols(i)] = dot(probs, dom).astype(BF16)
        probs = probs.astype(F32)
        grad = dot_nt(values, dom)
        ds = (probs * (grad - colsum(probs * grad))).astype(BF16)
        fac_o[slot(1), cols(i)] = (unstack_t(dot(keys.T, ds)) * SCALE).astype(BF16)
        fac_o[slot(4), cols(i)] = dot(ds, qm).astype(BF16)
    copies[1].wait()
    dh2 = dot_nt(fac_o[slot(1), :], wq[...])
    n2, rstd = norm(x1[...])
    sums_o[1:2, :] = colsum(dh2)
    sums_o[2:3, :] = colsum(n2 * dh2)
    dx1 = dx2 + norm_back(n2, rstd, (1.0 + scale2) * dh2)
    dx1_o[...] = dx1
    sums_o[0:1, :] = colsum(attn[...].astype(F32) * dx1)

    da = (gate1 * dx1).astype(BF16)
    fac_o[slot(6), :] = da
    copies[2].wait()
    do = dot_nt(da, wo[...]).astype(BF16)
    do_o[0:own, :] = do
    both = do.astype(F32) * o[...].astype(F32)
    for i in range(PAIRS):
        t = both[:, cols(i)].T
        delta = [colsum(t[:HEAD]), colsum(t[HEAD:])]
        delta = [d[:, 128 * j : 128 * (j + 1)] for d in delta for j in range(own // 128)]
        sums = [lse[i][:, 128 * j : 128 * (j + 1)] for j in range(2 * own // 128)]
        held = [two_terms(jnp.concatenate(rows, axis=0)) for rows in (sums, delta)]
        do_o[own:, cols(i)] = jnp.concatenate(held, axis=0)
    fac_o[7 * own : 7 * own + 16, :] = sums_o[...].astype(BF16)
    at = do_place(own) * (own + 16)
    fac_o[7 * own + 16 : at, :] = jnp.zeros((at - 7 * own - 16, D), BF16)
    fac_o[at:, :] = do_o[...]


def forward(chain, info, cap_len, blocks, order, span, o, h1, mod, ca, cb, up_b, down_b, *weights):
    own = 2 * span
    cap_total = len(blocks) * (blocks[0][0].shape[1] - span)
    thin, wide = sds((own, D), BF16), sds((own, D), F32)
    half = sds((span, D), BF16)
    outs = [
        sds((2 * STEPS + 4, own, D), BF16), half, half, sds((cap_total, D), BF16), thin, thin, wide, wide,
        thin, thin, sds((16, D), F32), sds((cap_total, 2 * D), BF16), thin,
        sds((PAIRS, cap_total, 2 * own), BF16),
    ]
    here = [blocks[0][0], blocks[2][0], o, h1, mod, ca, cb, up_b, down_b]
    square = pltpu.VMEM((D, D), BF16)

    def kernel(info, cap_len, even, odd, *refs):
        forward_kernel(span, order, info, cap_len, *block_refs(order, even, odd), *refs)

    return chain(
        kernel, outs, [info, cap_len, *here, *weights], FWD, "forward",
        in_specs=[smem()] * 2 + [vmem()] * len(here) + [pl.BlockSpec(memory_space=pl.ANY)] * len(weights),
        scratch=[
            square, square, pltpu.VMEM((D, 2 * D), BF16), square,
            pltpu.VMEM((STEPS, D, D), BF16), pltpu.VMEM((STEPS, D, D), BF16),
            pltpu.SemaphoreType.DMA((4 + 2 * STEPS,)),
        ]
        + [pltpu.VMEM((own, D), F32)] * 3
        + [pltpu.VMEM((cap_total, 128), F32)],
    )


def do_place(own):
    return -(-(7 * own + 16) // (own + 16))


def backward(chain, here, weights):
    own = here[0].shape[0]
    outs = [
        sds(((do_place(own) + 1) * (own + 16), D), BF16), sds((own, D), F32),
        sds((own + 16, D), BF16),
        sds((16, D), F32),
    ]
    square = pltpu.VMEM((D, D), BF16)
    return chain(
        backward_kernel, outs, [*here, *weights], BWD, "backward",
        in_specs=[vmem()] * len(here) + [pl.BlockSpec(memory_space=pl.ANY)] * len(weights),
        scratch=[square, square, square, pltpu.SemaphoreType.DMA((3,))],
    )


def pick_rows(info, x):
    source = lax.broadcasted_iota(jnp.int32, (D, D // 2), 0)
    column = lax.broadcasted_iota(jnp.int32, (D, D // 2), 1)
    block = sum((column >= 96 * i).astype(jnp.int32) for i in (1, 2, 3))
    wanted = 96 * jnp.bitwise_xor(info[1], 2 * block) + column - 96 * block
    choose = (source == wanted).astype(F32).astype(BF16)
    return dot(x, choose).astype(BF16)


def emit(first, info, tiles, blocks, send_o, keep_o):
    place = {True: 0, False: 0}
    for r in range(4):
        sent = bool(r & first)
        (send_o if sent else keep_o)[place[sent]] = tiles[jnp.bitwise_xor(info[0], r), blocks]
        place[sent] += 1


def down_grad_kernel(info, fac, fac_p, send_o, keep_o, tiles):
    for e in range(4):
        owner = jnp.bitwise_xor(info[1], 2 * e)
        half = pl.multiple_of(lax.rem(owner, 2) * 384, 128)
        where = (lax.div(owner, 2), slice(None), pl.ds(half, 384))
        grad = dot_tn(fac[where], fac[2 * STEPS + 1]) + dot_tn(fac_p[where], fac_p[9])
        for q in range(4):
            tiles[q, e] = grad[96 * q : 96 * (q + 1)].astype(BF16)
    emit(1, info, tiles, slice(0, 4), send_o, keep_o)


def up_grad_kernel(info, fac, fac_p, send_o, keep_o, tiles):
    x, xp = pick_rows(info, fac[8]), pick_rows(info, fac_p[8])
    for q in range(4):
        grad = dot_tn(x, fac[4 + q]) + dot_tn(xp, fac_p[4 + q])
        for e in range(4):
            tiles[q, e] = grad[96 * e : 96 * (e + 1)].astype(BF16)
    emit(2, info, tiles, slice(0, 4), send_o, keep_o)


def put(tiles, q, grad):
    for e in range(4):
        tiles[q, e] = grad[96 * e : 96 * (e + 1)].astype(BF16)


def emit_both(info, tiles, sx, kx, sy, ky):
    emit(1, info, tiles, slice(0, 2), sx, kx)
    emit(2, info, tiles, slice(2, 4), sy, ky)


def cross_grad_kernel(own, info, cap, fac, fac_p, wkv, sx, kx, sy, ky, dcap_o, tiles):
    def slot(ref, i):
        return ref[i * own : (i + 1) * own, :]

    def pair(x, y):
        left, left_p = pick_rows(info, slot(fac, x)), pick_rows(info, slot(fac_p, x))
        return dot_tn(left, slot(fac, y)) + dot_tn(left_p, slot(fac_p, y))

    put(tiles, 0, pair(0, 1))
    x = pick_rows(info, cap[...])
    rows = cap.shape[0] // 4
    xp = jnp.concatenate([x[rows * i : rows * (i + 1)] for i in (1, 0, 3, 2)], axis=0)
    for q in (1, 2):
        put(tiles, q, dot_tn(x, slot(fac, q + 3)) + dot_tn(xp, slot(fac_p, q + 3)))
    put(tiles, 3, pair(2, 3))
    emit_both(info, tiles, sx, kx, sy, ky)

    rows = cap.shape[0] // 8

    def even(x):
        places = [rows * order_place(k) for k in range(8)]
        parts = [
            total(slot(fac, x)[places[k] : places[k] + rows], slot(fac_p, x)[places[k + 1] : places[k + 1] + rows])
            for k in (0, 2, 4, 6)
        ]
        return jnp.concatenate(parts, axis=0)

    dcap_o[...] = (dot_nt(even(4), wkv[:, 0:D]) + dot_nt(even(5), wkv[:, D : 2 * D])).astype(BF16)


def attn_grad_kernel(info, da, o, h1, da_p, o_p, h1_p, dqkv, dqkv_p, sx, kx, sy, ky, tiles):
    own = da.shape[0]
    x, xp = pick_rows(info, h1[0]), pick_rows(info, h1_p[0])
    for i in range(3):
        slot = slice(i * own, (i + 1) * own)
        put(tiles, i, dot_tn(x, dqkv[slot, :]) + dot_tn(xp, dqkv_p[slot, :]))
    x, xp = pick_rows(info, o[0]), pick_rows(info, o_p[0])
    put(tiles, 3, dot_tn(x, da[...]) + dot_tn(xp, da_p[...]))
    emit_both(info, tiles, sx, kx, sy, ky)


def grad_call(chain, kernel, info, args, name, shape, outs, in_specs=None):
    return chain(
        kernel, [sds(o, BF16) for o in outs], [info, *args], 5, name, grid=(1,) if in_specs else None,
        in_specs=[smem()] + (in_specs or [vmem()] * len(args)),
        scratch=[pltpu.VMEM(shape, BF16)],
    )


def total(*refs):
    return sum(r.astype(F32) for r in refs).astype(BF16)


def add_first_kernel(keep, recv, keep_o, send_o):
    keep_o[...] = total(keep[0], recv[0])
    send_o[...] = total(keep[1], recv[1])


def add_both_kernel(kx, rx, ky, ry, kx_o, sx_o, ky_o, sy_o):
    add_first_kernel(kx, rx, kx_o, sx_o)
    add_first_kernel(ky, ry, ky_o, sy_o)


def sum_rows(early, early_p, late, late_p):
    first = late[0:2, :].astype(F32) + late_p[0:2, :].astype(F32)
    both = early[0:12, :].astype(F32) + early_p[0:12, :].astype(F32)
    return jnp.concatenate([first, both, jnp.zeros((2, D), F32)], axis=0).astype(BF16)


def mlp_second_kernel(ka, ra, kb, rb, fac, fac_p, late, late_p, keep_o, send_o):
    for g, (keep, recv) in enumerate(((ka, ra), (kb, rb))):
        for e in range(4):
            (send_o if e % 2 else keep_o)[e // 2, 96 * g : 96 * (g + 1), :] = total(keep[e], recv[e])
    rows = sum_rows(fac, fac_p, late, late_p)
    for ref in (keep_o, send_o):
        for i in range(2):
            ref[i, 192:208, :] = rows


def mlp_third_kernel(keep, recv, keep_o, send_o):
    keep_o[...] = total(keep[0], recv[0])
    send_o[0:192, :] = total(keep[1, 0:192, :], recv[1, 0:192, :])
    send_o[192:208, :] = total(keep[0, 192:208, :], recv[0, 192:208, :])


def mlp_fourth_kernel(keep, recv, out):
    out[0:192, :] = total(keep[0:192, :], recv[0:192, :])
    out[192:208, :] = keep[192:208, :]
    out[208:224, :] = recv[192:208, :]


def order_place(k):
    return 2 * (k % 4) + k // 4


def second_kernel(kx, rx, ky, ry, *refs):
    caption, (keep_o, send_o) = refs[:-2], refs[-2:]
    for e in range(4):
        out = send_o if e % 2 else keep_o
        keep, recv = ((kx, rx), (ky, ry))[e // 2]
        out[e // 2, 0:96, :] = total(keep[e % 2], recv[e % 2])
        if caption:
            rows = caption[0].shape[0] // 4
            out[e // 2, 96:, :] = caption[0][rows * e : rows * (e + 1), :]


def third_kernel(keep, recv, keep_o, send_o):
    keep_o[...] = total(keep[0], recv[0])
    send_o[...] = total(keep[1], recv[1])


def fourth_kernel(keep, recv, c_keep, c_recv, out, same_o, away_o):
    out[0:96, :] = total(keep[...], recv[...])
    out[96:, :] = total(c_keep[0:96, :], c_recv[0:96, :])
    same_o[...] = c_keep[96:, :].astype(F32)
    away_o[...] = c_recv[96:, :].astype(F32)


def swap(x, axis, size, k):
    return lax.ppermute(x, axis, [(i, i ^ k) for i in range(size)])


def over_x(x):
    return swap(x, "band", 4, 1)


def over_y(x):
    return swap(x, "band", 4, 2)


def to_band(x):
    return [x] + [swap(x, "band", 4, t) for t in (1, 2, 3)]


def mlp_finish_kernel(info, t0, t1, t2, t3, down_o, up_o):
    for r, tile in enumerate((t0, t1, t2, t3)):
        q = jnp.bitwise_xor(info[0], r)
        down_o[pl.ds(pl.multiple_of(96 * q, 96), 96), :] = tile[0:96, :].astype(F32)
        up_o[:, pl.ds(pl.multiple_of(D * q, D), D)] = tile[96:192, :].astype(F32)


def last_finish_kernel(info, t0, t1, t2, t3, in_o, out_o, cq_o, ckv_o, co_o, tiles):
    for r, tile in enumerate((t0, t1, t2, t3)):
        tiles[jnp.bitwise_xor(info[0], r)] = tile[...]
    for i in range(3):
        in_o[:, i * D : (i + 1) * D] = tiles[i, 0:96, :].astype(F32)
    out_o[...] = tiles[3, 0:96, :].astype(F32)
    cq_o[...] = tiles[0, 96:, :].astype(F32)
    ckv_o[:, 0:D] = tiles[1, 96:, :].astype(F32)
    ckv_o[:, D:] = tiles[2, 96:, :].astype(F32)
    co_o[...] = tiles[3, 96:, :].astype(F32)


def finish(chain, kernel, info, tiles, widths, name, scratch=(), held=()):
    outs = [sds(w, F32) for w in widths] + [sds(h.shape, h.dtype) for h in held]
    tiles = [*tiles, *held]
    return chain(
        kernel, outs, [info, *tiles], 5, name, grid=(1,), in_specs=[smem()] + [whole(t) for t in tiles],
        out_specs=[whole(o) for o in outs], scratch=scratch,
    )


def plain_reduce(x, y, owners):
    grad = lax.psum_scatter(dot_tn(x, y).astype(BF16), "seq", scatter_dimension=0, tiled=True)
    return lax.psum(grad, "band").astype(F32)


def on_device(bands, seqs, frames, caption, timesteps, cap_len, attn_in, attn_out, cross_query,
              cross_keyval, cross_out, mlp_up, up_bias, mlp_down, down_bias, ada_weight, ada_bias,
              time_first, first_bias, time_second, second_bias, cotangent):
    span = frames.shape[1]
    own = 2 * span
    cap_rows = caption.shape[1]
    items = timesteps.shape[0]
    halves = seqs // 2
    band = lax.axis_index("band")
    seq = lax.axis_index("seq")
    half = (seq >= halves).astype(jnp.int32)
    item = 2 * band + half
    info = jnp.stack([band, seq, half]).astype(jnp.int32)

    chain = Chain()

    order = [k for i in range(halves) for k in (i, i + halves)]
    same, other = pick(chain, info, frames, caption)
    even = [same] + [swap(same if k < halves else other, "seq", seqs, k) for k in range(2, seqs, 2)]

    steps = jnp.take(timesteps, jnp.bitwise_xor(jnp.arange(items), item))
    width = time_first.shape[0] // 2
    freq = jnp.exp(-math.log(10000.0) * jnp.arange(width, dtype=F32) / width)
    angle = steps.astype(F32)[:, None] * freq[None, :]
    embed = jnp.concatenate([jnp.cos(angle), jnp.sin(angle)], axis=1)
    row = lambda v: v.reshape(1, -1)
    pre_cond, mod = modulation(
        chain, embed, time_first, row(first_bias), time_second, row(second_bias), ada_weight, row(ada_bias)
    )
    cot_own, cot_other = pick(chain, info, cotangent)
    cot_other = swap(cot_other, "seq", seqs, halves)

    even = stack(chain, even, "blocks")
    odd = swap(even, "seq", seqs, 1)
    blocks = [(odd if k % 2 else even, k // 2) for k in order]
    joined, h1, mixed, lse = qkv_attend(chain, blocks, order, span, mod, attn_in)

    cap_total = seqs * cap_rows
    (big, out, out_back, cap_all, h2, o2, x1, dx2, attn, attn2, sums3, kv2, q2, p2) = forward(
        chain, info, cap_len, blocks, order, span, mixed, h1, mod, cot_own, cot_other, row(up_bias),
        row(down_bias), attn_out, cross_query, cross_keyval, cross_out, mlp_up, mlp_down,
    )
    fast = bands == 4 and seqs == 8
    if fast:
        big_p = swap(big, "seq", seqs, 1)
    fac, dx1, do, early = backward(
        chain, [dx2, mod, attn2, kv2, q2, p2, x1, attn, mixed, lse, h2, o2, sums3],
        [cross_out, cross_query, attn_out],
    )
    if fast:
        fac_p = swap(fac, "seq", seqs, 1)
    got = {k: (swap(do, "seq", seqs, k), 0) for k in range(2 if fast else 1, halves)}
    got[0] = (do, 0)
    if fast:
        got[1] = (fac_p, do_place(own))
        whole_tiles, pieces, halved = (4, 4, 96, D), [(2, 4, 96, D)] * 2, [(2, 2, 96, D)] * 4
        args = [big, big_p]
        sa, ka = grad_call(chain, down_grad_kernel, info, args, "down_grad", whole_tiles, pieces)
        ra = over_x(sa)
        sb, kb = grad_call(chain, up_grad_kernel, info, args, "up_grad", whole_tiles, pieces)
        rb = over_y(sb)
        cx, ckx, cy, cky, dcap = grad_call(
            chain, functools.partial(cross_grad_kernel, own), info, [cap_all, fac, fac_p, cross_keyval],
            "cross_grad", whole_tiles, halved + [(cap_total // 2, D)],
        )
        crx, cry = over_x(cx), over_y(cy)
    dq = attend_dq(chain, joined, do)
    do_blocks = [got[k] for k in range(halves)]
    dkv_first = attend_dkv(chain, dq, joined, do_blocks, 0)[0]
    dqkv, grad_own, back = attend_dkv(
        chain, dq, joined, do_blocks, 1, [dkv_first, even, attn_in, mod, dx1, out_back]
    )
    back = swap(back, "seq", seqs, halves)
    if fast:
        dqkv_p = swap(dqkv, "seq", seqs, 1)
        half, quarter, tile = sds((4, 96, D), BF16), sds((2, 96, D), BF16), sds((96, D), BF16)
        ka, sa, kb, sb = chain(add_both_kernel, [half] * 4, [ka, ra, kb, rb], 2, "mlp_add1")
        ra, rb = over_y(sa), over_x(sb)
        slots = [pl.BlockSpec((own, D), lambda *i: (6, 0))] + [
            pl.BlockSpec((1, own, D), functools.partial(lambda at, *i: (at, 0, 0), at))
            for at in (2 * STEPS + 2, 2 * STEPS + 3)
        ]
        tx, tkx, ty, tky = grad_call(
            chain, attn_grad_kernel, info, [fac, big, big, fac_p, big_p, big_p, dqkv, dqkv_p], "attn_grad",
            whole_tiles, halved, in_specs=slots * 2 + [whole(dqkv)] * 2,
        )
        trx, try_ = over_x(tx), over_y(ty)
        grad_frames, out = place(
            chain, info, [(grad_own, (back, 0)), (out, (back, 1))], [F32, BF16], "place_frames"
        )
        sum_at, late_at = 7 * own // 16, 3 * own // 16
        sum_spec = pl.BlockSpec((16, D), lambda *i: (sum_at, 0))
        late_spec = pl.BlockSpec((16, D), lambda *i: (late_at, 0))
        ckx, cx, cky, cy = chain(add_both_kernel, [quarter] * 4, [ckx, crx, cky, cry], 4, "cross_add1")
        crx, cry = over_y(cx), over_x(cy)
        keep, send = chain(
            mlp_second_kernel, [sds((2, 208, D), BF16)] * 2, [ka, ra, kb, rb, fac, fac_p, dqkv, dqkv_p], 4,
            "mlp_add2", grid=(1,), in_specs=[vmem()] * 4 + [sum_spec] * 2 + [late_spec] * 2,
        )
        recv = swap(send, "seq", seqs, 2)
        tkx, tx, tky, ty = chain(add_both_kernel, [quarter] * 4, [tkx, trx, tky, try_], 4, "attn_add1")
        trx, try_ = over_y(tx), over_x(ty)
        keep, send = chain(mlp_third_kernel, [sds((208, D), BF16)] * 2, [keep, recv], 4, "mlp_z1")
        recv = swap(send, "seq", seqs, 4)
        rows = 96 + cap_rows
        c_keep, c_send = chain(
            second_kernel, [sds((2, rows, D), BF16)] * 2, [ckx, crx, cky, cry, dcap], 4, "cross_add2",
        )
        c_recv = swap(c_send, "seq", seqs, 2)
        t_keep, t_send = chain(second_kernel, [quarter] * 2, [tkx, trx, tky, try_], 4, "attn_add2")
        t_recv = swap(t_send, "seq", seqs, 2)
        a_all = to_band(chain(mlp_fourth_kernel, [sds((224, D), BF16)], [keep, recv], 4, "mlp_z2")[0])
        c_keep, c_send = chain(third_kernel, [sds((rows, D), BF16)] * 2, [c_keep, c_recv], 4, "cross_z1")
        c_recv = swap(c_send, "seq", seqs, 4)
        t_keep, t_send = chain(third_kernel, [tile] * 2, [t_keep, t_recv], 4, "attn_z1")
        t_recv = swap(t_send, "seq", seqs, 4)
        t_done, cap_same, cap_away = chain(
            fourth_kernel, [sds((192, D), BF16)] + [sds((cap_rows, D), F32)] * 2,
            [t_keep, t_recv, c_keep, c_recv], 4, "other_z2",
        )
        t_all = to_band(t_done)
        g_down, g_up = finish(chain, mlp_finish_kernel, info, a_all, [(384, D), (96, FF)], "mlp_finish")
        grad_caption = place(chain, info, [(cap_same, cap_away)], [F32], "place_caption")[0]
        sums = a_all
    else:
        grad_frames, out = place(
            chain, info, [(grad_own, (back, 0)), (out, (back, 1))], [F32, BF16], "place_frames"
        )
        dkv2 = jnp.concatenate([fac[4 * own : 4 * own + cap_total], fac[5 * own : 5 * own + cap_total]], axis=1)
        dcap = dot_nt(dkv2, cross_keyval).astype(BF16).reshape(seqs, cap_rows, D)
        place_of = jnp.asarray([order.index(k) for k in range(seqs)])
        dcap = dcap[place_of[jnp.bitwise_xor(seq, jnp.arange(seqs))]].reshape(cap_total, D)
        dcap = jnp.where(half == 0, jnp.stack([dcap, 0 * dcap]), jnp.stack([0 * dcap, dcap]))
        grad_caption = lax.psum_scatter(dcap, "seq", scatter_dimension=1, tiled=True).astype(F32)
        rows = jnp.concatenate([dqkv[3 * own : 3 * own + 2].astype(F32), early[0:12], jnp.zeros((2, D), F32)])
        for k in range(1, halves):
            if k & (k - 1) == 0:
                rows = rows + swap(rows, "seq", seqs, k)
        rows = jnp.concatenate([rows, swap(rows, "seq", seqs, halves)]).astype(BF16)
        sums = [rows] + [swap(rows, "band", bands, t) for t in range(1, bands)]

    g_ada, gb_ada, g_t2, gb_t2, g_t1, gb_t1, gb_down, gb_up = mod_back(
        chain, info, sums, ada_weight, pre_cond, embed, time_second, seqs
    )

    if fast:
        g_in, g_out, g_cq, g_ckv, g_co = finish(
            chain, last_finish_kernel, info, t_all, [(96, 3 * D), (96, D), (96, D), (96, 2 * D), (96, D)],
            "last_finish", [pltpu.VMEM((4, 192, D), BF16)],
        )
    else:
        slot = lambda i: fac[i * own : (i + 1) * own]
        acted = jnp.concatenate([big[i] for i in range(FF // D)], axis=1)
        dupper = jnp.concatenate([big[FF // D + i] for i in range(FF // D)], axis=1)
        g_down = plain_reduce(acted, big[2 * STEPS + 1], seqs)
        g_up = plain_reduce(big[2 * STEPS], dupper, seqs)
        g_cq = plain_reduce(slot(0), slot(1), seqs)
        g_ckv = plain_reduce(cap_all, jnp.concatenate([slot(4), slot(5)], axis=1), seqs)
        g_co = plain_reduce(slot(2), slot(3), seqs)
        g_out = plain_reduce(mixed, slot(6), seqs)
        g_in = plain_reduce(h1, jnp.concatenate([dqkv[i * own : (i + 1) * own] for i in range(3)], axis=1), seqs)

    flat = lambda v: v.reshape(-1)
    return (
        out, grad_frames, grad_caption, g_in, g_out, g_cq, g_ckv, g_co, g_up, flat(gb_up), g_down,
        flat(gb_down), g_ada, flat(gb_ada), g_t1, flat(gb_t1), g_t2, flat(gb_t2),
    )


def solution(mesh):
    split = P("band", "seq", None)
    rows, flat = P("seq", None), P("seq")
    return jax.shard_map(
        functools.partial(on_device, mesh.shape["band"], mesh.shape["seq"]),
        mesh=mesh,
        in_specs=(split, split) + (P(),) * 17 + (split,),
        out_specs=(split, split, split, rows, rows, rows, rows, rows, rows, flat, rows, flat, rows, flat,
                   rows, flat, rows, flat),
        check_vma=False,
    )
```

```python
import functools
import math

import jax
import jax.numpy as jnp
from jax import lax
from jax.experimental import pallas as pl
from jax.experimental.pallas import tpu as pltpu
from jax.sharding import PartitionSpec as P

D = 768
HEAD = 64
PAIRS = 6
FF = 3072
EPSILON = 1e-06
NEGATIVE = -1e30
SCALE = 0.125
F32 = jnp.float32
BF16 = jnp.bfloat16
MIB = 1 << 20
MODMIB = 4
COST = 1000000
FWD = 9
BWD = 6


def dot(a, b):
    return jnp.dot(a, b, preferred_element_type=F32)


def dot_nt(a, b):
    return lax.dot_general(a, b, (((1,), (1,)), ((), ())), preferred_element_type=F32)


def dot_tn(a, b):
    return lax.dot_general(a, b, (((0,), (0,)), ((), ())), preferred_element_type=F32)


def split_dot(x, w, contract=0):
    high = x.astype(BF16).astype(F32)
    both = jnp.concatenate([high, x - high], axis=0).astype(BF16)
    out = lax.dot_general(
        both, w, (((1,), (contract,)), ((), ())), preferred_element_type=F32
    )
    return out[: x.shape[0]] + out[x.shape[0] :]


def silu(v):
    return v * (1.0 / (1.0 + jnp.exp(-v)))


def silu_grad(v):
    s = 1.0 / (1.0 + jnp.exp(-v))
    return s * (1.0 + v * (1.0 - s))


def norm(v):
    mean = jnp.mean(v, axis=-1, keepdims=True)
    centred = v - mean
    spread = jnp.mean(centred * centred, axis=-1, keepdims=True)
    rstd = lax.rsqrt(spread + EPSILON)
    return centred * rstd, rstd


def norm_back(n, rstd, w):
    return (
        w - jnp.mean(w, axis=-1, keepdims=True) - n * jnp.mean(w * n, axis=-1, keepdims=True)
    ) * rstd


def colsum(v):
    return jnp.sum(v, axis=0, keepdims=True)


def cols(i):
    return slice(i * 128, (i + 1) * 128)


def head_masks():
    lane = lax.broadcasted_iota(jnp.int32, (1, 128), 1)
    first = (lane < HEAD).astype(F32)
    return first.astype(BF16), (1.0 - first).astype(BF16)


def stack_heads(block):
    first, second = head_masks()
    return jnp.concatenate([block * first, block * second], axis=0)


def unstack_t(both):
    rows = both.shape[1] // 2
    pair = jnp.concatenate([both[:HEAD, :rows], both[HEAD:, rows:]], axis=0)
    return pair.T


def sds(shape, dtype):
    return jax.ShapeDtypeStruct(shape, dtype)


def vmem():
    return pl.BlockSpec(memory_space=pltpu.VMEM)


def smem():
    return pl.BlockSpec(memory_space=pltpu.SMEM)


def whole(a):
    return pl.BlockSpec(a.shape, lambda *i: (0,) * len(a.shape))


class Chain:
    def __init__(self):
        self.token = None

    def __call__(self, kernel, outs, args, mib, name, grid=None, in_specs=None, out_specs=None, scratch=()):
        outs = list(outs)
        in_specs = list(in_specs or [vmem()] * len(args))
        out_specs = list(out_specs or [vmem()] * len(outs))
        count = len(args)
        body = kernel
        if self.token is not None:
            args = [*args, self.token]
            in_specs.append(pl.BlockSpec(memory_space=pl.ANY))
            body = lambda *refs: kernel(*refs[:count], *refs[count + 1 :])
        results = pl.pallas_call(
            body,
            **({} if grid is None else {"grid": grid}),
            out_shape=outs,
            in_specs=in_specs,
            out_specs=out_specs,
            scratch_shapes=list(scratch),
            compiler_params=pltpu.CompilerParams(vmem_limit_bytes=mib * MIB),
            cost_estimate=pl.CostEstimate(flops=1000, bytes_accessed=COST, transcendentals=0),
            name=name,
        )(*args)
        self.token = min(results, key=lambda r: r.size * r.dtype.itemsize)
        return results

    def after(self, x):
        self.token = x


def room(mib, frames):
    return min(56, mib * max(1, frames // 1024))


def pick_kernel(info, *refs):
    half = info[2]
    parts, (mine_o, theirs_o, sems) = refs[:-3], refs[-3:]
    copies = []
    at = 0
    for x in parts:
        rows = pl.ds(at, x.shape[1])
        for source, out in ((half, mine_o), (1 - half, theirs_o)):
            copies.append(pltpu.make_async_copy(x.at[source], out.at[rows], sems.at[len(copies)]))
        at += x.shape[1]
    for copy in copies:
        copy.start()
    for copy in copies:
        copy.wait()


def pick(chain, info, *parts):
    out = sds((sum(x.shape[1] for x in parts), D), BF16)
    anywhere = pl.BlockSpec(memory_space=pl.ANY)
    return chain(
        pick_kernel, [out, out], [info, *parts], 4, "pick", in_specs=[smem()] + [anywhere] * len(parts),
        out_specs=[anywhere] * 2, scratch=[pltpu.SemaphoreType.DMA((2 * len(parts),))],
    )


def stack_kernel(*refs):
    for i, ref in enumerate(refs[:-1]):
        refs[-1][i] = ref[...]


def stack(chain, arrays, name):
    out = sds((len(arrays),) + arrays[0].shape, arrays[0].dtype)
    return chain(stack_kernel, [out], arrays, 4, name)[0]


def place_kernel(info, *refs):
    count = len(refs) // 3
    for i in range(count):
        kept, received, out = refs[2 * i], refs[2 * i + 1], refs[2 * count + i]
        out[info[2]] = kept[...].astype(out.dtype)
        out[1 - info[2]] = received[...].reshape(kept.shape).astype(out.dtype)


def place(chain, info, pairs, dtypes, name):
    args, specs = [info], [smem()]
    for kept, received in pairs:
        args.append(kept)
        specs.append(whole(kept))
        if isinstance(received, tuple):
            args.append(received[0])
            specs.append(pl.BlockSpec((1,) + kept.shape, functools.partial(lambda at, i: (at, 0, 0), received[1])))
        else:
            args.append(received)
            specs.append(whole(received))
    outs = [sds((2,) + kept.shape, dtype) for (kept, unused), dtype in zip(pairs, dtypes)]
    return chain(
        place_kernel, outs, args, 4, name, grid=(1,), in_specs=specs, out_specs=[whole(o) for o in outs]
    )


def mod_kernel(embed, t1, b1, t2, b2, w, b, both_o, mod_o, act):
    @pl.when(pl.program_id(0) == 0)
    def _():
        pre = split_dot(embed[...], t1[...]) + b1[...].astype(F32)
        cond = split_dot(silu(pre), t2[...]) + b2[...].astype(F32)
        both_o[0] = pre
        both_o[1] = cond
        act[...] = silu(cond)

    mod_o[...] = split_dot(act[...], w[...]) + b[...].astype(F32)


def modulation(chain, embed, t1, b1, t2, b2, w, b):
    items = embed.shape[0]
    outs = [sds((2, items, D), F32), sds((items, 9 * D), F32)]
    return chain(
        mod_kernel, outs, [embed, t1, b1, t2, b2, w, b], MODMIB, "modulation", grid=(9,),
        in_specs=[whole(v) for v in (embed, t1, b1, t2, b2)]
        + [pl.BlockSpec((D, D), lambda i: (0, i)), pl.BlockSpec((1, D), lambda i: (0, i))],
        out_specs=[whole(outs[0]), pl.BlockSpec((items, D), lambda i: (0, i))],
        scratch=[pltpu.VMEM((items, D), F32)],
    )


def outer_sum(left_t, right):
    lh = left_t.astype(BF16)
    ll = (left_t - lh.astype(F32)).astype(BF16)
    rh = right.astype(BF16)
    rl = (right - rh.astype(F32)).astype(BF16)
    return dot(lh, rh) + dot(ll, rh) + dot(lh, rl)


def own_rows_t(info, size, v):
    row = lax.broadcasted_iota(jnp.int32, (size, v.shape[1]), 0)
    column = lax.broadcasted_iota(jnp.int32, (size, v.shape[1]), 1)
    choose = (column == row + size * info[1]).astype(F32).astype(BF16)
    high = v.astype(BF16)
    rest = (v - high.astype(F32)).astype(BF16)
    return dot_nt(choose, high) + dot_nt(choose, rest)


def mod_back_kernel(bands, seqs, info, *refs):
    sums = refs[:bands]
    (both, embed, t2, w_h, g_ada_h, gb_ada, g_t2, gb_t2, g_t1, gb_t1, gb_down, gb_up,
     w, g_ada, sems, acc, dmod, all_bias) = refs[bands:]
    pieces = [pl.ds(i * D, D) for i in range(9)]
    copies = fetch([(w_h.at[:, piece], w.at[i]) for i, piece in enumerate(pieces)], sems)
    own_act = own_rows_t(info, D // seqs, silu(both[1]))
    bias = jnp.zeros((5, D), F32)
    for t in range(bands):
        held = sums[t][sums[t].shape[0] - 32 :, :].astype(F32)
        for u in range(2):
            r = 2 * t + u
            for p in range(9):
                dmod[p, r : r + 1, :] = held[16 * u + p : 16 * u + p + 1]
            bias += held[16 * u + 9 : 16 * u + 14]
    stores = []
    for i, piece in enumerate(pieces):
        part = dmod[i]
        g_ada[i] = outer_sum(own_act, part)
        stores.append(pltpu.make_async_copy(g_ada.at[i], g_ada_h.at[:, piece], sems.at[9 + i]))
        stores[-1].start()
        all_bias[:, i * D : (i + 1) * D] = jnp.broadcast_to(colsum(part), (8, D))
        copies[i].wait()
        term = split_dot(part, w[i], contract=1)
        if i:
            acc[...] += term
        else:
            acc[...] = term

    def own_part(row):
        size = row.shape[1] // seqs
        rows = jnp.broadcast_to(row, (8, row.shape[1]))
        return pltpu.roll(rows, row.shape[1] - info[1] * size, 1)[0:1, 0:size]

    size = 9 * D // seqs
    gb_ada[...] = pltpu.roll(all_bias[...], 9 * D - info[1] * size, 1)[0:1, 0:size]
    gb_down[...] = own_part(bias[0:1])
    gb_up[...] = own_part(jnp.concatenate([bias[1 + i : 2 + i] for i in range(4)], axis=1))
    dcond = acc[...] * silu_grad(both[1])
    g_t2[...] = outer_sum(own_rows_t(info, D // seqs, silu(both[0])), dcond)
    gb_t2[...] = own_part(colsum(dcond))
    dpre = split_dot(dcond, t2[...], contract=1) * silu_grad(both[0])
    g_t1[...] = outer_sum(own_rows_t(info, g_t1.shape[0], embed[...]), dpre)
    gb_t1[...] = own_part(colsum(dpre))
    for store in stores:
        store.wait()


def mod_back(chain, info, sums, w, both, embed, t2, seqs):
    bands = len(sums)
    items = 2 * bands
    m = D // seqs
    line = lambda n: sds((1, n // seqs), F32)
    outs = [
        sds((m, 9 * D), F32), line(9 * D), sds((m, D), F32), line(D), sds((embed.shape[1] // seqs, D), F32),
        line(D), line(D), line(FF),
    ]
    anywhere = pl.BlockSpec(memory_space=pl.ANY)
    here = [*sums, both, embed, t2]
    return chain(
        functools.partial(mod_back_kernel, bands, seqs), outs, [info, *here, w], 15, "modulation_back",
        grid=(1,), in_specs=[smem()] + [whole(v) for v in here] + [anywhere],
        out_specs=[anywhere] + [whole(o) for o in outs[1:]],
        scratch=[
            pltpu.VMEM((9, D, D), BF16), pltpu.VMEM((9, m, D), F32), pltpu.SemaphoreType.DMA((18,)),
            pltpu.VMEM((items, D), F32), pltpu.VMEM((9, items, D), F32), pltpu.VMEM((8, 9 * D), F32),
        ],
    )


def block_refs(order, even, odd):
    return [(odd if k % 2 else even).at[k // 2] for k in order]


def qkv_kernel(order, span, even, odd, mod, w, out, h1_o, h1):
    frames = block_refs(order, even, odd)
    blocks = len(order)
    own = 2 * span

    @pl.when(pl.program_id(0) == 0)
    def _():
        shift, scale = mod[0:1, 0:D], mod[0:1, D : 2 * D]
        for i in range(blocks):
            n, unused = norm(frames[i][0:span, :].astype(F32))
            h1[pl.ds(i * span, span), :] = (n * (1.0 + scale) + shift).astype(BF16)
        h1_o[...] = h1[0:own, :]

    factor = jnp.where(pl.program_id(0) == 0, SCALE, 1.0)

    @pl.loop(0, blocks * span // own)
    def _(i):
        rows = pl.ds(pl.multiple_of(i * own, own), own)
        out[0, rows, :] = (dot(h1[rows, :], w[...]) * factor).astype(BF16)


def qkv(chain, blocks, order, span, mod, w):
    total = len(order) * span
    outs = [sds((3, total, D), BF16), sds((2 * span, D), BF16)]
    args = [blocks[0][0], blocks[2][0], mod]
    return chain(
        functools.partial(qkv_kernel, order, span), outs, [*args, w], room(16, total), "qkv", grid=(3,),
        in_specs=[whole(v) for v in args] + [pl.BlockSpec((D, D), lambda i: (0, i))],
        out_specs=[pl.BlockSpec((1, total, D), lambda i: (i, 0, 0)), whole(outs[1])],
        scratch=[pltpu.VMEM((total, D), BF16)],
    )


def attend_kernel(q, k, v, o, lse):
    qm = stack_heads(q[0])
    scores = dot_nt(k[0], qm)
    peak = jnp.max(scores, axis=0, keepdims=True)
    weights = jnp.exp(scores - peak)
    total = jnp.sum(weights, axis=0, keepdims=True)
    both = dot(v[0].T, weights.astype(BF16)) * (1.0 / total)
    o[...] = unstack_t(both).astype(BF16)
    lse[0] = peak + jnp.log(total)


def part_spec(part, rows):
    return pl.BlockSpec((1, rows, 128), lambda i: (part, 0, i))


def attend(chain, joined, own):
    total = joined.shape[1]
    return chain(
        attend_kernel, [sds((own, D), BF16), sds((PAIRS, 1, 2 * own), F32)], [joined] * 3, room(8, total),
        "attend", grid=(PAIRS,),
        in_specs=[part_spec(0, own), part_spec(1, total), part_spec(2, total)],
        out_specs=[
            pl.BlockSpec((own, 128), lambda i: (0, i)),
            pl.BlockSpec((1, 1, 2 * own), lambda i: (i, 0, 0)),
        ],
    )


def qkv_attend_kernel(order, span, even, odd, mod, w, out_h, h1_o, o, lse, h1, joined, sems):
    own = 2 * span
    total = joined.shape[1]
    shift, scale = mod[0:1, 0:D], mod[0:1, D : 2 * D]
    for i, block in enumerate(block_refs(order, even, odd)):
        n, unused = norm(block[0:span, :].astype(F32))
        h1[pl.ds(i * span, span), :] = (n * (1.0 + scale) + shift).astype(BF16)
    h1_o[...] = h1[0:own, :]
    stores = []
    for part in (1, 2, 0):
        piece = w[:, part * D : (part + 1) * D]
        for i in range(total // own):
            rows = slice(i * own, (i + 1) * own)
            value = dot(h1[rows, :], piece)
            joined[part, rows, :] = ((value * SCALE) if part == 0 else value).astype(BF16)
        stores.append(pltpu.make_async_copy(joined.at[part], out_h.at[part], sems.at[part]))
        stores[-1].start()
    for i in range(PAIRS):
        qm = stack_heads(joined[0, 0:own, cols(i)])
        scores = dot_nt(joined[1, :, cols(i)], qm)
        peak = jnp.max(scores, axis=0, keepdims=True)
        weights = jnp.exp(scores - peak)
        sums = jnp.sum(weights, axis=0, keepdims=True)
        both = dot(joined[2, :, cols(i)].T, weights.astype(BF16)) * (1.0 / sums)
        o[:, cols(i)] = unstack_t(both).astype(BF16)
        lse[i] = peak + jnp.log(sums)
    for store in stores:
        store.wait()


def qkv_attend(chain, blocks, order, span, mod, w):
    total, own = len(order) * span, 2 * span
    if total > 1024:
        joined, h1 = qkv(chain, blocks, order, span, mod, w)
        mixed, lse = attend(chain, joined, own)
        return joined, h1, mixed, lse
    outs = [
        sds((3, total, D), BF16), sds((own, D), BF16), sds((own, D), BF16), sds((PAIRS, 1, 2 * own), F32)
    ]
    return chain(
        functools.partial(qkv_attend_kernel, order, span), outs, [blocks[0][0], blocks[2][0], mod, w], 10,
        "qkv_attend", out_specs=[pl.BlockSpec(memory_space=pl.ANY)] + [vmem()] * 3,
        scratch=[
            pltpu.VMEM((total, D), BF16), pltpu.VMEM((3, total, D), BF16), pltpu.SemaphoreType.DMA((3,))
        ],
    )


def two_terms(rows):
    high = rows.astype(BF16).astype(F32)
    return jnp.concatenate([high, rows - high], axis=0).astype(BF16)


def read_stats(block):
    own = block.shape[0] - 16
    held = block[own:, :].astype(F32)

    def line(at):
        rows = held[at : at + 4] + held[at + 4 : at + 8]
        return jnp.concatenate([rows[i : i + 1] for i in range(4)], axis=1)

    return line(0), line(8)


def attend_dq_kernel(q, k, v, do, dq):
    own = do.shape[0] - 16
    qm = stack_heads(q[0])
    dom = stack_heads(do[0:own, :])
    lse, delta = read_stats(do)
    probs = jnp.exp(dot_nt(k[0], qm) - lse)
    grad = dot_nt(v[0], dom)
    ds = (probs * (grad - delta)).astype(BF16)
    dq[...] = (unstack_t(dot(k[0].T, ds)) * SCALE).astype(BF16)


def attend_dq(chain, joined, do):
    own = do.shape[0] - 16
    total = joined.shape[1]
    return chain(
        attend_dq_kernel, [sds((own, D), BF16)], [joined, joined, joined, do], room(5, total),
        "attend_dq", grid=(PAIRS,),
        in_specs=[
            part_spec(0, own), part_spec(1, total), part_spec(2, total),
            pl.BlockSpec((own + 16, 128), lambda i: (0, i)),
        ],
        out_specs=[pl.BlockSpec((own, 128), lambda i: (0, i))],
    )[0]


def attend_dkv_kernel(chunks, dq, q, k, v, *refs):
    do, out = refs[:chunks], refs[-1]
    keys, values = k[0], v[0]
    own = keys.shape[0]
    dk = jnp.zeros((own, 128), F32)
    dv = jnp.zeros((own, 128), F32)
    for i in range(chunks):
        qm = stack_heads(q[0, i * own : (i + 1) * own, :])
        block = do[i][...]
        dom = stack_heads(block[0:own, :])
        lse, delta = read_stats(block)
        probs = jnp.exp(dot_nt(keys, qm) - lse)
        dv += dot(probs.astype(BF16), dom)
        grad = dot_nt(values, dom)
        ds = (probs * (grad - delta)).astype(BF16)
        dk += dot(ds, qm)
    lanes = pl.ds(pl.multiple_of(128 * pl.program_id(0), 128), 128)
    out[0:own, lanes] = dq[...]
    out[own : 2 * own, lanes] = dk.astype(BF16)
    out[2 * own : 3 * own, lanes] = dv.astype(BF16)


def last_kernel(chunks, *refs):
    first, even, w, mod, dx1, away, out, own_o, back_o, part = refs[4 + chunks :]
    attend_dkv_kernel(chunks, *refs[: 4 + chunks], part)
    own = part.shape[0] // 3
    half = part.shape[1]

    @pl.when(pl.program_id(0) == PAIRS // 2 - 1)
    def _():
        out[0 : 3 * own, 0:half] = first[...]
        out[0 : 3 * own, half:] = part[...]
        scale1 = mod[0:1, D : 2 * D]
        dh1 = sum(dot_nt(out[i * own : (i + 1) * own, :], w[:, i * D : (i + 1) * D]) for i in range(3))
        span = own_o.shape[0]
        n1, rstd = norm(start_rows(even.at[0], even.at[even.shape[0] // 2], span))
        sums = jnp.concatenate([colsum(dh1), colsum(n1 * dh1), jnp.zeros((14, D), F32)], axis=0)
        out[3 * own :, :] = sums.astype(BF16)
        grad = dx1[...] + norm_back(n1, rstd, (1.0 + scale1) * dh1)
        own_o[...] = grad[:span]
        back_o[0] = grad[span:].astype(BF16)
        back_o[1] = away[...]


def attend_dkv(chain, dq, joined, do, half, rest=()):
    own = dq.shape[0]
    span = own // 2
    shift = half * (PAIRS // 2)
    pair = lambda part, rows: pl.BlockSpec((1, rows, 128), lambda i: (part, 0, i + shift))
    specs = [
        pl.BlockSpec((own + 16, 128), functools.partial(lambda at, i: (at, i + shift), at)) for unused, at in do
    ]
    outs = [sds((3 * own, D // 2), BF16)]
    kernel = attend_dkv_kernel
    scratch = []
    if rest:
        outs = [sds((3 * own + 16, D), BF16), sds((span, D), F32), sds((2, span, D), BF16)]
        kernel = last_kernel
        scratch = [pltpu.VMEM((3 * own, D // 2), BF16)]
    return chain(
        functools.partial(kernel, len(do)), outs,
        [dq, joined, joined, joined, *(array for array, unused in do), *rest],
        room(4, joined.shape[1]) + (3 if rest else 0), "attend_dkv", grid=(PAIRS // 2,),
        in_specs=[pl.BlockSpec((own, 128), lambda i: (0, i + shift))]
        + [pair(0, joined.shape[1]), pair(1, own), pair(2, own)]
        + specs + [whole(v) for v in rest],
        out_specs=[whole(o) for o in outs], scratch=scratch,
    )


def start_rows(fa, fb, span):
    return jnp.concatenate([fa[0:span, :], fb[0:span, :]], axis=0).astype(F32)


def gelu_both(u):
    c = math.sqrt(2.0 / math.pi)
    square = u * u
    t = jnp.tanh(c * u * (1.0 + 0.044715 * square))
    half = 0.5 * (1.0 + t)
    slope = half + 0.5 * u * (1.0 - t * t) * (c * (1.0 + 3 * 0.044715 * square))
    return u * half, slope


STEPS = FF // D


def fetch(pairs, sems):
    copies = [pltpu.make_async_copy(a, b, sems.at[i]) for i, (a, b) in enumerate(pairs)]
    for copy in copies:
        copy.start()
    return copies


def forward_kernel(span, order, *refs):
    count = len(order)
    info, cap_len, *blocks = refs[: 2 + count]
    (o, h1, mod, ca, cb, up_b, down_b, wo, wq, wkv, wc, up, down,
     big_o, out_o, away_o, cap_o, h2_o, o2_o, x1, dx2_o, attn_o, attn2_o, sums_o, kv2, q2, p2,
     x2, low, dh3, offset) = refs[2 + count :]
    cap_rows = blocks[0].shape[0] - span

    big_o[2 * STEPS + 2] = o[...]
    big_o[2 * STEPS + 3] = h1[...]

    gate1, shift2, scale2, gate2, shift3, scale3, gate3 = (
        mod[0:1, i * D : (i + 1) * D] for i in range(2, 9)
    )

    length = cap_len[2 * info[0] + info[2]]
    for i, k in enumerate(order):
        here = slice(i * cap_rows, (i + 1) * cap_rows)
        cap_o[here, :] = blocks[i][span:, :]
        first = jnp.bitwise_xor(info[1], k) * cap_rows
        token = first + lax.broadcasted_iota(jnp.int32, (cap_rows, 128), 0)
        offset[here, :] = jnp.where(token < length, 0.0, NEGATIVE)
    dy = jnp.concatenate([ca[...], cb[...]], axis=0).astype(F32)
    big_o[2 * STEPS + 1] = (gate3 * dy).astype(BF16)

    attn = dot(o[...], wo[...])
    x1[...] = start_rows(blocks[0], blocks[1], span) + gate1 * attn
    attn_o[...] = attn.astype(BF16)
    n2, unused = norm(x1[...])
    h2 = (n2 * (1.0 + scale2) + shift2).astype(BF16)
    h2_o[...] = h2
    kv2[...] = dot(cap_o[...], wkv[...]).astype(BF16)
    q2[...] = (dot(h2, wq[...]) * SCALE).astype(BF16)
    for i in range(PAIRS):
        qm = stack_heads(q2[:, cols(i)])
        scores = dot_nt(kv2[:, cols(i)], qm) + offset[:, 0:1]
        peak = jnp.max(scores, axis=0, keepdims=True)
        weights = jnp.exp(scores - peak)
        probs = (weights * (1.0 / jnp.sum(weights, axis=0, keepdims=True))).astype(BF16)
        p2[i] = probs
        both = dot(kv2[:, D + i * 128 : D + (i + 1) * 128].T, probs)
        o2_o[:, cols(i)] = unstack_t(both).astype(BF16)
    attn2 = dot(o2_o[...], wc[...])
    x2[...] = x1[...] + gate2 * attn2
    attn2_o[...] = attn2.astype(BF16)

    n3, unused = norm(x2[...])
    big_o[2 * STEPS] = (n3 * (1.0 + scale3) + shift3).astype(BF16)
    for i in range(STEPS):
        piece = slice(i * D, (i + 1) * D)
        acted, slope = gelu_both(dot(big_o[2 * STEPS], up[:, piece]) + up_b[:, piece].astype(F32))
        acted = acted.astype(BF16)
        big_o[i] = acted
        dupper = (slope * dot_nt(big_o[2 * STEPS + 1], down[piece, :])).astype(BF16)
        big_o[STEPS + i] = dupper
        sums_o[8 + i : 9 + i, :] = colsum(dupper.astype(F32))
        if i:
            low[...] += dot(acted, down[piece, :])
            dh3[...] += dot_nt(dupper, up[:, piece])
        else:
            low[...] = dot(acted, down[piece, :])
            dh3[...] = dot_nt(dupper, up[:, piece])
    lower = low[...] + down_b[...].astype(F32)
    value = x2[...]
    result = (value + gate3 * lower).astype(BF16)
    out_o[...] = result[:span]
    away_o[...] = result[span:]
    dy = jnp.concatenate([ca[...], cb[...]], axis=0).astype(F32)
    n3, rstd = norm(value)
    back = dh3[...]
    sums_o[0:4, :] = jnp.zeros((4, D), F32)
    sums_o[4:5, :] = colsum(back)
    sums_o[5:6, :] = colsum(n3 * back)
    sums_o[6:7, :] = colsum(lower * dy)
    sums_o[7:8, :] = colsum(big_o[2 * STEPS + 1].astype(F32))
    sums_o[12:16, :] = jnp.zeros((4, D), F32)
    dx2_o[...] = dy + norm_back(n3, rstd, (1.0 + scale3) * back)


def backward_kernel(dx2_r, mod, attn2, kv2, q2, p2, x1, attn, o, lse, h2, o2, sums3,
                    wc, wq, wo, fac_o, dx1_o, do_o, sums_o):
    own = o.shape[0]
    slot = lambda i: slice(i * own, (i + 1) * own)
    gate1, scale2, gate2 = (mod[0:1, i * D : (i + 1) * D] for i in (2, 4, 5))
    sums_o[...] = sums3[...]
    fac_o[slot(0), :] = h2[...]
    fac_o[slot(2), :] = o2[...]
    dx2 = dx2_r[...]
    sums_o[3:4, :] = colsum(attn2[...].astype(F32) * dx2)
    da2 = (gate2 * dx2).astype(BF16)
    fac_o[slot(3), :] = da2
    do2 = dot_nt(da2, wc[...]).astype(BF16)
    for i in range(PAIRS):
        qm = stack_heads(q2[:, cols(i)])
        dom = stack_heads(do2[:, cols(i)])
        keys, values = kv2[:, cols(i)], kv2[:, D + i * 128 : D + (i + 1) * 128]
        probs = p2[i]
        fac_o[slot(5), cols(i)] = dot(probs, dom).astype(BF16)
        probs = probs.astype(F32)
        grad = dot_nt(values, dom)
        ds = (probs * (grad - colsum(probs * grad))).astype(BF16)
        fac_o[slot(1), cols(i)] = (unstack_t(dot(keys.T, ds)) * SCALE).astype(BF16)
        fac_o[slot(4), cols(i)] = dot(ds, qm).astype(BF16)
    dh2 = dot_nt(fac_o[slot(1), :], wq[...])
    n2, rstd = norm(x1[...])
    sums_o[1:2, :] = colsum(dh2)
    sums_o[2:3, :] = colsum(n2 * dh2)
    dx1 = dx2 + norm_back(n2, rstd, (1.0 + scale2) * dh2)
    dx1_o[...] = dx1
    sums_o[0:1, :] = colsum(attn[...].astype(F32) * dx1)

    da = (gate1 * dx1).astype(BF16)
    fac_o[slot(6), :] = da
    do = dot_nt(da, wo[...]).astype(BF16)
    do_o[0:own, :] = do
    both = do.astype(F32) * o[...].astype(F32)
    for i in range(PAIRS):
        t = both[:, cols(i)].T
        delta = [colsum(t[:HEAD]), colsum(t[HEAD:])]
        delta = [d[:, 128 * j : 128 * (j + 1)] for d in delta for j in range(own // 128)]
        sums = [lse[i][:, 128 * j : 128 * (j + 1)] for j in range(2 * own // 128)]
        held = [two_terms(jnp.concatenate(rows, axis=0)) for rows in (sums, delta)]
        do_o[own:, cols(i)] = jnp.concatenate(held, axis=0)
    fac_o[7 * own : 7 * own + 16, :] = sums_o[...].astype(BF16)
    at = do_place(own) * (own + 16)
    fac_o[7 * own + 16 : at, :] = jnp.zeros((at - 7 * own - 16, D), BF16)
    fac_o[at:, :] = do_o[...]


def forward(chain, info, cap_len, blocks, order, span, o, h1, mod, ca, cb, up_b, down_b, *weights):
    own = 2 * span
    cap_total = len(blocks) * (blocks[0][0].shape[1] - span)
    thin, wide = sds((own, D), BF16), sds((own, D), F32)
    half = sds((span, D), BF16)
    outs = [
        sds((2 * STEPS + 4, own, D), BF16), half, half, sds((cap_total, D), BF16), thin, thin, wide, wide,
        thin, thin, sds((16, D), F32), sds((cap_total, 2 * D), BF16), thin,
        sds((PAIRS, cap_total, 2 * own), BF16),
    ]
    here = [blocks[0][0], blocks[2][0], o, h1, mod, ca, cb, up_b, down_b]
    square = pltpu.VMEM((D, D), BF16)

    def kernel(info, cap_len, even, odd, *refs):
        forward_kernel(span, order, info, cap_len, *block_refs(order, even, odd), *refs)

    return chain(
        kernel, outs, [info, cap_len, *here, *weights], FWD, "forward",
        in_specs=[smem()] * 2 + [vmem()] * (len(here) + len(weights)),
        scratch=[pltpu.VMEM((own, D), F32)] * 3
        + [pltpu.VMEM((cap_total, 128), F32)],
    )


def do_place(own):
    return -(-(7 * own + 16) // (own + 16))


def backward(chain, here, weights):
    own = here[0].shape[0]
    outs = [
        sds(((do_place(own) + 1) * (own + 16), D), BF16), sds((own, D), F32),
        sds((own + 16, D), BF16),
        sds((16, D), F32),
    ]
    square = pltpu.VMEM((D, D), BF16)
    return chain(
        backward_kernel, outs, [*here, *weights], BWD, "backward",
    )


def pick_rows(info, x):
    source = lax.broadcasted_iota(jnp.int32, (D, D // 2), 0)
    column = lax.broadcasted_iota(jnp.int32, (D, D // 2), 1)
    block = sum((column >= 96 * i).astype(jnp.int32) for i in (1, 2, 3))
    wanted = 96 * jnp.bitwise_xor(info[1], 2 * block) + column - 96 * block
    choose = (source == wanted).astype(F32).astype(BF16)
    return dot(x, choose).astype(BF16)


def emit(first, info, tiles, blocks, send_o, keep_o):
    place = {True: 0, False: 0}
    for r in range(4):
        sent = bool(r & first)
        (send_o if sent else keep_o)[place[sent]] = tiles[jnp.bitwise_xor(info[0], r), blocks]
        place[sent] += 1


def down_grad_kernel(info, fac, fac_p, send_o, keep_o, tiles):
    for e in range(4):
        owner = jnp.bitwise_xor(info[1], 2 * e)
        half = pl.multiple_of(lax.rem(owner, 2) * 384, 128)
        where = (lax.div(owner, 2), slice(None), pl.ds(half, 384))
        grad = dot_tn(fac[where], fac[2 * STEPS + 1]) + dot_tn(fac_p[where], fac_p[9])
        for q in range(4):
            tiles[q, e] = grad[96 * q : 96 * (q + 1)].astype(BF16)
    emit(1, info, tiles, slice(0, 4), send_o, keep_o)


def up_grad_kernel(info, fac, fac_p, send_o, keep_o, tiles):
    x, xp = pick_rows(info, fac[8]), pick_rows(info, fac_p[8])
    for q in range(4):
        grad = dot_tn(x, fac[4 + q]) + dot_tn(xp, fac_p[4 + q])
        for e in range(4):
            tiles[q, e] = grad[96 * e : 96 * (e + 1)].astype(BF16)
    emit(2, info, tiles, slice(0, 4), send_o, keep_o)


def put(tiles, q, grad):
    for e in range(4):
        tiles[q, e] = grad[96 * e : 96 * (e + 1)].astype(BF16)


def emit_both(info, tiles, sx, kx, sy, ky):
    emit(1, info, tiles, slice(0, 2), sx, kx)
    emit(2, info, tiles, slice(2, 4), sy, ky)


def cross_grad_kernel(own, info, cap, fac, fac_p, wkv, sx, kx, sy, ky, dcap_o, tiles):
    def slot(ref, i):
        return ref[i * own : (i + 1) * own, :]

    def pair(x, y):
        left, left_p = pick_rows(info, slot(fac, x)), pick_rows(info, slot(fac_p, x))
        return dot_tn(left, slot(fac, y)) + dot_tn(left_p, slot(fac_p, y))

    put(tiles, 0, pair(0, 1))
    x = pick_rows(info, cap[...])
    rows = cap.shape[0] // 4
    xp = jnp.concatenate([x[rows * i : rows * (i + 1)] for i in (1, 0, 3, 2)], axis=0)
    for q in (1, 2):
        put(tiles, q, dot_tn(x, slot(fac, q + 3)) + dot_tn(xp, slot(fac_p, q + 3)))
    put(tiles, 3, pair(2, 3))
    emit_both(info, tiles, sx, kx, sy, ky)

    rows = cap.shape[0] // 8

    def even(x):
        places = [rows * order_place(k) for k in range(8)]
        parts = [
            total(slot(fac, x)[places[k] : places[k] + rows], slot(fac_p, x)[places[k + 1] : places[k + 1] + rows])
            for k in (0, 2, 4, 6)
        ]
        return jnp.concatenate(parts, axis=0)

    dcap_o[...] = (dot_nt(even(4), wkv[:, 0:D]) + dot_nt(even(5), wkv[:, D : 2 * D])).astype(BF16)


def attn_grad_kernel(info, da, o, h1, da_p, o_p, h1_p, dqkv, dqkv_p, sx, kx, sy, ky, tiles):
    own = da.shape[0]
    x, xp = pick_rows(info, h1[0]), pick_rows(info, h1_p[0])
    for i in range(3):
        slot = slice(i * own, (i + 1) * own)
        put(tiles, i, dot_tn(x, dqkv[slot, :]) + dot_tn(xp, dqkv_p[slot, :]))
    x, xp = pick_rows(info, o[0]), pick_rows(info, o_p[0])
    put(tiles, 3, dot_tn(x, da[...]) + dot_tn(xp, da_p[...]))
    emit_both(info, tiles, sx, kx, sy, ky)


def grad_call(chain, kernel, info, args, name, shape, outs, in_specs=None):
    return chain(
        kernel, [sds(o, BF16) for o in outs], [info, *args], 5, name, grid=(1,) if in_specs else None,
        in_specs=[smem()] + (in_specs or [vmem()] * len(args)),
        scratch=[pltpu.VMEM(shape, BF16)],
    )


def total(*refs):
    return sum(r.astype(F32) for r in refs).astype(BF16)


def add_first_kernel(keep, recv, keep_o, send_o):
    keep_o[...] = total(keep[0], recv[0])
    send_o[...] = total(keep[1], recv[1])


def add_both_kernel(kx, rx, ky, ry, kx_o, sx_o, ky_o, sy_o):
    add_first_kernel(kx, rx, kx_o, sx_o)
    add_first_kernel(ky, ry, ky_o, sy_o)


def sum_rows(early, early_p, late, late_p):
    first = late[0:2, :].astype(F32) + late_p[0:2, :].astype(F32)
    both = early[0:12, :].astype(F32) + early_p[0:12, :].astype(F32)
    return jnp.concatenate([first, both, jnp.zeros((2, D), F32)], axis=0).astype(BF16)


def mlp_second_kernel(ka, ra, kb, rb, fac, fac_p, late, late_p, keep_o, send_o):
    for g, (keep, recv) in enumerate(((ka, ra), (kb, rb))):
        for e in range(4):
            (send_o if e % 2 else keep_o)[e // 2, 96 * g : 96 * (g + 1), :] = total(keep[e], recv[e])
    rows = sum_rows(fac, fac_p, late, late_p)
    for ref in (keep_o, send_o):
        for i in range(2):
            ref[i, 192:208, :] = rows


def mlp_third_kernel(keep, recv, keep_o, send_o):
    keep_o[...] = total(keep[0], recv[0])
    send_o[0:192, :] = total(keep[1, 0:192, :], recv[1, 0:192, :])
    send_o[192:208, :] = total(keep[0, 192:208, :], recv[0, 192:208, :])


def mlp_fourth_kernel(keep, recv, out):
    out[0:192, :] = total(keep[0:192, :], recv[0:192, :])
    out[192:208, :] = keep[192:208, :]
    out[208:224, :] = recv[192:208, :]


def order_place(k):
    return 2 * (k % 4) + k // 4


def second_kernel(kx, rx, ky, ry, *refs):
    caption, (keep_o, send_o) = refs[:-2], refs[-2:]
    for e in range(4):
        out = send_o if e % 2 else keep_o
        keep, recv = ((kx, rx), (ky, ry))[e // 2]
        out[e // 2, 0:96, :] = total(keep[e % 2], recv[e % 2])
        if caption:
            rows = caption[0].shape[0] // 4
            out[e // 2, 96:, :] = caption[0][rows * e : rows * (e + 1), :]


def third_kernel(keep, recv, keep_o, send_o):
    keep_o[...] = total(keep[0], recv[0])
    send_o[...] = total(keep[1], recv[1])


def fourth_kernel(keep, recv, c_keep, c_recv, out, same_o, away_o):
    out[0:96, :] = total(keep[...], recv[...])
    out[96:, :] = total(c_keep[0:96, :], c_recv[0:96, :])
    same_o[...] = c_keep[96:, :].astype(F32)
    away_o[...] = c_recv[96:, :].astype(F32)


def swap(x, axis, size, k):
    return lax.ppermute(x, axis, [(i, i ^ k) for i in range(size)])


def over_x(x):
    return swap(x, "band", 4, 1)


def over_y(x):
    return swap(x, "band", 4, 2)


def to_band(x):
    return [x] + [swap(x, "band", 4, t) for t in (1, 2, 3)]


def mlp_finish_kernel(info, t0, t1, t2, t3, down_o, up_o):
    for r, tile in enumerate((t0, t1, t2, t3)):
        q = jnp.bitwise_xor(info[0], r)
        down_o[pl.ds(pl.multiple_of(96 * q, 96), 96), :] = tile[0:96, :].astype(F32)
        up_o[:, pl.ds(pl.multiple_of(D * q, D), D)] = tile[96:192, :].astype(F32)


def last_finish_kernel(info, t0, t1, t2, t3, in_o, out_o, cq_o, ckv_o, co_o, tiles):
    for r, tile in enumerate((t0, t1, t2, t3)):
        tiles[jnp.bitwise_xor(info[0], r)] = tile[...]
    for i in range(3):
        in_o[:, i * D : (i + 1) * D] = tiles[i, 0:96, :].astype(F32)
    out_o[...] = tiles[3, 0:96, :].astype(F32)
    cq_o[...] = tiles[0, 96:, :].astype(F32)
    ckv_o[:, 0:D] = tiles[1, 96:, :].astype(F32)
    ckv_o[:, D:] = tiles[2, 96:, :].astype(F32)
    co_o[...] = tiles[3, 96:, :].astype(F32)


def finish(chain, kernel, info, tiles, widths, name, scratch=(), held=()):
    outs = [sds(w, F32) for w in widths] + [sds(h.shape, h.dtype) for h in held]
    tiles = [*tiles, *held]
    return chain(
        kernel, outs, [info, *tiles], 5, name, grid=(1,), in_specs=[smem()] + [whole(t) for t in tiles],
        out_specs=[whole(o) for o in outs], scratch=scratch,
    )


def plain_reduce(x, y, owners):
    grad = lax.psum_scatter(dot_tn(x, y).astype(BF16), "seq", scatter_dimension=0, tiled=True)
    return lax.psum(grad, "band").astype(F32)


def on_device(bands, seqs, frames, caption, timesteps, cap_len, attn_in, attn_out, cross_query,
              cross_keyval, cross_out, mlp_up, up_bias, mlp_down, down_bias, ada_weight, ada_bias,
              time_first, first_bias, time_second, second_bias, cotangent):
    span = frames.shape[1]
    own = 2 * span
    cap_rows = caption.shape[1]
    items = timesteps.shape[0]
    halves = seqs // 2
    band = lax.axis_index("band")
    seq = lax.axis_index("seq")
    half = (seq >= halves).astype(jnp.int32)
    item = 2 * band + half
    info = jnp.stack([band, seq, half]).astype(jnp.int32)

    chain = Chain()

    order = [k for i in range(halves) for k in (i, i + halves)]
    same, other = pick(chain, info, frames, caption)
    even = [same] + [swap(same if k < halves else other, "seq", seqs, k) for k in range(2, seqs, 2)]

    steps = jnp.take(timesteps, jnp.bitwise_xor(jnp.arange(items), item))
    width = time_first.shape[0] // 2
    freq = jnp.exp(-math.log(10000.0) * jnp.arange(width, dtype=F32) / width)
    angle = steps.astype(F32)[:, None] * freq[None, :]
    embed = jnp.concatenate([jnp.cos(angle), jnp.sin(angle)], axis=1)
    row = lambda v: v.reshape(1, -1)
    pre_cond, mod = modulation(
        chain, embed, time_first, row(first_bias), time_second, row(second_bias), ada_weight, row(ada_bias)
    )
    cot_own, cot_other = pick(chain, info, cotangent)
    cot_other = swap(cot_other, "seq", seqs, halves)

    even = stack(chain, even, "blocks")
    odd = swap(even, "seq", seqs, 1)
    blocks = [(odd if k % 2 else even, k // 2) for k in order]
    joined, h1, mixed, lse = qkv_attend(chain, blocks, order, span, mod, attn_in)

    cap_total = seqs * cap_rows
    (big, out, out_back, cap_all, h2, o2, x1, dx2, attn, attn2, sums3, kv2, q2, p2) = forward(
        chain, info, cap_len, blocks, order, span, mixed, h1, mod, cot_own, cot_other, row(up_bias),
        row(down_bias), attn_out, cross_query, cross_keyval, cross_out, mlp_up, mlp_down,
    )
    fast = bands == 4 and seqs == 8
    if fast:
        big_p = swap(big, "seq", seqs, 1)
    fac, dx1, do, early = backward(
        chain, [dx2, mod, attn2, kv2, q2, p2, x1, attn, mixed, lse, h2, o2, sums3],
        [cross_out, cross_query, attn_out],
    )
    if fast:
        fac_p = swap(fac, "seq", seqs, 1)
    got = {k: (swap(do, "seq", seqs, k), 0) for k in range(2 if fast else 1, halves)}
    got[0] = (do, 0)
    if fast:
        got[1] = (fac_p, do_place(own))
        whole_tiles, pieces, halved = (4, 4, 96, D), [(2, 4, 96, D)] * 2, [(2, 2, 96, D)] * 4
        args = [big, big_p]
        sa, ka = grad_call(chain, down_grad_kernel, info, args, "down_grad", whole_tiles, pieces)
        ra = over_x(sa)
        sb, kb = grad_call(chain, up_grad_kernel, info, args, "up_grad", whole_tiles, pieces)
        rb = over_y(sb)
        cx, ckx, cy, cky, dcap = grad_call(
            chain, functools.partial(cross_grad_kernel, own), info, [cap_all, fac, fac_p, cross_keyval],
            "cross_grad", whole_tiles, halved + [(cap_total // 2, D)],
        )
        crx, cry = over_x(cx), over_y(cy)
    dq = attend_dq(chain, joined, do)
    do_blocks = [got[k] for k in range(halves)]
    dkv_first = attend_dkv(chain, dq, joined, do_blocks, 0)[0]
    dqkv, grad_own, back = attend_dkv(
        chain, dq, joined, do_blocks, 1, [dkv_first, even, attn_in, mod, dx1, out_back]
    )
    back = swap(back, "seq", seqs, halves)
    if fast:
        dqkv_p = swap(dqkv, "seq", seqs, 1)
        half, quarter, tile = sds((4, 96, D), BF16), sds((2, 96, D), BF16), sds((96, D), BF16)
        ka, sa, kb, sb = chain(add_both_kernel, [half] * 4, [ka, ra, kb, rb], 2, "mlp_add1")
        ra, rb = over_y(sa), over_x(sb)
        slots = [pl.BlockSpec((own, D), lambda *i: (6, 0))] + [
            pl.BlockSpec((1, own, D), functools.partial(lambda at, *i: (at, 0, 0), at))
            for at in (2 * STEPS + 2, 2 * STEPS + 3)
        ]
        tx, tkx, ty, tky = grad_call(
            chain, attn_grad_kernel, info, [fac, big, big, fac_p, big_p, big_p, dqkv, dqkv_p], "attn_grad",
            whole_tiles, halved, in_specs=slots * 2 + [whole(dqkv)] * 2,
        )
        trx, try_ = over_x(tx), over_y(ty)
        grad_frames, out = place(
            chain, info, [(grad_own, (back, 0)), (out, (back, 1))], [F32, BF16], "place_frames"
        )
        sum_at, late_at = 7 * own // 16, 3 * own // 16
        sum_spec = pl.BlockSpec((16, D), lambda *i: (sum_at, 0))
        late_spec = pl.BlockSpec((16, D), lambda *i: (late_at, 0))
        ckx, cx, cky, cy = chain(add_both_kernel, [quarter] * 4, [ckx, crx, cky, cry], 4, "cross_add1")
        crx, cry = over_y(cx), over_x(cy)
        keep, send = chain(
            mlp_second_kernel, [sds((2, 208, D), BF16)] * 2, [ka, ra, kb, rb, fac, fac_p, dqkv, dqkv_p], 4,
            "mlp_add2", grid=(1,), in_specs=[vmem()] * 4 + [sum_spec] * 2 + [late_spec] * 2,
        )
        recv = swap(send, "seq", seqs, 2)
        tkx, tx, tky, ty = chain(add_both_kernel, [quarter] * 4, [tkx, trx, tky, try_], 4, "attn_add1")
        trx, try_ = over_y(tx), over_x(ty)
        keep, send = chain(mlp_third_kernel, [sds((208, D), BF16)] * 2, [keep, recv], 4, "mlp_z1")
        recv = swap(send, "seq", seqs, 4)
        rows = 96 + cap_rows
        c_keep, c_send = chain(
            second_kernel, [sds((2, rows, D), BF16)] * 2, [ckx, crx, cky, cry, dcap], 4, "cross_add2",
        )
        c_recv = swap(c_send, "seq", seqs, 2)
        t_keep, t_send = chain(second_kernel, [quarter] * 2, [tkx, trx, tky, try_], 4, "attn_add2")
        t_recv = swap(t_send, "seq", seqs, 2)
        a_all = to_band(chain(mlp_fourth_kernel, [sds((224, D), BF16)], [keep, recv], 4, "mlp_z2")[0])
        c_keep, c_send = chain(third_kernel, [sds((rows, D), BF16)] * 2, [c_keep, c_recv], 4, "cross_z1")
        c_recv = swap(c_send, "seq", seqs, 4)
        t_keep, t_send = chain(third_kernel, [tile] * 2, [t_keep, t_recv], 4, "attn_z1")
        t_recv = swap(t_send, "seq", seqs, 4)
        t_done, cap_same, cap_away = chain(
            fourth_kernel, [sds((192, D), BF16)] + [sds((cap_rows, D), F32)] * 2,
            [t_keep, t_recv, c_keep, c_recv], 4, "other_z2",
        )
        t_all = to_band(t_done)
        g_down, g_up = finish(chain, mlp_finish_kernel, info, a_all, [(384, D), (96, FF)], "mlp_finish")
        grad_caption = place(chain, info, [(cap_same, cap_away)], [F32], "place_caption")[0]
        sums = a_all
    else:
        grad_frames, out = place(
            chain, info, [(grad_own, (back, 0)), (out, (back, 1))], [F32, BF16], "place_frames"
        )
        dkv2 = jnp.concatenate([fac[4 * own : 4 * own + cap_total], fac[5 * own : 5 * own + cap_total]], axis=1)
        dcap = dot_nt(dkv2, cross_keyval).astype(BF16).reshape(seqs, cap_rows, D)
        place_of = jnp.asarray([order.index(k) for k in range(seqs)])
        dcap = dcap[place_of[jnp.bitwise_xor(seq, jnp.arange(seqs))]].reshape(cap_total, D)
        dcap = jnp.where(half == 0, jnp.stack([dcap, 0 * dcap]), jnp.stack([0 * dcap, dcap]))
        grad_caption = lax.psum_scatter(dcap, "seq", scatter_dimension=1, tiled=True).astype(F32)
        rows = jnp.concatenate([dqkv[3 * own : 3 * own + 2].astype(F32), early[0:12], jnp.zeros((2, D), F32)])
        for k in range(1, halves):
            if k & (k - 1) == 0:
                rows = rows + swap(rows, "seq", seqs, k)
        rows = jnp.concatenate([rows, swap(rows, "seq", seqs, halves)]).astype(BF16)
        sums = [rows] + [swap(rows, "band", bands, t) for t in range(1, bands)]

    g_ada, gb_ada, g_t2, gb_t2, g_t1, gb_t1, gb_down, gb_up = mod_back(
        chain, info, sums, ada_weight, pre_cond, embed, time_second, seqs
    )

    if fast:
        g_in, g_out, g_cq, g_ckv, g_co = finish(
            chain, last_finish_kernel, info, t_all, [(96, 3 * D), (96, D), (96, D), (96, 2 * D), (96, D)],
            "last_finish", [pltpu.VMEM((4, 192, D), BF16)],
        )
    else:
        slot = lambda i: fac[i * own : (i + 1) * own]
        acted = jnp.concatenate([big[i] for i in range(FF // D)], axis=1)
        dupper = jnp.concatenate([big[FF // D + i] for i in range(FF // D)], axis=1)
        g_down = plain_reduce(acted, big[2 * STEPS + 1], seqs)
        g_up = plain_reduce(big[2 * STEPS], dupper, seqs)
        g_cq = plain_reduce(slot(0), slot(1), seqs)
        g_ckv = plain_reduce(cap_all, jnp.concatenate([slot(4), slot(5)], axis=1), seqs)
        g_co = plain_reduce(slot(2), slot(3), seqs)
        g_out = plain_reduce(mixed, slot(6), seqs)
        g_in = plain_reduce(h1, jnp.concatenate([dqkv[i * own : (i + 1) * own] for i in range(3)], axis=1), seqs)

    flat = lambda v: v.reshape(-1)
    return (
        out, grad_frames, grad_caption, g_in, g_out, g_cq, g_ckv, g_co, g_up, flat(gb_up), g_down,
        flat(gb_down), g_ada, flat(gb_ada), g_t1, flat(gb_t1), g_t2, flat(gb_t2),
    )


def solution(mesh):
    split = P("band", "seq", None)
    rows, flat = P("seq", None), P("seq")
    return jax.shard_map(
        functools.partial(on_device, mesh.shape["band"], mesh.shape["seq"]),
        mesh=mesh,
        in_specs=(split, split) + (P(),) * 17 + (split,),
        out_specs=(split, split, split, rows, rows, rows, rows, rows, rows, flat, rows, flat, rows, flat,
                   rows, flat, rows, flat),
        check_vma=False,
    )
```

```python
import functools
import math

import jax
import jax.numpy as jnp
from jax import lax
from jax.experimental import pallas as pl
from jax.experimental.pallas import tpu as pltpu
from jax.sharding import PartitionSpec as P

D = 768
HEAD = 64
PAIRS = 6
FF = 3072
EPSILON = 1e-06
NEGATIVE = -1e30
SCALE = 0.125
F32 = jnp.float32
BF16 = jnp.bfloat16
MIB = 1 << 20
MODMIB = 4
COST = 1000000
FWD = 9
BWD = 6


def dot(a, b):
    return jnp.dot(a, b, preferred_element_type=F32)


def dot_nt(a, b):
    return lax.dot_general(a, b, (((1,), (1,)), ((), ())), preferred_element_type=F32)


def dot_tn(a, b):
    return lax.dot_general(a, b, (((0,), (0,)), ((), ())), preferred_element_type=F32)


def split_dot(x, w, contract=0):
    high = x.astype(BF16).astype(F32)
    both = jnp.concatenate([high, x - high], axis=0).astype(BF16)
    out = lax.dot_general(
        both, w, (((1,), (contract,)), ((), ())), preferred_element_type=F32
    )
    return out[: x.shape[0]] + out[x.shape[0] :]


def silu(v):
    return v * (1.0 / (1.0 + jnp.exp(-v)))


def silu_grad(v):
    s = 1.0 / (1.0 + jnp.exp(-v))
    return s * (1.0 + v * (1.0 - s))


def norm(v):
    mean = jnp.mean(v, axis=-1, keepdims=True)
    centred = v - mean
    spread = jnp.mean(centred * centred, axis=-1, keepdims=True)
    rstd = lax.rsqrt(spread + EPSILON)
    return centred * rstd, rstd


def norm_back(n, rstd, w):
    return (
        w - jnp.mean(w, axis=-1, keepdims=True) - n * jnp.mean(w * n, axis=-1, keepdims=True)
    ) * rstd


def colsum(v):
    return jnp.sum(v, axis=0, keepdims=True)


def cols(i):
    return slice(i * 128, (i + 1) * 128)


def head_masks():
    lane = lax.broadcasted_iota(jnp.int32, (1, 128), 1)
    first = (lane < HEAD).astype(F32)
    return first.astype(BF16), (1.0 - first).astype(BF16)


def stack_heads(block):
    first, second = head_masks()
    return jnp.concatenate([block * first, block * second], axis=0)


def unstack_t(both):
    rows = both.shape[1] // 2
    pair = jnp.concatenate([both[:HEAD, :rows], both[HEAD:, rows:]], axis=0)
    return pair.T


def sds(shape, dtype):
    return jax.ShapeDtypeStruct(shape, dtype)


def vmem():
    return pl.BlockSpec(memory_space=pltpu.VMEM)


def smem():
    return pl.BlockSpec(memory_space=pltpu.SMEM)


def whole(a):
    return pl.BlockSpec(a.shape, lambda *i: (0,) * len(a.shape))


class Chain:
    def __init__(self):
        self.token = None

    def __call__(self, kernel, outs, args, mib, name, grid=None, in_specs=None, out_specs=None, scratch=(), early=()):
        outs = list(outs)
        in_specs = list(in_specs or [vmem()] * len(args))
        out_specs = list(out_specs or [vmem()] * len(outs))
        count = len(args)
        body = kernel
        unread = [*early] + ([] if self.token is None else [self.token])
        if unread:
            args = [*args, *unread]
            in_specs += [vmem()] * len(early) + [pl.BlockSpec(memory_space=pl.ANY)] * (len(unread) - len(early))
            body = lambda *refs: kernel(*refs[:count], *refs[count + len(unread) :])
        results = pl.pallas_call(
            body,
            **({} if grid is None else {"grid": grid}),
            out_shape=outs,
            in_specs=in_specs,
            out_specs=out_specs,
            scratch_shapes=list(scratch),
            compiler_params=pltpu.CompilerParams(vmem_limit_bytes=mib * MIB),
            cost_estimate=pl.CostEstimate(flops=1000000000, bytes_accessed=COST, transcendentals=0),
            name=name,
        )(*args)
        self.token = min(results, key=lambda r: r.size * r.dtype.itemsize)
        return results

    def after(self, x):
        self.token = x


def room(mib, frames):
    return min(56, mib * max(1, frames // 1024))


def pick_kernel(info, *refs):
    half = info[2]
    parts, (mine_o, theirs_o, sems) = refs[:-3], refs[-3:]
    copies = []
    at = 0
    for x in parts:
        rows = pl.ds(at, x.shape[1])
        for source, out in ((half, mine_o), (1 - half, theirs_o)):
            copies.append(pltpu.make_async_copy(x.at[source], out.at[rows], sems.at[len(copies)]))
        at += x.shape[1]
    for copy in copies:
        copy.start()
    for copy in copies:
        copy.wait()


def pick(chain, info, *parts, early=()):
    out = sds((sum(x.shape[1] for x in parts), D), BF16)
    anywhere = pl.BlockSpec(memory_space=pl.ANY)
    return chain(
        pick_kernel, [out, out], [info, *parts], 4, "pick", in_specs=[smem()] + [anywhere] * len(parts),
        out_specs=[anywhere] * 2, scratch=[pltpu.SemaphoreType.DMA((2 * len(parts),))],
        early=early,
    )


def stack_kernel(*refs):
    for i, ref in enumerate(refs[:-1]):
        refs[-1][i] = ref[...]


def stack(chain, arrays, name):
    out = sds((len(arrays),) + arrays[0].shape, arrays[0].dtype)
    return chain(stack_kernel, [out], arrays, 4, name)[0]


def place_kernel(info, *refs):
    count = len(refs) // 3
    for i in range(count):
        kept, received, out = refs[2 * i], refs[2 * i + 1], refs[2 * count + i]
        out[info[2]] = kept[...].astype(out.dtype)
        out[1 - info[2]] = received[...].reshape(kept.shape).astype(out.dtype)


def place(chain, info, pairs, dtypes, name):
    args, specs = [info], [smem()]
    for kept, received in pairs:
        args.append(kept)
        specs.append(whole(kept))
        if isinstance(received, tuple):
            args.append(received[0])
            specs.append(pl.BlockSpec((1,) + kept.shape, functools.partial(lambda at, i: (at, 0, 0), received[1])))
        else:
            args.append(received)
            specs.append(whole(received))
    outs = [sds((2,) + kept.shape, dtype) for (kept, unused), dtype in zip(pairs, dtypes)]
    return chain(
        place_kernel, outs, args, 4, name, grid=(1,), in_specs=specs, out_specs=[whole(o) for o in outs]
    )


def mod_kernel(embed, t1, b1, t2, b2, w, b, both_o, mod_o, act):
    @pl.when(pl.program_id(0) == 0)
    def _():
        pre = split_dot(embed[...], t1[...]) + b1[...].astype(F32)
        cond = split_dot(silu(pre), t2[...]) + b2[...].astype(F32)
        both_o[0] = pre
        both_o[1] = cond
        act[...] = silu(cond)

    mod_o[...] = split_dot(act[...], w[...]) + b[...].astype(F32)


def modulation(chain, embed, t1, b1, t2, b2, w, b):
    items = embed.shape[0]
    outs = [sds((2, items, D), F32), sds((items, 9 * D), F32)]
    return chain(
        mod_kernel, outs, [embed, t1, b1, t2, b2, w, b], MODMIB, "modulation", grid=(9,),
        in_specs=[whole(v) for v in (embed, t1, b1, t2, b2)]
        + [pl.BlockSpec((D, D), lambda i: (0, i)), pl.BlockSpec((1, D), lambda i: (0, i))],
        out_specs=[whole(outs[0]), pl.BlockSpec((items, D), lambda i: (0, i))],
        scratch=[pltpu.VMEM((items, D), F32)],
    )


def outer_sum(left_t, right):
    lh = left_t.astype(BF16)
    ll = (left_t - lh.astype(F32)).astype(BF16)
    rh = right.astype(BF16)
    rl = (right - rh.astype(F32)).astype(BF16)
    return dot(lh, rh) + dot(ll, rh) + dot(lh, rl)


def own_rows_t(info, size, v):
    row = lax.broadcasted_iota(jnp.int32, (size, v.shape[1]), 0)
    column = lax.broadcasted_iota(jnp.int32, (size, v.shape[1]), 1)
    choose = (column == row + size * info[1]).astype(F32).astype(BF16)
    high = v.astype(BF16)
    rest = (v - high.astype(F32)).astype(BF16)
    return dot_nt(choose, high) + dot_nt(choose, rest)


def mod_back_kernel(bands, seqs, info, *refs):
    sums = refs[:bands]
    (both, embed, t2, w_h, g_ada_h, gb_ada, g_t2, gb_t2, g_t1, gb_t1, gb_down, gb_up,
     w, g_ada, sems, acc, dmod, all_bias) = refs[bands:]
    pieces = [pl.ds(i * D, D) for i in range(9)]
    copies = fetch([(w_h.at[:, piece], w.at[i]) for i, piece in enumerate(pieces)], sems)
    own_act = own_rows_t(info, D // seqs, silu(both[1]))
    bias = jnp.zeros((5, D), F32)
    for t in range(bands):
        held = sums[t][sums[t].shape[0] - 32 :, :].astype(F32)
        for u in range(2):
            r = 2 * t + u
            for p in range(9):
                dmod[p, r : r + 1, :] = held[16 * u + p : 16 * u + p + 1]
            bias += held[16 * u + 9 : 16 * u + 14]
    stores = []
    for i, piece in enumerate(pieces):
        part = dmod[i]
        g_ada[i] = outer_sum(own_act, part)
        stores.append(pltpu.make_async_copy(g_ada.at[i], g_ada_h.at[:, piece], sems.at[9 + i]))
        stores[-1].start()
        all_bias[:, i * D : (i + 1) * D] = jnp.broadcast_to(colsum(part), (8, D))
        copies[i].wait()
        term = split_dot(part, w[i], contract=1)
        if i:
            acc[...] += term
        else:
            acc[...] = term

    def own_part(row):
        size = row.shape[1] // seqs
        rows = jnp.broadcast_to(row, (8, row.shape[1]))
        return pltpu.roll(rows, row.shape[1] - info[1] * size, 1)[0:1, 0:size]

    size = 9 * D // seqs
    gb_ada[...] = pltpu.roll(all_bias[...], 9 * D - info[1] * size, 1)[0:1, 0:size]
    gb_down[...] = own_part(bias[0:1])
    gb_up[...] = own_part(jnp.concatenate([bias[1 + i : 2 + i] for i in range(4)], axis=1))
    dcond = acc[...] * silu_grad(both[1])
    g_t2[...] = outer_sum(own_rows_t(info, D // seqs, silu(both[0])), dcond)
    gb_t2[...] = own_part(colsum(dcond))
    dpre = split_dot(dcond, t2[...], contract=1) * silu_grad(both[0])
    g_t1[...] = outer_sum(own_rows_t(info, g_t1.shape[0], embed[...]), dpre)
    gb_t1[...] = own_part(colsum(dpre))
    for store in stores:
        store.wait()


def mod_back(chain, info, sums, w, both, embed, t2, seqs):
    bands = len(sums)
    items = 2 * bands
    m = D // seqs
    line = lambda n: sds((1, n // seqs), F32)
    outs = [
        sds((m, 9 * D), F32), line(9 * D), sds((m, D), F32), line(D), sds((embed.shape[1] // seqs, D), F32),
        line(D), line(D), line(FF),
    ]
    anywhere = pl.BlockSpec(memory_space=pl.ANY)
    here = [*sums, both, embed, t2]
    return chain(
        functools.partial(mod_back_kernel, bands, seqs), outs, [info, *here, w], 15, "modulation_back",
        grid=(1,), in_specs=[smem()] + [whole(v) for v in here] + [anywhere],
        out_specs=[anywhere] + [whole(o) for o in outs[1:]],
        scratch=[
            pltpu.VMEM((9, D, D), BF16), pltpu.VMEM((9, m, D), F32), pltpu.SemaphoreType.DMA((18,)),
            pltpu.VMEM((items, D), F32), pltpu.VMEM((9, items, D), F32), pltpu.VMEM((8, 9 * D), F32),
        ],
    )


def block_refs(order, even, odd):
    return [(odd if k % 2 else even).at[k // 2] for k in order]


def qkv_kernel(order, span, even, odd, mod, w, out, h1_o, h1):
    frames = block_refs(order, even, odd)
    blocks = len(order)
    own = 2 * span

    @pl.when(pl.program_id(0) == 0)
    def _():
        shift, scale = mod[0:1, 0:D], mod[0:1, D : 2 * D]
        for i in range(blocks):
            n, unused = norm(frames[i][0:span, :].astype(F32))
            h1[pl.ds(i * span, span), :] = (n * (1.0 + scale) + shift).astype(BF16)
        h1_o[...] = h1[0:own, :]

    factor = jnp.where(pl.program_id(0) == 0, SCALE, 1.0)

    @pl.loop(0, blocks * span // own)
    def _(i):
        rows = pl.ds(pl.multiple_of(i * own, own), own)
        out[0, rows, :] = (dot(h1[rows, :], w[...]) * factor).astype(BF16)


def qkv(chain, blocks, order, span, mod, w):
    total = len(order) * span
    outs = [sds((3, total, D), BF16), sds((2 * span, D), BF16)]
    args = [blocks[0][0], blocks[2][0], mod]
    return chain(
        functools.partial(qkv_kernel, order, span), outs, [*args, w], room(16, total), "qkv", grid=(3,),
        in_specs=[whole(v) for v in args] + [pl.BlockSpec((D, D), lambda i: (0, i))],
        out_specs=[pl.BlockSpec((1, total, D), lambda i: (i, 0, 0)), whole(outs[1])],
        scratch=[pltpu.VMEM((total, D), BF16)],
    )


def attend_kernel(q, k, v, o, lse):
    qm = stack_heads(q[0])
    scores = dot_nt(k[0], qm)
    peak = jnp.max(scores, axis=0, keepdims=True)
    weights = jnp.exp(scores - peak)
    total = jnp.sum(weights, axis=0, keepdims=True)
    both = dot(v[0].T, weights.astype(BF16)) * (1.0 / total)
    o[...] = unstack_t(both).astype(BF16)
    lse[0] = peak + jnp.log(total)


def part_spec(part, rows):
    return pl.BlockSpec((1, rows, 128), lambda i: (part, 0, i))


def attend(chain, joined, own):
    total = joined.shape[1]
    return chain(
        attend_kernel, [sds((own, D), BF16), sds((PAIRS, 1, 2 * own), F32)], [joined] * 3, room(8, total),
        "attend", grid=(PAIRS,),
        in_specs=[part_spec(0, own), part_spec(1, total), part_spec(2, total)],
        out_specs=[
            pl.BlockSpec((own, 128), lambda i: (0, i)),
            pl.BlockSpec((1, 1, 2 * own), lambda i: (i, 0, 0)),
        ],
    )


def qkv_attend_kernel(order, span, even, odd, mod, w, out_h, h1_o, o, lse, h1, joined, sems):
    own = 2 * span
    total = joined.shape[1]
    shift, scale = mod[0:1, 0:D], mod[0:1, D : 2 * D]
    for i, block in enumerate(block_refs(order, even, odd)):
        n, unused = norm(block[0:span, :].astype(F32))
        h1[pl.ds(i * span, span), :] = (n * (1.0 + scale) + shift).astype(BF16)
    h1_o[...] = h1[0:own, :]
    stores = []
    for part in (1, 2, 0):
        piece = w[:, part * D : (part + 1) * D]
        for i in range(total // own):
            rows = slice(i * own, (i + 1) * own)
            value = dot(h1[rows, :], piece)
            joined[part, rows, :] = ((value * SCALE) if part == 0 else value).astype(BF16)
        stores.append(pltpu.make_async_copy(joined.at[part], out_h.at[part], sems.at[part]))
        stores[-1].start()
    for i in range(PAIRS):
        qm = stack_heads(joined[0, 0:own, cols(i)])
        scores = dot_nt(joined[1, :, cols(i)], qm)
        peak = jnp.max(scores, axis=0, keepdims=True)
        weights = jnp.exp(scores - peak)
        sums = jnp.sum(weights, axis=0, keepdims=True)
        both = dot(joined[2, :, cols(i)].T, weights.astype(BF16)) * (1.0 / sums)
        o[:, cols(i)] = unstack_t(both).astype(BF16)
        lse[i] = peak + jnp.log(sums)
    for store in stores:
        store.wait()


def qkv_attend(chain, blocks, order, span, mod, w):
    total, own = len(order) * span, 2 * span
    if total > 1024:
        joined, h1 = qkv(chain, blocks, order, span, mod, w)
        mixed, lse = attend(chain, joined, own)
        return joined, h1, mixed, lse
    outs = [
        sds((3, total, D), BF16), sds((own, D), BF16), sds((own, D), BF16), sds((PAIRS, 1, 2 * own), F32)
    ]
    return chain(
        functools.partial(qkv_attend_kernel, order, span), outs, [blocks[0][0], blocks[2][0], mod, w], 10,
        "qkv_attend", out_specs=[pl.BlockSpec(memory_space=pl.ANY)] + [vmem()] * 3,
        scratch=[
            pltpu.VMEM((total, D), BF16), pltpu.VMEM((3, total, D), BF16), pltpu.SemaphoreType.DMA((3,))
        ],
    )


def two_terms(rows):
    high = rows.astype(BF16).astype(F32)
    return jnp.concatenate([high, rows - high], axis=0).astype(BF16)


def read_stats(block):
    own = block.shape[0] - 16
    held = block[own:, :].astype(F32)

    def line(at):
        rows = held[at : at + 4] + held[at + 4 : at + 8]
        return jnp.concatenate([rows[i : i + 1] for i in range(4)], axis=1)

    return line(0), line(8)


def attend_dq_kernel(q, k, v, do, dq):
    own = do.shape[0] - 16
    qm = stack_heads(q[0])
    dom = stack_heads(do[0:own, :])
    lse, delta = read_stats(do)
    probs = jnp.exp(dot_nt(k[0], qm) - lse)
    grad = dot_nt(v[0], dom)
    ds = (probs * (grad - delta)).astype(BF16)
    dq[...] = (unstack_t(dot(k[0].T, ds)) * SCALE).astype(BF16)


def attend_dq(chain, joined, do):
    own = do.shape[0] - 16
    total = joined.shape[1]
    return chain(
        attend_dq_kernel, [sds((own, D), BF16)], [joined, joined, joined, do], room(5, total),
        "attend_dq", grid=(PAIRS,),
        in_specs=[
            part_spec(0, own), part_spec(1, total), part_spec(2, total),
            pl.BlockSpec((own + 16, 128), lambda i: (0, i)),
        ],
        out_specs=[pl.BlockSpec((own, 128), lambda i: (0, i))],
    )[0]


def attend_dkv_kernel(chunks, dq, q, k, v, *refs):
    do, out = refs[:chunks], refs[-1]
    keys, values = k[0], v[0]
    own = keys.shape[0]
    dk = jnp.zeros((own, 128), F32)
    dv = jnp.zeros((own, 128), F32)
    for i in range(chunks):
        qm = stack_heads(q[0, i * own : (i + 1) * own, :])
        block = do[i][...]
        dom = stack_heads(block[0:own, :])
        lse, delta = read_stats(block)
        probs = jnp.exp(dot_nt(keys, qm) - lse)
        dv += dot(probs.astype(BF16), dom)
        grad = dot_nt(values, dom)
        ds = (probs * (grad - delta)).astype(BF16)
        dk += dot(ds, qm)
    lanes = pl.ds(pl.multiple_of(128 * pl.program_id(0), 128), 128)
    out[0:own, lanes] = dq[...]
    out[own : 2 * own, lanes] = dk.astype(BF16)
    out[2 * own : 3 * own, lanes] = dv.astype(BF16)


def last_kernel(chunks, *refs):
    first, even, w, mod, dx1, away, out, own_o, back_o, part = refs[4 + chunks :]
    attend_dkv_kernel(chunks, *refs[: 4 + chunks], part)
    own = part.shape[0] // 3
    half = part.shape[1]

    @pl.when(pl.program_id(0) == PAIRS // 2 - 1)
    def _():
        out[0 : 3 * own, 0:half] = first[...]
        out[0 : 3 * own, half:] = part[...]
        scale1 = mod[0:1, D : 2 * D]
        dh1 = sum(dot_nt(out[i * own : (i + 1) * own, :], w[:, i * D : (i + 1) * D]) for i in range(3))
        span = own_o.shape[0]
        n1, rstd = norm(start_rows(even.at[0], even.at[even.shape[0] // 2], span))
        sums = jnp.concatenate([colsum(dh1), colsum(n1 * dh1), jnp.zeros((14, D), F32)], axis=0)
        out[3 * own :, :] = sums.astype(BF16)
        grad = dx1[...] + norm_back(n1, rstd, (1.0 + scale1) * dh1)
        own_o[...] = grad[:span]
        back_o[0] = grad[span:].astype(BF16)
        back_o[1] = away[...]


def attend_dkv(chain, dq, joined, do, half, rest=()):
    own = dq.shape[0]
    span = own // 2
    shift = half * (PAIRS // 2)
    pair = lambda part, rows: pl.BlockSpec((1, rows, 128), lambda i: (part, 0, i + shift))
    specs = [
        pl.BlockSpec((own + 16, 128), functools.partial(lambda at, i: (at, i + shift), at)) for unused, at in do
    ]
    outs = [sds((3 * own, D // 2), BF16)]
    kernel = attend_dkv_kernel
    scratch = []
    if rest:
        outs = [sds((3 * own + 16, D), BF16), sds((span, D), F32), sds((2, span, D), BF16)]
        kernel = last_kernel
        scratch = [pltpu.VMEM((3 * own, D // 2), BF16)]
    return chain(
        functools.partial(kernel, len(do)), outs,
        [dq, joined, joined, joined, *(array for array, unused in do), *rest],
        room(4, joined.shape[1]) + (3 if rest else 0), "attend_dkv", grid=(PAIRS // 2,),
        in_specs=[pl.BlockSpec((own, 128), lambda i: (0, i + shift))]
        + [pair(0, joined.shape[1]), pair(1, own), pair(2, own)]
        + specs + [whole(v) for v in rest],
        out_specs=[whole(o) for o in outs], scratch=scratch,
    )


def start_rows(fa, fb, span):
    return jnp.concatenate([fa[0:span, :], fb[0:span, :]], axis=0).astype(F32)


def gelu_both(u):
    c = math.sqrt(2.0 / math.pi)
    square = u * u
    t = jnp.tanh(c * u * (1.0 + 0.044715 * square))
    half = 0.5 * (1.0 + t)
    slope = half + 0.5 * u * (1.0 - t * t) * (c * (1.0 + 3 * 0.044715 * square))
    return u * half, slope


STEPS = FF // D


def fetch(pairs, sems):
    copies = [pltpu.make_async_copy(a, b, sems.at[i]) for i, (a, b) in enumerate(pairs)]
    for copy in copies:
        copy.start()
    return copies


def forward_kernel(span, order, *refs):
    count = len(order)
    info, cap_len, *blocks = refs[: 2 + count]
    (o, h1, mod, ca, cb, up_b, down_b, wo, wq, wkv, wc, up, down,
     big_o, out_o, away_o, cap_o, h2_o, o2_o, x1, dx2_o, attn_o, attn2_o, sums_o, kv2, q2, p2,
     x2, low, dh3, offset) = refs[2 + count :]
    cap_rows = blocks[0].shape[0] - span

    big_o[2 * STEPS + 2] = o[...]
    big_o[2 * STEPS + 3] = h1[...]

    gate1, shift2, scale2, gate2, shift3, scale3, gate3 = (
        mod[0:1, i * D : (i + 1) * D] for i in range(2, 9)
    )

    length = cap_len[2 * info[0] + info[2]]
    for i, k in enumerate(order):
        here = slice(i * cap_rows, (i + 1) * cap_rows)
        cap_o[here, :] = blocks[i][span:, :]
        first = jnp.bitwise_xor(info[1], k) * cap_rows
        token = first + lax.broadcasted_iota(jnp.int32, (cap_rows, 128), 0)
        offset[here, :] = jnp.where(token < length, 0.0, NEGATIVE)
    dy = jnp.concatenate([ca[...], cb[...]], axis=0).astype(F32)
    big_o[2 * STEPS + 1] = (gate3 * dy).astype(BF16)

    attn = dot(o[...], wo[...])
    x1[...] = start_rows(blocks[0], blocks[1], span) + gate1 * attn
    attn_o[...] = attn.astype(BF16)
    n2, unused = norm(x1[...])
    h2 = (n2 * (1.0 + scale2) + shift2).astype(BF16)
    h2_o[...] = h2
    kv2[...] = dot(cap_o[...], wkv[...]).astype(BF16)
    q2[...] = (dot(h2, wq[...]) * SCALE).astype(BF16)
    for i in range(PAIRS):
        qm = stack_heads(q2[:, cols(i)])
        scores = dot_nt(kv2[:, cols(i)], qm) + offset[:, 0:1]
        peak = jnp.max(scores, axis=0, keepdims=True)
        weights = jnp.exp(scores - peak)
        probs = (weights * (1.0 / jnp.sum(weights, axis=0, keepdims=True))).astype(BF16)
        p2[i] = probs
        both = dot(kv2[:, D + i * 128 : D + (i + 1) * 128].T, probs)
        o2_o[:, cols(i)] = unstack_t(both).astype(BF16)
    attn2 = dot(o2_o[...], wc[...])
    x2[...] = x1[...] + gate2 * attn2
    attn2_o[...] = attn2.astype(BF16)

    n3, unused = norm(x2[...])
    big_o[2 * STEPS] = (n3 * (1.0 + scale3) + shift3).astype(BF16)
    for i in range(STEPS):
        piece = slice(i * D, (i + 1) * D)
        acted, slope = gelu_both(dot(big_o[2 * STEPS], up[:, piece]) + up_b[:, piece].astype(F32))
        acted = acted.astype(BF16)
        big_o[i] = acted
        dupper = (slope * dot_nt(big_o[2 * STEPS + 1], down[piece, :])).astype(BF16)
        big_o[STEPS + i] = dupper
        sums_o[8 + i : 9 + i, :] = colsum(dupper.astype(F32))
        if i:
            low[...] += dot(acted, down[piece, :])
            dh3[...] += dot_nt(dupper, up[:, piece])
        else:
            low[...] = dot(acted, down[piece, :])
            dh3[...] = dot_nt(dupper, up[:, piece])
    lower = low[...] + down_b[...].astype(F32)
    value = x2[...]
    result = (value + gate3 * lower).astype(BF16)
    out_o[...] = result[:span]
    away_o[...] = result[span:]
    dy = jnp.concatenate([ca[...], cb[...]], axis=0).astype(F32)
    n3, rstd = norm(value)
    back = dh3[...]
    sums_o[0:4, :] = jnp.zeros((4, D), F32)
    sums_o[4:5, :] = colsum(back)
    sums_o[5:6, :] = colsum(n3 * back)
    sums_o[6:7, :] = colsum(lower * dy)
    sums_o[7:8, :] = colsum(big_o[2 * STEPS + 1].astype(F32))
    sums_o[12:16, :] = jnp.zeros((4, D), F32)
    dx2_o[...] = dy + norm_back(n3, rstd, (1.0 + scale3) * back)


def backward_kernel(dx2_r, mod, attn2, kv2, q2, p2, x1, attn, o, lse, h2, o2, sums3,
                    wc, wq, wo, fac_o, dx1_o, do_o, sums_o):
    own = o.shape[0]
    slot = lambda i: slice(i * own, (i + 1) * own)
    gate1, scale2, gate2 = (mod[0:1, i * D : (i + 1) * D] for i in (2, 4, 5))
    sums_o[...] = sums3[...]
    fac_o[slot(0), :] = h2[...]
    fac_o[slot(2), :] = o2[...]
    dx2 = dx2_r[...]
    sums_o[3:4, :] = colsum(attn2[...].astype(F32) * dx2)
    da2 = (gate2 * dx2).astype(BF16)
    fac_o[slot(3), :] = da2
    do2 = dot_nt(da2, wc[...]).astype(BF16)
    for i in range(PAIRS):
        qm = stack_heads(q2[:, cols(i)])
        dom = stack_heads(do2[:, cols(i)])
        keys, values = kv2[:, cols(i)], kv2[:, D + i * 128 : D + (i + 1) * 128]
        probs = p2[i]
        fac_o[slot(5), cols(i)] = dot(probs, dom).astype(BF16)
        probs = probs.astype(F32)
        grad = dot_nt(values, dom)
        ds = (probs * (grad - colsum(probs * grad))).astype(BF16)
        fac_o[slot(1), cols(i)] = (unstack_t(dot(keys.T, ds)) * SCALE).astype(BF16)
        fac_o[slot(4), cols(i)] = dot(ds, qm).astype(BF16)
    dh2 = dot_nt(fac_o[slot(1), :], wq[...])
    n2, rstd = norm(x1[...])
    sums_o[1:2, :] = colsum(dh2)
    sums_o[2:3, :] = colsum(n2 * dh2)
    dx1 = dx2 + norm_back(n2, rstd, (1.0 + scale2) * dh2)
    dx1_o[...] = dx1
    sums_o[0:1, :] = colsum(attn[...].astype(F32) * dx1)

    da = (gate1 * dx1).astype(BF16)
    fac_o[slot(6), :] = da
    do = dot_nt(da, wo[...]).astype(BF16)
    do_o[0:own, :] = do
    both = do.astype(F32) * o[...].astype(F32)
    for i in range(PAIRS):
        t = both[:, cols(i)].T
        delta = [colsum(t[:HEAD]), colsum(t[HEAD:])]
        delta = [d[:, 128 * j : 128 * (j + 1)] for d in delta for j in range(own // 128)]
        sums = [lse[i][:, 128 * j : 128 * (j + 1)] for j in range(2 * own // 128)]
        held = [two_terms(jnp.concatenate(rows, axis=0)) for rows in (sums, delta)]
        do_o[own:, cols(i)] = jnp.concatenate(held, axis=0)
    fac_o[7 * own : 7 * own + 16, :] = sums_o[...].astype(BF16)
    at = do_place(own) * (own + 16)
    fac_o[7 * own + 16 : at, :] = jnp.zeros((at - 7 * own - 16, D), BF16)
    fac_o[at:, :] = do_o[...]


def forward(chain, info, cap_len, blocks, order, span, o, h1, mod, ca, cb, up_b, down_b, *weights):
    own = 2 * span
    cap_total = len(blocks) * (blocks[0][0].shape[1] - span)
    thin, wide = sds((own, D), BF16), sds((own, D), F32)
    half = sds((span, D), BF16)
    outs = [
        sds((2 * STEPS + 4, own, D), BF16), half, half, sds((cap_total, D), BF16), thin, thin, wide, wide,
        thin, thin, sds((16, D), F32), sds((cap_total, 2 * D), BF16), thin,
        sds((PAIRS, cap_total, 2 * own), BF16),
    ]
    here = [blocks[0][0], blocks[2][0], o, h1, mod, ca, cb, up_b, down_b]
    square = pltpu.VMEM((D, D), BF16)

    def kernel(info, cap_len, even, odd, *refs):
        forward_kernel(span, order, info, cap_len, *block_refs(order, even, odd), *refs)

    return chain(
        kernel, outs, [info, cap_len, *here, *weights], FWD, "forward",
        in_specs=[smem()] * 2 + [vmem()] * (len(here) + len(weights)),
        scratch=[pltpu.VMEM((own, D), F32)] * 3
        + [pltpu.VMEM((cap_total, 128), F32)],
    )


def do_place(own):
    return -(-(7 * own + 16) // (own + 16))


def backward(chain, here, weights):
    own = here[0].shape[0]
    outs = [
        sds(((do_place(own) + 1) * (own + 16), D), BF16), sds((own, D), F32),
        sds((own + 16, D), BF16),
        sds((16, D), F32),
    ]
    square = pltpu.VMEM((D, D), BF16)
    return chain(
        backward_kernel, outs, [*here, *weights], BWD, "backward",
    )


def pick_rows(info, x):
    source = lax.broadcasted_iota(jnp.int32, (D, D // 2), 0)
    column = lax.broadcasted_iota(jnp.int32, (D, D // 2), 1)
    block = sum((column >= 96 * i).astype(jnp.int32) for i in (1, 2, 3))
    wanted = 96 * jnp.bitwise_xor(info[1], 2 * block) + column - 96 * block
    choose = (source == wanted).astype(F32).astype(BF16)
    return dot(x, choose).astype(BF16)


def emit(first, info, tiles, blocks, send_o, keep_o):
    place = {True: 0, False: 0}
    for r in range(4):
        sent = bool(r & first)
        (send_o if sent else keep_o)[place[sent]] = tiles[jnp.bitwise_xor(info[0], r), blocks]
        place[sent] += 1


def down_grad_kernel(info, fac, fac_p, send_o, keep_o, tiles):
    for e in range(4):
        owner = jnp.bitwise_xor(info[1], 2 * e)
        half = pl.multiple_of(lax.rem(owner, 2) * 384, 128)
        where = (lax.div(owner, 2), slice(None), pl.ds(half, 384))
        grad = dot_tn(fac[where], fac[2 * STEPS + 1]) + dot_tn(fac_p[where], fac_p[9])
        for q in range(4):
            tiles[q, e] = grad[96 * q : 96 * (q + 1)].astype(BF16)
    emit(1, info, tiles, slice(0, 4), send_o, keep_o)


def up_grad_kernel(info, fac, fac_p, send_o, keep_o, tiles):
    x, xp = pick_rows(info, fac[8]), pick_rows(info, fac_p[8])
    for q in range(4):
        grad = dot_tn(x, fac[4 + q]) + dot_tn(xp, fac_p[4 + q])
        for e in range(4):
            tiles[q, e] = grad[96 * e : 96 * (e + 1)].astype(BF16)
    emit(2, info, tiles, slice(0, 4), send_o, keep_o)


def put(tiles, q, grad):
    for e in range(4):
        tiles[q, e] = grad[96 * e : 96 * (e + 1)].astype(BF16)


def emit_both(info, tiles, sx, kx, sy, ky):
    emit(1, info, tiles, slice(0, 2), sx, kx)
    emit(2, info, tiles, slice(2, 4), sy, ky)


def cross_grad_kernel(own, info, cap, fac, fac_p, wkv, sx, kx, sy, ky, dcap_o, tiles):
    def slot(ref, i):
        return ref[i * own : (i + 1) * own, :]

    def pair(x, y):
        left, left_p = pick_rows(info, slot(fac, x)), pick_rows(info, slot(fac_p, x))
        return dot_tn(left, slot(fac, y)) + dot_tn(left_p, slot(fac_p, y))

    put(tiles, 0, pair(0, 1))
    x = pick_rows(info, cap[...])
    rows = cap.shape[0] // 4
    xp = jnp.concatenate([x[rows * i : rows * (i + 1)] for i in (1, 0, 3, 2)], axis=0)
    for q in (1, 2):
        put(tiles, q, dot_tn(x, slot(fac, q + 3)) + dot_tn(xp, slot(fac_p, q + 3)))
    put(tiles, 3, pair(2, 3))
    emit_both(info, tiles, sx, kx, sy, ky)

    rows = cap.shape[0] // 8

    def even(x):
        places = [rows * order_place(k) for k in range(8)]
        parts = [
            total(slot(fac, x)[places[k] : places[k] + rows], slot(fac_p, x)[places[k + 1] : places[k + 1] + rows])
            for k in (0, 2, 4, 6)
        ]
        return jnp.concatenate(parts, axis=0)

    dcap_o[...] = (dot_nt(even(4), wkv[:, 0:D]) + dot_nt(even(5), wkv[:, D : 2 * D])).astype(BF16)


def attn_grad_kernel(info, da, o, h1, da_p, o_p, h1_p, dqkv, dqkv_p, sx, kx, sy, ky, tiles):
    own = da.shape[0]
    x, xp = pick_rows(info, h1[0]), pick_rows(info, h1_p[0])
    for i in range(3):
        slot = slice(i * own, (i + 1) * own)
        put(tiles, i, dot_tn(x, dqkv[slot, :]) + dot_tn(xp, dqkv_p[slot, :]))
    x, xp = pick_rows(info, o[0]), pick_rows(info, o_p[0])
    put(tiles, 3, dot_tn(x, da[...]) + dot_tn(xp, da_p[...]))
    emit_both(info, tiles, sx, kx, sy, ky)


def grad_call(chain, kernel, info, args, name, shape, outs, in_specs=None):
    return chain(
        kernel, [sds(o, BF16) for o in outs], [info, *args], 5, name, grid=(1,) if in_specs else None,
        in_specs=[smem()] + (in_specs or [vmem()] * len(args)),
        scratch=[pltpu.VMEM(shape, BF16)],
    )


def total(*refs):
    return sum(r.astype(F32) for r in refs).astype(BF16)


def add_first_kernel(keep, recv, keep_o, send_o):
    keep_o[...] = total(keep[0], recv[0])
    send_o[...] = total(keep[1], recv[1])


def add_both_kernel(kx, rx, ky, ry, kx_o, sx_o, ky_o, sy_o):
    add_first_kernel(kx, rx, kx_o, sx_o)
    add_first_kernel(ky, ry, ky_o, sy_o)


def sum_rows(early, early_p, late, late_p):
    first = late[0:2, :].astype(F32) + late_p[0:2, :].astype(F32)
    both = early[0:12, :].astype(F32) + early_p[0:12, :].astype(F32)
    return jnp.concatenate([first, both, jnp.zeros((2, D), F32)], axis=0).astype(BF16)


def mlp_second_kernel(ka, ra, kb, rb, fac, fac_p, late, late_p, keep_o, send_o):
    for g, (keep, recv) in enumerate(((ka, ra), (kb, rb))):
        for e in range(4):
            (send_o if e % 2 else keep_o)[e // 2, 96 * g : 96 * (g + 1), :] = total(keep[e], recv[e])
    rows = sum_rows(fac, fac_p, late, late_p)
    for ref in (keep_o, send_o):
        for i in range(2):
            ref[i, 192:208, :] = rows


def mlp_third_kernel(keep, recv, keep_o, send_o):
    keep_o[...] = total(keep[0], recv[0])
    send_o[0:192, :] = total(keep[1, 0:192, :], recv[1, 0:192, :])
    send_o[192:208, :] = total(keep[0, 192:208, :], recv[0, 192:208, :])


def mlp_fourth_kernel(keep, recv, out):
    out[0:192, :] = total(keep[0:192, :], recv[0:192, :])
    out[192:208, :] = keep[192:208, :]
    out[208:224, :] = recv[192:208, :]


def order_place(k):
    return 2 * (k % 4) + k // 4


def second_kernel(kx, rx, ky, ry, *refs):
    caption, (keep_o, send_o) = refs[:-2], refs[-2:]
    for e in range(4):
        out = send_o if e % 2 else keep_o
        keep, recv = ((kx, rx), (ky, ry))[e // 2]
        out[e // 2, 0:96, :] = total(keep[e % 2], recv[e % 2])
        if caption:
            rows = caption[0].shape[0] // 4
            out[e // 2, 96:, :] = caption[0][rows * e : rows * (e + 1), :]


def third_kernel(keep, recv, keep_o, send_o):
    keep_o[...] = total(keep[0], recv[0])
    send_o[...] = total(keep[1], recv[1])


def fourth_kernel(keep, recv, c_keep, c_recv, out, same_o, away_o):
    out[0:96, :] = total(keep[...], recv[...])
    out[96:, :] = total(c_keep[0:96, :], c_recv[0:96, :])
    same_o[...] = c_keep[96:, :].astype(F32)
    away_o[...] = c_recv[96:, :].astype(F32)


def swap(x, axis, size, k):
    return lax.ppermute(x, axis, [(i, i ^ k) for i in range(size)])


def over_x(x):
    return swap(x, "band", 4, 1)


def over_y(x):
    return swap(x, "band", 4, 2)


def to_band(x):
    return [x] + [swap(x, "band", 4, t) for t in (1, 2, 3)]


def mlp_finish_kernel(info, t0, t1, t2, t3, down_o, up_o):
    for r, tile in enumerate((t0, t1, t2, t3)):
        q = jnp.bitwise_xor(info[0], r)
        down_o[pl.ds(pl.multiple_of(96 * q, 96), 96), :] = tile[0:96, :].astype(F32)
        up_o[:, pl.ds(pl.multiple_of(D * q, D), D)] = tile[96:192, :].astype(F32)


def last_finish_kernel(info, t0, t1, t2, t3, in_o, out_o, cq_o, ckv_o, co_o, tiles):
    for r, tile in enumerate((t0, t1, t2, t3)):
        tiles[jnp.bitwise_xor(info[0], r)] = tile[...]
    for i in range(3):
        in_o[:, i * D : (i + 1) * D] = tiles[i, 0:96, :].astype(F32)
    out_o[...] = tiles[3, 0:96, :].astype(F32)
    cq_o[...] = tiles[0, 96:, :].astype(F32)
    ckv_o[:, 0:D] = tiles[1, 96:, :].astype(F32)
    ckv_o[:, D:] = tiles[2, 96:, :].astype(F32)
    co_o[...] = tiles[3, 96:, :].astype(F32)


def finish(chain, kernel, info, tiles, widths, name, scratch=(), held=()):
    outs = [sds(w, F32) for w in widths] + [sds(h.shape, h.dtype) for h in held]
    tiles = [*tiles, *held]
    return chain(
        kernel, outs, [info, *tiles], 5, name, grid=(1,), in_specs=[smem()] + [whole(t) for t in tiles],
        out_specs=[whole(o) for o in outs], scratch=scratch,
    )


def plain_reduce(x, y, owners):
    grad = lax.psum_scatter(dot_tn(x, y).astype(BF16), "seq", scatter_dimension=0, tiled=True)
    return lax.psum(grad, "band").astype(F32)


def on_device(bands, seqs, frames, caption, timesteps, cap_len, attn_in, attn_out, cross_query,
              cross_keyval, cross_out, mlp_up, up_bias, mlp_down, down_bias, ada_weight, ada_bias,
              time_first, first_bias, time_second, second_bias, cotangent):
    span = frames.shape[1]
    own = 2 * span
    cap_rows = caption.shape[1]
    items = timesteps.shape[0]
    halves = seqs // 2
    band = lax.axis_index("band")
    seq = lax.axis_index("seq")
    half = (seq >= halves).astype(jnp.int32)
    item = 2 * band + half
    info = jnp.stack([band, seq, half]).astype(jnp.int32)

    chain = Chain()

    order = [k for i in range(halves) for k in (i, i + halves)]
    def item_rows(which):
        return jnp.concatenate(
            [lax.dynamic_index_in_dim(x, which, keepdims=False) for x in (frames, caption)]
        )

    other, same = item_rows(1 - half), item_rows(half)
    even = [same] + [swap(same if k < halves else other, "seq", seqs, k) for k in range(2, seqs, 2)]

    steps = jnp.take(timesteps, jnp.bitwise_xor(jnp.arange(items), item))
    width = time_first.shape[0] // 2
    freq = jnp.exp(-math.log(10000.0) * jnp.arange(width, dtype=F32) / width)
    angle = steps.astype(F32)[:, None] * freq[None, :]
    embed = jnp.concatenate([jnp.cos(angle), jnp.sin(angle)], axis=1)
    row = lambda v: v.reshape(1, -1)
    pre_cond, mod = modulation(
        chain, embed, time_first, row(first_bias), time_second, row(second_bias), ada_weight, row(ada_bias)
    )
    cot_own, cot_other = pick(chain, info, cotangent, early=[mlp_up, mlp_down])
    cot_other = swap(cot_other, "seq", seqs, halves)

    even = stack(chain, even, "blocks")
    odd = swap(even, "seq", seqs, 1)
    blocks = [(odd if k % 2 else even, k // 2) for k in order]
    joined, h1, mixed, lse = qkv_attend(chain, blocks, order, span, mod, attn_in)

    cap_total = seqs * cap_rows
    (big, out, out_back, cap_all, h2, o2, x1, dx2, attn, attn2, sums3, kv2, q2, p2) = forward(
        chain, info, cap_len, blocks, order, span, mixed, h1, mod, cot_own, cot_other, row(up_bias),
        row(down_bias), attn_out, cross_query, cross_keyval, cross_out, mlp_up, mlp_down,
    )
    fast = bands == 4 and seqs == 8
    if fast:
        big_p = swap(big, "seq", seqs, 1)
    fac, dx1, do, early = backward(
        chain, [dx2, mod, attn2, kv2, q2, p2, x1, attn, mixed, lse, h2, o2, sums3],
        [cross_out, cross_query, attn_out],
    )
    if fast:
        fac_p = swap(fac, "seq", seqs, 1)
    got = {k: (swap(do, "seq", seqs, k), 0) for k in range(2 if fast else 1, halves)}
    got[0] = (do, 0)
    if fast:
        got[1] = (fac_p, do_place(own))
        whole_tiles, pieces, halved = (4, 4, 96, D), [(2, 4, 96, D)] * 2, [(2, 2, 96, D)] * 4
        args = [big, big_p]
        sa, ka = grad_call(chain, down_grad_kernel, info, args, "down_grad", whole_tiles, pieces)
        ra = over_x(sa)
        sb, kb = grad_call(chain, up_grad_kernel, info, args, "up_grad", whole_tiles, pieces)
        rb = over_y(sb)
        cx, ckx, cy, cky, dcap = grad_call(
            chain, functools.partial(cross_grad_kernel, own), info, [cap_all, fac, fac_p, cross_keyval],
            "cross_grad", whole_tiles, halved + [(cap_total // 2, D)],
        )
        crx, cry = over_x(cx), over_y(cy)
    dq = attend_dq(chain, joined, do)
    do_blocks = [got[k] for k in range(halves)]
    dkv_first = attend_dkv(chain, dq, joined, do_blocks, 0)[0]
    dqkv, grad_own, back = attend_dkv(
        chain, dq, joined, do_blocks, 1, [dkv_first, even, attn_in, mod, dx1, out_back]
    )
    back = swap(back, "seq", seqs, halves)
    if fast:
        dqkv_p = swap(dqkv, "seq", seqs, 1)
        half, quarter, tile = sds((4, 96, D), BF16), sds((2, 96, D), BF16), sds((96, D), BF16)
        ka, sa, kb, sb = chain(add_both_kernel, [half] * 4, [ka, ra, kb, rb], 2, "mlp_add1")
        ra, rb = over_y(sa), over_x(sb)
        slots = [pl.BlockSpec((own, D), lambda *i: (6, 0))] + [
            pl.BlockSpec((1, own, D), functools.partial(lambda at, *i: (at, 0, 0), at))
            for at in (2 * STEPS + 2, 2 * STEPS + 3)
        ]
        tx, tkx, ty, tky = grad_call(
            chain, attn_grad_kernel, info, [fac, big, big, fac_p, big_p, big_p, dqkv, dqkv_p], "attn_grad",
            whole_tiles, halved, in_specs=slots * 2 + [whole(dqkv)] * 2,
        )
        trx, try_ = over_x(tx), over_y(ty)
        sum_at, late_at = 7 * own // 16, 3 * own // 16
        sum_spec = pl.BlockSpec((16, D), lambda *i: (sum_at, 0))
        late_spec = pl.BlockSpec((16, D), lambda *i: (late_at, 0))
        keep, send = chain(
            mlp_second_kernel, [sds((2, 208, D), BF16)] * 2, [ka, ra, kb, rb, fac, fac_p, dqkv, dqkv_p], 4,
            "mlp_add2", grid=(1,), in_specs=[vmem()] * 4 + [sum_spec] * 2 + [late_spec] * 2,
        )
        recv = swap(send, "seq", seqs, 2)
        grad_frames, out = place(
            chain, info, [(grad_own, (back, 0)), (out, (back, 1))], [F32, BF16], "place_frames"
        )
        ckx, cx, cky, cy = chain(add_both_kernel, [quarter] * 4, [ckx, crx, cky, cry], 4, "cross_add1")
        crx, cry = over_y(cx), over_x(cy)
        tkx, tx, tky, ty = chain(add_both_kernel, [quarter] * 4, [tkx, trx, tky, try_], 4, "attn_add1")
        trx, try_ = over_y(tx), over_x(ty)
        keep, send = chain(mlp_third_kernel, [sds((208, D), BF16)] * 2, [keep, recv], 4, "mlp_z1")
        recv = swap(send, "seq", seqs, 4)
        rows = 96 + cap_rows
        c_keep, c_send = chain(
            second_kernel, [sds((2, rows, D), BF16)] * 2, [ckx, crx, cky, cry, dcap], 4, "cross_add2",
        )
        c_recv = swap(c_send, "seq", seqs, 2)
        t_keep, t_send = chain(second_kernel, [quarter] * 2, [tkx, trx, tky, try_], 4, "attn_add2")
        t_recv = swap(t_send, "seq", seqs, 2)
        a_all = to_band(chain(mlp_fourth_kernel, [sds((224, D), BF16)], [keep, recv], 4, "mlp_z2")[0])
        c_keep, c_send = chain(third_kernel, [sds((rows, D), BF16)] * 2, [c_keep, c_recv], 4, "cross_z1")
        c_recv = swap(c_send, "seq", seqs, 4)
        t_keep, t_send = chain(third_kernel, [tile] * 2, [t_keep, t_recv], 4, "attn_z1")
        t_recv = swap(t_send, "seq", seqs, 4)
        t_done, cap_same, cap_away = chain(
            fourth_kernel, [sds((192, D), BF16)] + [sds((cap_rows, D), F32)] * 2,
            [t_keep, t_recv, c_keep, c_recv], 4, "other_z2",
        )
        t_all = to_band(t_done)
        g_down, g_up = finish(chain, mlp_finish_kernel, info, a_all, [(384, D), (96, FF)], "mlp_finish")
        grad_caption = place(chain, info, [(cap_same, cap_away)], [F32], "place_caption")[0]
        sums = a_all
    else:
        grad_frames, out = place(
            chain, info, [(grad_own, (back, 0)), (out, (back, 1))], [F32, BF16], "place_frames"
        )
        dkv2 = jnp.concatenate([fac[4 * own : 4 * own + cap_total], fac[5 * own : 5 * own + cap_total]], axis=1)
        dcap = dot_nt(dkv2, cross_keyval).astype(BF16).reshape(seqs, cap_rows, D)
        place_of = jnp.asarray([order.index(k) for k in range(seqs)])
        dcap = dcap[place_of[jnp.bitwise_xor(seq, jnp.arange(seqs))]].reshape(cap_total, D)
        dcap = jnp.where(half == 0, jnp.stack([dcap, 0 * dcap]), jnp.stack([0 * dcap, dcap]))
        grad_caption = lax.psum_scatter(dcap, "seq", scatter_dimension=1, tiled=True).astype(F32)
        rows = jnp.concatenate([dqkv[3 * own : 3 * own + 2].astype(F32), early[0:12], jnp.zeros((2, D), F32)])
        for k in range(1, halves):
            if k & (k - 1) == 0:
                rows = rows + swap(rows, "seq", seqs, k)
        rows = jnp.concatenate([rows, swap(rows, "seq", seqs, halves)]).astype(BF16)
        sums = [rows] + [swap(rows, "band", bands, t) for t in range(1, bands)]

    g_ada, gb_ada, g_t2, gb_t2, g_t1, gb_t1, gb_down, gb_up = mod_back(
        chain, info, sums, ada_weight, pre_cond, embed, time_second, seqs
    )

    if fast:
        g_in, g_out, g_cq, g_ckv, g_co = finish(
            chain, last_finish_kernel, info, t_all, [(96, 3 * D), (96, D), (96, D), (96, 2 * D), (96, D)],
            "last_finish", [pltpu.VMEM((4, 192, D), BF16)],
        )
    else:
        slot = lambda i: fac[i * own : (i + 1) * own]
        acted = jnp.concatenate([big[i] for i in range(FF // D)], axis=1)
        dupper = jnp.concatenate([big[FF // D + i] for i in range(FF // D)], axis=1)
        g_down = plain_reduce(acted, big[2 * STEPS + 1], seqs)
        g_up = plain_reduce(big[2 * STEPS], dupper, seqs)
        g_cq = plain_reduce(slot(0), slot(1), seqs)
        g_ckv = plain_reduce(cap_all, jnp.concatenate([slot(4), slot(5)], axis=1), seqs)
        g_co = plain_reduce(slot(2), slot(3), seqs)
        g_out = plain_reduce(mixed, slot(6), seqs)
        g_in = plain_reduce(h1, jnp.concatenate([dqkv[i * own : (i + 1) * own] for i in range(3)], axis=1), seqs)

    flat = lambda v: v.reshape(-1)
    return (
        out, grad_frames, grad_caption, g_in, g_out, g_cq, g_ckv, g_co, g_up, flat(gb_up), g_down,
        flat(gb_down), g_ada, flat(gb_ada), g_t1, flat(gb_t1), g_t2, flat(gb_t2),
    )


def solution(mesh):
    split = P("band", "seq", None)
    rows, flat = P("seq", None), P("seq")
    return jax.shard_map(
        functools.partial(on_device, mesh.shape["band"], mesh.shape["seq"]),
        mesh=mesh,
        in_specs=(split, split) + (P(),) * 17 + (split,),
        out_specs=(split, split, split, rows, rows, rows, rows, rows, rows, flat, rows, flat, rows, flat,
                   rows, flat, rows, flat),
        check_vma=False,
    )
```

```python
import functools
import math

import jax
import jax.numpy as jnp
from jax import lax
from jax.experimental import pallas as pl
from jax.experimental.pallas import tpu as pltpu
from jax.sharding import PartitionSpec as P

D = 768
HEAD = 64
PAIRS = 6
FF = 3072
EPSILON = 1e-06
NEGATIVE = -1e30
SCALE = 0.125
F32 = jnp.float32
BF16 = jnp.bfloat16
MIB = 1 << 20
MODMIB = 4
COST = 1000000
FWD = 9
BWD = 6


def dot(a, b):
    return jnp.dot(a, b, preferred_element_type=F32)


def dot_nt(a, b):
    return lax.dot_general(a, b, (((1,), (1,)), ((), ())), preferred_element_type=F32)


def dot_tn(a, b):
    return lax.dot_general(a, b, (((0,), (0,)), ((), ())), preferred_element_type=F32)


def split_dot(x, w, contract=0):
    high = x.astype(BF16).astype(F32)
    both = jnp.concatenate([high, x - high], axis=0).astype(BF16)
    out = lax.dot_general(
        both, w, (((1,), (contract,)), ((), ())), preferred_element_type=F32
    )
    return out[: x.shape[0]] + out[x.shape[0] :]


def silu(v):
    return v * (1.0 / (1.0 + jnp.exp(-v)))


def silu_grad(v):
    s = 1.0 / (1.0 + jnp.exp(-v))
    return s * (1.0 + v * (1.0 - s))


def norm(v):
    mean = jnp.mean(v, axis=-1, keepdims=True)
    centred = v - mean
    spread = jnp.mean(centred * centred, axis=-1, keepdims=True)
    rstd = lax.rsqrt(spread + EPSILON)
    return centred * rstd, rstd


def norm_back(n, rstd, w):
    return (
        w - jnp.mean(w, axis=-1, keepdims=True) - n * jnp.mean(w * n, axis=-1, keepdims=True)
    ) * rstd


def colsum(v):
    return jnp.sum(v, axis=0, keepdims=True)


def cols(i):
    return slice(i * 128, (i + 1) * 128)


def head_masks():
    lane = lax.broadcasted_iota(jnp.int32, (1, 128), 1)
    first = (lane < HEAD).astype(F32)
    return first.astype(BF16), (1.0 - first).astype(BF16)


def stack_heads(block):
    first, second = head_masks()
    return jnp.concatenate([block * first, block * second], axis=0)


def unstack_t(both):
    rows = both.shape[1] // 2
    pair = jnp.concatenate([both[:HEAD, :rows], both[HEAD:, rows:]], axis=0)
    return pair.T


def sds(shape, dtype):
    return jax.ShapeDtypeStruct(shape, dtype)


def vmem():
    return pl.BlockSpec(memory_space=pltpu.VMEM)


def smem():
    return pl.BlockSpec(memory_space=pltpu.SMEM)


def whole(a):
    return pl.BlockSpec(a.shape, lambda *i: (0,) * len(a.shape))


class Chain:
    def __init__(self):
        self.token = None

    def __call__(self, kernel, outs, args, mib, name, grid=None, in_specs=None, out_specs=None, scratch=(), early=()):
        outs = list(outs)
        in_specs = list(in_specs or [vmem()] * len(args))
        out_specs = list(out_specs or [vmem()] * len(outs))
        count = len(args)
        body = kernel
        unread = [*early] + ([] if self.token is None else [self.token])
        if unread:
            args = [*args, *unread]
            in_specs += [vmem()] * len(early) + [pl.BlockSpec(memory_space=pl.ANY)] * (len(unread) - len(early))
            body = lambda *refs: kernel(*refs[:count], *refs[count + len(unread) :])
        results = pl.pallas_call(
            body,
            **({} if grid is None else {"grid": grid}),
            out_shape=outs,
            in_specs=in_specs,
            out_specs=out_specs,
            scratch_shapes=list(scratch),
            compiler_params=pltpu.CompilerParams(vmem_limit_bytes=mib * MIB),
            cost_estimate=pl.CostEstimate(flops=1000000000, bytes_accessed=COST, transcendentals=0),
            name=name,
        )(*args)
        self.token = min(results, key=lambda r: r.size * r.dtype.itemsize)
        return results

    def after(self, x):
        self.token = x


def room(mib, frames):
    return min(56, mib * max(1, frames // 1024))


def pick_kernel(info, *refs):
    half = info[2]
    parts, (mine_o, theirs_o, sems) = refs[:-3], refs[-3:]
    copies = []
    at = 0
    for x in parts:
        rows = pl.ds(at, x.shape[1])
        for source, out in ((half, mine_o), (1 - half, theirs_o)):
            copies.append(pltpu.make_async_copy(x.at[source], out.at[rows], sems.at[len(copies)]))
        at += x.shape[1]
    for copy in copies:
        copy.start()
    for copy in copies:
        copy.wait()


def pick(chain, info, *parts, early=()):
    out = sds((sum(x.shape[1] for x in parts), D), BF16)
    anywhere = pl.BlockSpec(memory_space=pl.ANY)
    return chain(
        pick_kernel, [out, out], [info, *parts], 4, "pick", in_specs=[smem()] + [anywhere] * len(parts),
        out_specs=[anywhere] * 2, scratch=[pltpu.SemaphoreType.DMA((2 * len(parts),))],
        early=early,
    )


def stack_kernel(*refs):
    for i, ref in enumerate(refs[:-1]):
        refs[-1][i] = ref[...]


def stack(chain, arrays, name):
    out = sds((len(arrays),) + arrays[0].shape, arrays[0].dtype)
    return chain(stack_kernel, [out], arrays, 4, name)[0]


def place_kernel(info, *refs):
    count = len(refs) // 3
    for i in range(count):
        kept, received, out = refs[2 * i], refs[2 * i + 1], refs[2 * count + i]
        out[info[2]] = kept[...].astype(out.dtype)
        out[1 - info[2]] = received[...].reshape(kept.shape).astype(out.dtype)


def place(chain, info, pairs, dtypes, name):
    args, specs = [info], [smem()]
    for kept, received in pairs:
        args.append(kept)
        specs.append(whole(kept))
        if isinstance(received, tuple):
            args.append(received[0])
            specs.append(pl.BlockSpec((1,) + kept.shape, functools.partial(lambda at, i: (at, 0, 0), received[1])))
        else:
            args.append(received)
            specs.append(whole(received))
    outs = [sds((2,) + kept.shape, dtype) for (kept, unused), dtype in zip(pairs, dtypes)]
    return chain(
        place_kernel, outs, args, 4, name, grid=(1,), in_specs=specs, out_specs=[whole(o) for o in outs]
    )


def mod_kernel(embed, t1, b1, t2, b2, w, b, both_o, mod_o, act):
    @pl.when(pl.program_id(0) == 0)
    def _():
        pre = split_dot(embed[...], t1[...]) + b1[...].astype(F32)
        cond = split_dot(silu(pre), t2[...]) + b2[...].astype(F32)
        both_o[0] = pre
        both_o[1] = cond
        act[...] = silu(cond)

    mod_o[...] = split_dot(act[...], w[...]) + b[...].astype(F32)


def modulation(chain, embed, t1, b1, t2, b2, w, b):
    items = embed.shape[0]
    outs = [sds((2, items, D), F32), sds((items, 9 * D), F32)]
    return chain(
        mod_kernel, outs, [embed, t1, b1, t2, b2, w, b], MODMIB, "modulation", grid=(9,),
        in_specs=[whole(v) for v in (embed, t1, b1, t2, b2)]
        + [pl.BlockSpec((D, D), lambda i: (0, i)), pl.BlockSpec((1, D), lambda i: (0, i))],
        out_specs=[whole(outs[0]), pl.BlockSpec((items, D), lambda i: (0, i))],
        scratch=[pltpu.VMEM((items, D), F32)],
    )


def outer_sum(left_t, right):
    lh = left_t.astype(BF16)
    ll = (left_t - lh.astype(F32)).astype(BF16)
    rh = right.astype(BF16)
    rl = (right - rh.astype(F32)).astype(BF16)
    return dot(lh, rh) + dot(ll, rh) + dot(lh, rl)


def own_rows_t(info, size, v):
    row = lax.broadcasted_iota(jnp.int32, (size, v.shape[1]), 0)
    column = lax.broadcasted_iota(jnp.int32, (size, v.shape[1]), 1)
    choose = (column == row + size * info[1]).astype(F32).astype(BF16)
    high = v.astype(BF16)
    rest = (v - high.astype(F32)).astype(BF16)
    return dot_nt(choose, high) + dot_nt(choose, rest)


def mod_back_kernel(bands, seqs, info, *refs):
    sums = refs[:bands]
    (both, embed, t2, w_h, g_ada_h, gb_ada, g_t2, gb_t2, g_t1, gb_t1, gb_down, gb_up,
     w, g_ada, sems, acc, dmod, all_bias) = refs[bands:]
    pieces = [pl.ds(i * D, D) for i in range(9)]
    copies = fetch([(w_h.at[:, piece], w.at[i]) for i, piece in enumerate(pieces)], sems)
    own_act = own_rows_t(info, D // seqs, silu(both[1]))
    bias = jnp.zeros((5, D), F32)
    for t in range(bands):
        held = sums[t][sums[t].shape[0] - 32 :, :].astype(F32)
        for u in range(2):
            r = 2 * t + u
            for p in range(9):
                dmod[p, r : r + 1, :] = held[16 * u + p : 16 * u + p + 1]
            bias += held[16 * u + 9 : 16 * u + 14]
    stores = []
    for i, piece in enumerate(pieces):
        part = dmod[i]
        g_ada[i] = outer_sum(own_act, part)
        stores.append(pltpu.make_async_copy(g_ada.at[i], g_ada_h.at[:, piece], sems.at[9 + i]))
        stores[-1].start()
        all_bias[:, i * D : (i + 1) * D] = jnp.broadcast_to(colsum(part), (8, D))
        copies[i].wait()
        term = split_dot(part, w[i], contract=1)
        if i:
            acc[...] += term
        else:
            acc[...] = term

    def own_part(row):
        size = row.shape[1] // seqs
        rows = jnp.broadcast_to(row, (8, row.shape[1]))
        return pltpu.roll(rows, row.shape[1] - info[1] * size, 1)[0:1, 0:size]

    size = 9 * D // seqs
    gb_ada[...] = pltpu.roll(all_bias[...], 9 * D - info[1] * size, 1)[0:1, 0:size]
    gb_down[...] = own_part(bias[0:1])
    gb_up[...] = own_part(jnp.concatenate([bias[1 + i : 2 + i] for i in range(4)], axis=1))
    dcond = acc[...] * silu_grad(both[1])
    g_t2[...] = outer_sum(own_rows_t(info, D // seqs, silu(both[0])), dcond)
    gb_t2[...] = own_part(colsum(dcond))
    dpre = split_dot(dcond, t2[...], contract=1) * silu_grad(both[0])
    g_t1[...] = outer_sum(own_rows_t(info, g_t1.shape[0], embed[...]), dpre)
    gb_t1[...] = own_part(colsum(dpre))
    for store in stores:
        store.wait()


def mod_back(chain, info, sums, w, both, embed, t2, seqs):
    bands = len(sums)
    items = 2 * bands
    m = D // seqs
    line = lambda n: sds((1, n // seqs), F32)
    outs = [
        sds((m, 9 * D), F32), line(9 * D), sds((m, D), F32), line(D), sds((embed.shape[1] // seqs, D), F32),
        line(D), line(D), line(FF),
    ]
    anywhere = pl.BlockSpec(memory_space=pl.ANY)
    here = [*sums, both, embed, t2]
    return chain(
        functools.partial(mod_back_kernel, bands, seqs), outs, [info, *here, w], 15, "modulation_back",
        grid=(1,), in_specs=[smem()] + [whole(v) for v in here] + [anywhere],
        out_specs=[anywhere] + [whole(o) for o in outs[1:]],
        scratch=[
            pltpu.VMEM((9, D, D), BF16), pltpu.VMEM((9, m, D), F32), pltpu.SemaphoreType.DMA((18,)),
            pltpu.VMEM((items, D), F32), pltpu.VMEM((9, items, D), F32), pltpu.VMEM((8, 9 * D), F32),
        ],
    )


def block_refs(order, even, odd):
    return [(odd if k % 2 else even).at[k // 2] for k in order]


def qkv_kernel(order, span, even, odd, mod, w, out, h1_o, h1):
    frames = block_refs(order, even, odd)
    blocks = len(order)
    own = 2 * span

    @pl.when(pl.program_id(0) == 0)
    def _():
        shift, scale = mod[0:1, 0:D], mod[0:1, D : 2 * D]
        for i in range(blocks):
            n, unused = norm(frames[i][0:span, :].astype(F32))
            h1[pl.ds(i * span, span), :] = (n * (1.0 + scale) + shift).astype(BF16)
        h1_o[...] = h1[0:own, :]

    factor = jnp.where(pl.program_id(0) == 0, SCALE, 1.0)

    @pl.loop(0, blocks * span // own)
    def _(i):
        rows = pl.ds(pl.multiple_of(i * own, own), own)
        out[0, rows, :] = (dot(h1[rows, :], w[...]) * factor).astype(BF16)


def qkv(chain, blocks, order, span, mod, w):
    total = len(order) * span
    outs = [sds((3, total, D), BF16), sds((2 * span, D), BF16)]
    args = [blocks[0][0], blocks[2][0], mod]
    return chain(
        functools.partial(qkv_kernel, order, span), outs, [*args, w], room(16, total), "qkv", grid=(3,),
        in_specs=[whole(v) for v in args] + [pl.BlockSpec((D, D), lambda i: (0, i))],
        out_specs=[pl.BlockSpec((1, total, D), lambda i: (i, 0, 0)), whole(outs[1])],
        scratch=[pltpu.VMEM((total, D), BF16)],
    )


def attend_kernel(q, k, v, o, lse):
    qm = stack_heads(q[0])
    scores = dot_nt(k[0], qm)
    peak = jnp.max(scores, axis=0, keepdims=True)
    weights = jnp.exp(scores - peak)
    total = jnp.sum(weights, axis=0, keepdims=True)
    both = dot(v[0].T, weights.astype(BF16)) * (1.0 / total)
    o[...] = unstack_t(both).astype(BF16)
    lse[0] = peak + jnp.log(total)


def part_spec(part, rows):
    return pl.BlockSpec((1, rows, 128), lambda i: (part, 0, i))


def attend(chain, joined, own):
    total = joined.shape[1]
    return chain(
        attend_kernel, [sds((own, D), BF16), sds((PAIRS, 1, 2 * own), F32)], [joined] * 3, room(8, total),
        "attend", grid=(PAIRS,),
        in_specs=[part_spec(0, own), part_spec(1, total), part_spec(2, total)],
        out_specs=[
            pl.BlockSpec((own, 128), lambda i: (0, i)),
            pl.BlockSpec((1, 1, 2 * own), lambda i: (i, 0, 0)),
        ],
    )


def qkv_attend_kernel(order, span, even, odd, mod, w, out_h, h1_o, o, lse, h1, joined, sems):
    own = 2 * span
    total = joined.shape[1]
    shift, scale = mod[0:1, 0:D], mod[0:1, D : 2 * D]
    for i, block in enumerate(block_refs(order, even, odd)):
        n, unused = norm(block[0:span, :].astype(F32))
        h1[pl.ds(i * span, span), :] = (n * (1.0 + scale) + shift).astype(BF16)
    h1_o[...] = h1[0:own, :]
    stores = []
    for part in (1, 2, 0):
        piece = w[:, part * D : (part + 1) * D]
        for i in range(total // own):
            rows = slice(i * own, (i + 1) * own)
            value = dot(h1[rows, :], piece)
            joined[part, rows, :] = ((value * SCALE) if part == 0 else value).astype(BF16)
        stores.append(pltpu.make_async_copy(joined.at[part], out_h.at[part], sems.at[part]))
        stores[-1].start()
    for i in range(PAIRS):
        qm = stack_heads(joined[0, 0:own, cols(i)])
        scores = dot_nt(joined[1, :, cols(i)], qm)
        peak = jnp.max(scores, axis=0, keepdims=True)
        weights = jnp.exp(scores - peak)
        sums = jnp.sum(weights, axis=0, keepdims=True)
        both = dot(joined[2, :, cols(i)].T, weights.astype(BF16)) * (1.0 / sums)
        o[:, cols(i)] = unstack_t(both).astype(BF16)
        lse[i] = peak + jnp.log(sums)
    for store in stores:
        store.wait()


def qkv_attend(chain, blocks, order, span, mod, w):
    total, own = len(order) * span, 2 * span
    if total > 1024:
        joined, h1 = qkv(chain, blocks, order, span, mod, w)
        mixed, lse = attend(chain, joined, own)
        return joined, h1, mixed, lse
    outs = [
        sds((3, total, D), BF16), sds((own, D), BF16), sds((own, D), BF16), sds((PAIRS, 1, 2 * own), F32)
    ]
    return chain(
        functools.partial(qkv_attend_kernel, order, span), outs, [blocks[0][0], blocks[2][0], mod, w], 10,
        "qkv_attend", out_specs=[pl.BlockSpec(memory_space=pl.ANY)] + [vmem()] * 3,
        scratch=[
            pltpu.VMEM((total, D), BF16), pltpu.VMEM((3, total, D), BF16), pltpu.SemaphoreType.DMA((3,))
        ],
    )


def two_terms(rows):
    high = rows.astype(BF16).astype(F32)
    return jnp.concatenate([high, rows - high], axis=0).astype(BF16)


def read_stats(block):
    own = block.shape[0] - 16
    held = block[own:, :].astype(F32)

    def line(at):
        rows = held[at : at + 4] + held[at + 4 : at + 8]
        return jnp.concatenate([rows[i : i + 1] for i in range(4)], axis=1)

    return line(0), line(8)


def attend_dq_kernel(q, k, v, do, dq):
    own = do.shape[0] - 16
    qm = stack_heads(q[0])
    dom = stack_heads(do[0:own, :])
    lse, delta = read_stats(do)
    probs = jnp.exp(dot_nt(k[0], qm) - lse)
    grad = dot_nt(v[0], dom)
    ds = (probs * (grad - delta)).astype(BF16)
    dq[...] = (unstack_t(dot(k[0].T, ds)) * SCALE).astype(BF16)


def attend_dq(chain, joined, do):
    own = do.shape[0] - 16
    total = joined.shape[1]
    return chain(
        attend_dq_kernel, [sds((own, D), BF16)], [joined, joined, joined, do], room(5, total),
        "attend_dq", grid=(PAIRS,),
        in_specs=[
            part_spec(0, own), part_spec(1, total), part_spec(2, total),
            pl.BlockSpec((own + 16, 128), lambda i: (0, i)),
        ],
        out_specs=[pl.BlockSpec((own, 128), lambda i: (0, i))],
    )[0]


def attend_dkv_kernel(chunks, dq, q, k, v, *refs):
    do, out = refs[:chunks], refs[-1]
    keys, values = k[0], v[0]
    own = keys.shape[0]
    dk = jnp.zeros((own, 128), F32)
    dv = jnp.zeros((own, 128), F32)
    for i in range(chunks):
        qm = stack_heads(q[0, i * own : (i + 1) * own, :])
        block = do[i][...]
        dom = stack_heads(block[0:own, :])
        lse, delta = read_stats(block)
        probs = jnp.exp(dot_nt(keys, qm) - lse)
        dv += dot(probs.astype(BF16), dom)
        grad = dot_nt(values, dom)
        ds = (probs * (grad - delta)).astype(BF16)
        dk += dot(ds, qm)
    lanes = pl.ds(pl.multiple_of(128 * pl.program_id(0), 128), 128)
    out[0:own, lanes] = dq[...]
    out[own : 2 * own, lanes] = dk.astype(BF16)
    out[2 * own : 3 * own, lanes] = dv.astype(BF16)


def last_kernel(chunks, *refs):
    first, even, w, mod, dx1, away, out, own_o, back_o, part = refs[4 + chunks :]
    attend_dkv_kernel(chunks, *refs[: 4 + chunks], part)
    own = part.shape[0] // 3
    half = part.shape[1]

    @pl.when(pl.program_id(0) == PAIRS // 2 - 1)
    def _():
        out[0 : 3 * own, 0:half] = first[...]
        out[0 : 3 * own, half:] = part[...]
        scale1 = mod[0:1, D : 2 * D]
        dh1 = sum(dot_nt(out[i * own : (i + 1) * own, :], w[:, i * D : (i + 1) * D]) for i in range(3))
        span = own_o.shape[0]
        n1, rstd = norm(start_rows(even.at[0], even.at[even.shape[0] // 2], span))
        sums = jnp.concatenate([colsum(dh1), colsum(n1 * dh1), jnp.zeros((14, D), F32)], axis=0)
        out[3 * own :, :] = sums.astype(BF16)
        grad = dx1[...] + norm_back(n1, rstd, (1.0 + scale1) * dh1)
        own_o[...] = grad[:span]
        back_o[0] = grad[span:].astype(BF16)
        back_o[1] = away[...]


def attend_dkv(chain, dq, joined, do, half, rest=()):
    own = dq.shape[0]
    span = own // 2
    shift = half * (PAIRS // 2)
    pair = lambda part, rows: pl.BlockSpec((1, rows, 128), lambda i: (part, 0, i + shift))
    specs = [
        pl.BlockSpec((own + 16, 128), functools.partial(lambda at, i: (at, i + shift), at)) for unused, at in do
    ]
    outs = [sds((3 * own, D // 2), BF16)]
    kernel = attend_dkv_kernel
    scratch = []
    if rest:
        outs = [sds((3 * own + 16, D), BF16), sds((span, D), F32), sds((2, span, D), BF16)]
        kernel = last_kernel
        scratch = [pltpu.VMEM((3 * own, D // 2), BF16)]
    return chain(
        functools.partial(kernel, len(do)), outs,
        [dq, joined, joined, joined, *(array for array, unused in do), *rest],
        room(4, joined.shape[1]) + (3 if rest else 0), "attend_dkv", grid=(PAIRS // 2,),
        in_specs=[pl.BlockSpec((own, 128), lambda i: (0, i + shift))]
        + [pair(0, joined.shape[1]), pair(1, own), pair(2, own)]
        + specs + [whole(v) for v in rest],
        out_specs=[whole(o) for o in outs], scratch=scratch,
    )


def start_rows(fa, fb, span):
    return jnp.concatenate([fa[0:span, :], fb[0:span, :]], axis=0).astype(F32)


def gelu_both(u):
    c = math.sqrt(2.0 / math.pi)
    square = u * u
    t = jnp.tanh(c * u * (1.0 + 0.044715 * square))
    half = 0.5 * (1.0 + t)
    slope = half + 0.5 * u * (1.0 - t * t) * (c * (1.0 + 3 * 0.044715 * square))
    return u * half, slope


STEPS = FF // D


def fetch(pairs, sems):
    copies = [pltpu.make_async_copy(a, b, sems.at[i]) for i, (a, b) in enumerate(pairs)]
    for copy in copies:
        copy.start()
    return copies


def forward_kernel(span, order, *refs):
    count = len(order)
    info, cap_len, *blocks = refs[: 2 + count]
    (o, h1, mod, ca, cb, up_b, down_b, wo, wq, wkv, wc, up, down,
     big_o, out_o, away_o, cap_o, h2_o, o2_o, x1, dx2_o, attn_o, attn2_o, sums_o, kv2, q2, p2,
     x2, low, dh3, offset) = refs[2 + count :]
    cap_rows = blocks[0].shape[0] - span

    big_o[2 * STEPS + 2] = o[...]
    big_o[2 * STEPS + 3] = h1[...]

    gate1, shift2, scale2, gate2, shift3, scale3, gate3 = (
        mod[0:1, i * D : (i + 1) * D] for i in range(2, 9)
    )

    length = cap_len[2 * info[0] + info[2]]
    for i, k in enumerate(order):
        here = slice(i * cap_rows, (i + 1) * cap_rows)
        cap_o[here, :] = blocks[i][span:, :]
        first = jnp.bitwise_xor(info[1], k) * cap_rows
        token = first + lax.broadcasted_iota(jnp.int32, (cap_rows, 128), 0)
        offset[here, :] = jnp.where(token < length, 0.0, NEGATIVE)
    dy = jnp.concatenate([ca[...], cb[...]], axis=0).astype(F32)
    big_o[2 * STEPS + 1] = (gate3 * dy).astype(BF16)

    attn = dot(o[...], wo[...])
    x1[...] = start_rows(blocks[0], blocks[1], span) + gate1 * attn
    attn_o[...] = attn.astype(BF16)
    n2, unused = norm(x1[...])
    h2 = (n2 * (1.0 + scale2) + shift2).astype(BF16)
    h2_o[...] = h2
    kv2[...] = dot(cap_o[...], wkv[...]).astype(BF16)
    q2[...] = (dot(h2, wq[...]) * SCALE).astype(BF16)
    for i in range(PAIRS):
        qm = stack_heads(q2[:, cols(i)])
        scores = dot_nt(kv2[:, cols(i)], qm) + offset[:, 0:1]
        peak = jnp.max(scores, axis=0, keepdims=True)
        weights = jnp.exp(scores - peak)
        probs = (weights * (1.0 / jnp.sum(weights, axis=0, keepdims=True))).astype(BF16)
        p2[i] = probs
        both = dot(kv2[:, D + i * 128 : D + (i + 1) * 128].T, probs)
        o2_o[:, cols(i)] = unstack_t(both).astype(BF16)
    attn2 = dot(o2_o[...], wc[...])
    x2[...] = x1[...] + gate2 * attn2
    attn2_o[...] = attn2.astype(BF16)

    n3, unused = norm(x2[...])
    big_o[2 * STEPS] = (n3 * (1.0 + scale3) + shift3).astype(BF16)
    for i in range(STEPS):
        piece = slice(i * D, (i + 1) * D)
        acted, slope = gelu_both(dot(big_o[2 * STEPS], up[:, piece]) + up_b[:, piece].astype(F32))
        acted = acted.astype(BF16)
        big_o[i] = acted
        dupper = (slope * dot_nt(big_o[2 * STEPS + 1], down[piece, :])).astype(BF16)
        big_o[STEPS + i] = dupper
        sums_o[8 + i : 9 + i, :] = colsum(dupper.astype(F32))
        if i:
            low[...] += dot(acted, down[piece, :])
            dh3[...] += dot_nt(dupper, up[:, piece])
        else:
            low[...] = dot(acted, down[piece, :])
            dh3[...] = dot_nt(dupper, up[:, piece])
    lower = low[...] + down_b[...].astype(F32)
    value = x2[...]
    result = (value + gate3 * lower).astype(BF16)
    out_o[...] = result[:span]
    away_o[...] = result[span:]
    dy = jnp.concatenate([ca[...], cb[...]], axis=0).astype(F32)
    n3, rstd = norm(value)
    back = dh3[...]
    sums_o[0:4, :] = jnp.zeros((4, D), F32)
    sums_o[4:5, :] = colsum(back)
    sums_o[5:6, :] = colsum(n3 * back)
    sums_o[6:7, :] = colsum(lower * dy)
    sums_o[7:8, :] = colsum(big_o[2 * STEPS + 1].astype(F32))
    sums_o[12:16, :] = jnp.zeros((4, D), F32)
    dx2_o[...] = dy + norm_back(n3, rstd, (1.0 + scale3) * back)


def backward_kernel(dx2_r, mod, attn2, kv2, q2, p2, x1, attn, o, lse, h2, o2, sums3,
                    wc, wq, wo, fac_o, dx1_o, do_o, sums_o):
    own = o.shape[0]
    slot = lambda i: slice(i * own, (i + 1) * own)
    gate1, scale2, gate2 = (mod[0:1, i * D : (i + 1) * D] for i in (2, 4, 5))
    sums_o[...] = sums3[...]
    fac_o[slot(0), :] = h2[...]
    fac_o[slot(2), :] = o2[...]
    dx2 = dx2_r[...]
    sums_o[3:4, :] = colsum(attn2[...].astype(F32) * dx2)
    da2 = (gate2 * dx2).astype(BF16)
    fac_o[slot(3), :] = da2
    do2 = dot_nt(da2, wc[...]).astype(BF16)
    for i in range(PAIRS):
        qm = stack_heads(q2[:, cols(i)])
        dom = stack_heads(do2[:, cols(i)])
        keys, values = kv2[:, cols(i)], kv2[:, D + i * 128 : D + (i + 1) * 128]
        probs = p2[i]
        fac_o[slot(5), cols(i)] = dot(probs, dom).astype(BF16)
        probs = probs.astype(F32)
        grad = dot_nt(values, dom)
        ds = (probs * (grad - colsum(probs * grad))).astype(BF16)
        fac_o[slot(1), cols(i)] = (unstack_t(dot(keys.T, ds)) * SCALE).astype(BF16)
        fac_o[slot(4), cols(i)] = dot(ds, qm).astype(BF16)
    dh2 = dot_nt(fac_o[slot(1), :], wq[...])
    n2, rstd = norm(x1[...])
    sums_o[1:2, :] = colsum(dh2)
    sums_o[2:3, :] = colsum(n2 * dh2)
    dx1 = dx2 + norm_back(n2, rstd, (1.0 + scale2) * dh2)
    dx1_o[...] = dx1
    sums_o[0:1, :] = colsum(attn[...].astype(F32) * dx1)

    da = (gate1 * dx1).astype(BF16)
    fac_o[slot(6), :] = da
    do = dot_nt(da, wo[...]).astype(BF16)
    do_o[0:own, :] = do
    both = do.astype(F32) * o[...].astype(F32)
    for i in range(PAIRS):
        t = both[:, cols(i)].T
        delta = [colsum(t[:HEAD]), colsum(t[HEAD:])]
        delta = [d[:, 128 * j : 128 * (j + 1)] for d in delta for j in range(own // 128)]
        sums = [lse[i][:, 128 * j : 128 * (j + 1)] for j in range(2 * own // 128)]
        held = [two_terms(jnp.concatenate(rows, axis=0)) for rows in (sums, delta)]
        do_o[own:, cols(i)] = jnp.concatenate(held, axis=0)
    fac_o[7 * own : 7 * own + 16, :] = sums_o[...].astype(BF16)
    at = do_place(own) * (own + 16)
    fac_o[7 * own + 16 : at, :] = jnp.zeros((at - 7 * own - 16, D), BF16)
    fac_o[at:, :] = do_o[...]


def forward(chain, info, cap_len, blocks, order, span, o, h1, mod, ca, cb, up_b, down_b, *weights):
    own = 2 * span
    cap_total = len(blocks) * (blocks[0][0].shape[1] - span)
    thin, wide = sds((own, D), BF16), sds((own, D), F32)
    half = sds((span, D), BF16)
    outs = [
        sds((2 * STEPS + 4, own, D), BF16), half, half, sds((cap_total, D), BF16), thin, thin, wide, wide,
        thin, thin, sds((16, D), F32), sds((cap_total, 2 * D), BF16), thin,
        sds((PAIRS, cap_total, 2 * own), BF16),
    ]
    here = [blocks[0][0], blocks[2][0], o, h1, mod, ca, cb, up_b, down_b]
    square = pltpu.VMEM((D, D), BF16)

    def kernel(info, cap_len, even, odd, *refs):
        forward_kernel(span, order, info, cap_len, *block_refs(order, even, odd), *refs)

    return chain(
        kernel, outs, [info, cap_len, *here, *weights], FWD, "forward",
        in_specs=[smem()] * 2 + [vmem()] * (len(here) + len(weights)),
        scratch=[pltpu.VMEM((own, D), F32)] * 3
        + [pltpu.VMEM((cap_total, 128), F32)],
    )


def do_place(own):
    return -(-(7 * own + 16) // (own + 16))


def backward(chain, here, weights):
    own = here[0].shape[0]
    outs = [
        sds(((do_place(own) + 1) * (own + 16), D), BF16), sds((own, D), F32),
        sds((own + 16, D), BF16),
        sds((16, D), F32),
    ]
    square = pltpu.VMEM((D, D), BF16)
    return chain(
        backward_kernel, outs, [*here, *weights], BWD, "backward",
    )


def pick_rows(info, x):
    source = lax.broadcasted_iota(jnp.int32, (D, D // 2), 0)
    column = lax.broadcasted_iota(jnp.int32, (D, D // 2), 1)
    block = sum((column >= 96 * i).astype(jnp.int32) for i in (1, 2, 3))
    wanted = 96 * jnp.bitwise_xor(info[1], 2 * block) + column - 96 * block
    choose = (source == wanted).astype(F32).astype(BF16)
    return dot(x, choose).astype(BF16)


def emit(first, info, tiles, blocks, send_o, keep_o):
    place = {True: 0, False: 0}
    for r in range(4):
        sent = bool(r & first)
        (send_o if sent else keep_o)[place[sent]] = tiles[jnp.bitwise_xor(info[0], r), blocks]
        place[sent] += 1


def down_grad_kernel(info, fac, fac_p, send_o, keep_o, tiles):
    for e in range(4):
        owner = jnp.bitwise_xor(info[1], 2 * e)
        half = pl.multiple_of(lax.rem(owner, 2) * 384, 128)
        where = (lax.div(owner, 2), slice(None), pl.ds(half, 384))
        grad = dot_tn(fac[where], fac[2 * STEPS + 1]) + dot_tn(fac_p[where], fac_p[9])
        for q in range(4):
            tiles[q, e] = grad[96 * q : 96 * (q + 1)].astype(BF16)
    emit(1, info, tiles, slice(0, 4), send_o, keep_o)


def up_grad_kernel(info, fac, fac_p, send_o, keep_o, tiles):
    x, xp = pick_rows(info, fac[8]), pick_rows(info, fac_p[8])
    for q in range(4):
        grad = dot_tn(x, fac[4 + q]) + dot_tn(xp, fac_p[4 + q])
        for e in range(4):
            tiles[q, e] = grad[96 * e : 96 * (e + 1)].astype(BF16)
    emit(2, info, tiles, slice(0, 4), send_o, keep_o)


def put(tiles, q, grad):
    for e in range(4):
        tiles[q, e] = grad[96 * e : 96 * (e + 1)].astype(BF16)


def emit_both(info, tiles, sx, kx, sy, ky):
    emit(1, info, tiles, slice(0, 2), sx, kx)
    emit(2, info, tiles, slice(2, 4), sy, ky)


def cross_grad_kernel(own, info, cap, fac, fac_p, wkv, sx, kx, sy, ky, dcap_o, tiles):
    def slot(ref, i):
        return ref[i * own : (i + 1) * own, :]

    def pair(x, y):
        left, left_p = pick_rows(info, slot(fac, x)), pick_rows(info, slot(fac_p, x))
        return dot_tn(left, slot(fac, y)) + dot_tn(left_p, slot(fac_p, y))

    put(tiles, 0, pair(0, 1))
    x = pick_rows(info, cap[...])
    rows = cap.shape[0] // 4
    xp = jnp.concatenate([x[rows * i : rows * (i + 1)] for i in (1, 0, 3, 2)], axis=0)
    for q in (1, 2):
        put(tiles, q, dot_tn(x, slot(fac, q + 3)) + dot_tn(xp, slot(fac_p, q + 3)))
    put(tiles, 3, pair(2, 3))
    emit_both(info, tiles, sx, kx, sy, ky)

    rows = cap.shape[0] // 8

    def even(x):
        places = [rows * order_place(k) for k in range(8)]
        parts = [
            total(slot(fac, x)[places[k] : places[k] + rows], slot(fac_p, x)[places[k + 1] : places[k + 1] + rows])
            for k in (0, 2, 4, 6)
        ]
        return jnp.concatenate(parts, axis=0)

    dcap_o[...] = (dot_nt(even(4), wkv[:, 0:D]) + dot_nt(even(5), wkv[:, D : 2 * D])).astype(BF16)


def attn_grad_kernel(info, da, o, h1, da_p, o_p, h1_p, dqkv, dqkv_p, sx, kx, sy, ky, tiles):
    own = da.shape[0]
    x, xp = pick_rows(info, h1[0]), pick_rows(info, h1_p[0])
    for i in range(3):
        slot = slice(i * own, (i + 1) * own)
        put(tiles, i, dot_tn(x, dqkv[slot, :]) + dot_tn(xp, dqkv_p[slot, :]))
    x, xp = pick_rows(info, o[0]), pick_rows(info, o_p[0])
    put(tiles, 3, dot_tn(x, da[...]) + dot_tn(xp, da_p[...]))
    emit_both(info, tiles, sx, kx, sy, ky)


def grad_call(chain, kernel, info, args, name, shape, outs, in_specs=None):
    return chain(
        kernel, [sds(o, BF16) for o in outs], [info, *args], 5, name, grid=(1,) if in_specs else None,
        in_specs=[smem()] + (in_specs or [vmem()] * len(args)),
        scratch=[pltpu.VMEM(shape, BF16)],
    )


def total(*refs):
    return sum(r.astype(F32) for r in refs).astype(BF16)


def add_first_kernel(keep, recv, keep_o, send_o):
    keep_o[...] = total(keep[0], recv[0])
    send_o[...] = total(keep[1], recv[1])


def add_both_kernel(kx, rx, ky, ry, kx_o, sx_o, ky_o, sy_o):
    add_first_kernel(kx, rx, kx_o, sx_o)
    add_first_kernel(ky, ry, ky_o, sy_o)


def sum_rows(early, early_p, late, late_p):
    first = late[0:2, :].astype(F32) + late_p[0:2, :].astype(F32)
    both = early[0:12, :].astype(F32) + early_p[0:12, :].astype(F32)
    return jnp.concatenate([first, both, jnp.zeros((2, D), F32)], axis=0).astype(BF16)


def mlp_second_kernel(ka, ra, kb, rb, fac, fac_p, late, late_p, keep_o, send_o):
    for g, (keep, recv) in enumerate(((ka, ra), (kb, rb))):
        for e in range(4):
            (send_o if e % 2 else keep_o)[e // 2, 96 * g : 96 * (g + 1), :] = total(keep[e], recv[e])
    rows = sum_rows(fac, fac_p, late, late_p)
    for ref in (keep_o, send_o):
        for i in range(2):
            ref[i, 192:208, :] = rows


def mlp_third_kernel(keep, recv, keep_o, send_o):
    keep_o[...] = total(keep[0], recv[0])
    send_o[0:192, :] = total(keep[1, 0:192, :], recv[1, 0:192, :])
    send_o[192:208, :] = total(keep[0, 192:208, :], recv[0, 192:208, :])


def mlp_fourth_kernel(keep, recv, out):
    out[0:192, :] = total(keep[0:192, :], recv[0:192, :])
    out[192:208, :] = keep[192:208, :]
    out[208:224, :] = recv[192:208, :]


def order_place(k):
    return 2 * (k % 4) + k // 4


def second_kernel(kx, rx, ky, ry, *refs):
    caption, (keep_o, send_o) = refs[:-2], refs[-2:]
    for e in range(4):
        out = send_o if e % 2 else keep_o
        keep, recv = ((kx, rx), (ky, ry))[e // 2]
        out[e // 2, 0:96, :] = total(keep[e % 2], recv[e % 2])
        if caption:
            rows = caption[0].shape[0] // 4
            out[e // 2, 96:, :] = caption[0][rows * e : rows * (e + 1), :]


def third_kernel(keep, recv, keep_o, send_o):
    keep_o[...] = total(keep[0], recv[0])
    send_o[...] = total(keep[1], recv[1])


def fourth_kernel(keep, recv, c_keep, c_recv, out, same_o, away_o):
    out[0:96, :] = total(keep[...], recv[...])
    out[96:, :] = total(c_keep[0:96, :], c_recv[0:96, :])
    same_o[...] = c_keep[96:, :].astype(F32)
    away_o[...] = c_recv[96:, :].astype(F32)


def swap(x, axis, size, k):
    return lax.ppermute(x, axis, [(i, i ^ k) for i in range(size)])


def over_x(x):
    return swap(x, "band", 4, 1)


def over_y(x):
    return swap(x, "band", 4, 2)


def to_band(x):
    return [x] + [swap(x, "band", 4, t) for t in (1, 2, 3)]


def mlp_finish_kernel(info, t0, t1, t2, t3, down_o, up_o):
    for r, tile in enumerate((t0, t1, t2, t3)):
        q = jnp.bitwise_xor(info[0], r)
        down_o[pl.ds(pl.multiple_of(96 * q, 96), 96), :] = tile[0:96, :].astype(F32)
        up_o[:, pl.ds(pl.multiple_of(D * q, D), D)] = tile[96:192, :].astype(F32)


def last_finish_kernel(info, t0, t1, t2, t3, in_o, out_o, cq_o, ckv_o, co_o, tiles):
    for r, tile in enumerate((t0, t1, t2, t3)):
        tiles[jnp.bitwise_xor(info[0], r)] = tile[...]
    for i in range(3):
        in_o[:, i * D : (i + 1) * D] = tiles[i, 0:96, :].astype(F32)
    out_o[...] = tiles[3, 0:96, :].astype(F32)
    cq_o[...] = tiles[0, 96:, :].astype(F32)
    ckv_o[:, 0:D] = tiles[1, 96:, :].astype(F32)
    ckv_o[:, D:] = tiles[2, 96:, :].astype(F32)
    co_o[...] = tiles[3, 96:, :].astype(F32)


def finish(chain, kernel, info, tiles, widths, name, scratch=(), held=()):
    outs = [sds(w, F32) for w in widths] + [sds(h.shape, h.dtype) for h in held]
    tiles = [*tiles, *held]
    return chain(
        kernel, outs, [info, *tiles], 5, name, grid=(1,), in_specs=[smem()] + [whole(t) for t in tiles],
        out_specs=[whole(o) for o in outs], scratch=scratch,
    )


def plain_reduce(x, y, owners):
    grad = lax.psum_scatter(dot_tn(x, y).astype(BF16), "seq", scatter_dimension=0, tiled=True)
    return lax.psum(grad, "band").astype(F32)


def on_device(bands, seqs, frames, caption, timesteps, cap_len, attn_in, attn_out, cross_query,
              cross_keyval, cross_out, mlp_up, up_bias, mlp_down, down_bias, ada_weight, ada_bias,
              time_first, first_bias, time_second, second_bias, cotangent):
    span = frames.shape[1]
    own = 2 * span
    cap_rows = caption.shape[1]
    items = timesteps.shape[0]
    halves = seqs // 2
    band = lax.axis_index("band")
    seq = lax.axis_index("seq")
    half = (seq >= halves).astype(jnp.int32)
    item = 2 * band + half
    info = jnp.stack([band, seq, half]).astype(jnp.int32)

    chain = Chain()

    order = [k for i in range(halves) for k in (i, i + halves)]
    def item_rows(which):
        return jnp.concatenate(
            [lax.dynamic_index_in_dim(x, which, keepdims=False) for x in (frames, caption)]
        )

    other, same = item_rows(1 - half), item_rows(half)
    even = [same] + [swap(same if k < halves else other, "seq", seqs, k) for k in range(2, seqs, 2)]

    steps = jnp.take(timesteps, jnp.bitwise_xor(jnp.arange(items), item))
    width = time_first.shape[0] // 2
    freq = jnp.exp(-math.log(10000.0) * jnp.arange(width, dtype=F32) / width)
    angle = steps.astype(F32)[:, None] * freq[None, :]
    embed = jnp.concatenate([jnp.cos(angle), jnp.sin(angle)], axis=1)
    row = lambda v: v.reshape(1, -1)
    pre_cond, mod = modulation(
        chain, embed, time_first, row(first_bias), time_second, row(second_bias), ada_weight, row(ada_bias)
    )
    cot_own, cot_other = pick(chain, info, cotangent, early=[mlp_up, mlp_down])
    cot_other = swap(cot_other, "seq", seqs, halves)

    even = stack(chain, even, "blocks")
    odd = swap(even, "seq", seqs, 1)
    blocks = [(odd if k % 2 else even, k // 2) for k in order]
    joined, h1, mixed, lse = qkv_attend(chain, blocks, order, span, mod, attn_in)

    cap_total = seqs * cap_rows
    (big, out, out_back, cap_all, h2, o2, x1, dx2, attn, attn2, sums3, kv2, q2, p2) = forward(
        chain, info, cap_len, blocks, order, span, mixed, h1, mod, cot_own, cot_other, row(up_bias),
        row(down_bias), attn_out, cross_query, cross_keyval, cross_out, mlp_up, mlp_down,
    )
    fast = bands == 4 and seqs == 8
    if fast:
        big_p = swap(big, "seq", seqs, 1)
    fac, dx1, do, early = backward(
        chain, [dx2, mod, attn2, kv2, q2, p2, x1, attn, mixed, lse, h2, o2, sums3],
        [cross_out, cross_query, attn_out],
    )
    if fast:
        fac_p = swap(fac, "seq", seqs, 1)
    got = {k: (swap(do, "seq", seqs, k), 0) for k in range(2 if fast else 1, halves)}
    got[0] = (do, 0)
    if fast:
        got[1] = (fac_p, do_place(own))
        whole_tiles, pieces, halved = (4, 4, 96, D), [(2, 4, 96, D)] * 2, [(2, 2, 96, D)] * 4
        args = [big, big_p]
        sa, ka = grad_call(chain, down_grad_kernel, info, args, "down_grad", whole_tiles, pieces)
        ra = over_x(sa)
        sb, kb = grad_call(chain, up_grad_kernel, info, args, "up_grad", whole_tiles, pieces)
        rb = over_y(sb)
        cx, ckx, cy, cky, dcap = grad_call(
            chain, functools.partial(cross_grad_kernel, own), info, [cap_all, fac, fac_p, cross_keyval],
            "cross_grad", whole_tiles, halved + [(cap_total // 2, D)],
        )
        crx, cry = over_x(cx), over_y(cy)
    dq = attend_dq(chain, joined, do)
    do_blocks = [got[k] for k in range(halves)]
    dkv_first = attend_dkv(chain, dq, joined, do_blocks, 0)[0]
    dqkv, grad_own, back = attend_dkv(
        chain, dq, joined, do_blocks, 1, [dkv_first, even, attn_in, mod, dx1, out_back]
    )
    back = swap(back, "seq", seqs, halves)
    if fast:
        dqkv_p = swap(dqkv, "seq", seqs, 1)
        half, quarter, tile = sds((4, 96, D), BF16), sds((2, 96, D), BF16), sds((96, D), BF16)
        ka, sa, kb, sb = chain(add_both_kernel, [half] * 4, [ka, ra, kb, rb], 2, "mlp_add1")
        ra, rb = over_y(sa), over_x(sb)
        slots = [pl.BlockSpec((own, D), lambda *i: (6, 0))] + [
            pl.BlockSpec((1, own, D), functools.partial(lambda at, *i: (at, 0, 0), at))
            for at in (2 * STEPS + 2, 2 * STEPS + 3)
        ]
        tx, tkx, ty, tky = grad_call(
            chain, attn_grad_kernel, info, [fac, big, big, fac_p, big_p, big_p, dqkv, dqkv_p], "attn_grad",
            whole_tiles, halved, in_specs=slots * 2 + [whole(dqkv)] * 2,
        )
        trx, try_ = over_x(tx), over_y(ty)
        sum_at, late_at = 7 * own // 16, 3 * own // 16
        sum_spec = pl.BlockSpec((16, D), lambda *i: (sum_at, 0))
        late_spec = pl.BlockSpec((16, D), lambda *i: (late_at, 0))
        keep, send = chain(
            mlp_second_kernel, [sds((2, 208, D), BF16)] * 2, [ka, ra, kb, rb, fac, fac_p, dqkv, dqkv_p], 4,
            "mlp_add2", grid=(1,), in_specs=[vmem()] * 4 + [sum_spec] * 2 + [late_spec] * 2,
        )
        recv = swap(send, "seq", seqs, 2)
        grad_frames, out = place(
            chain, info, [(grad_own, (back, 0)), (out, (back, 1))], [F32, BF16], "place_frames"
        )
        ckx, cx, cky, cy = chain(add_both_kernel, [quarter] * 4, [ckx, crx, cky, cry], 4, "cross_add1")
        crx, cry = over_y(cx), over_x(cy)
        tkx, tx, tky, ty = chain(add_both_kernel, [quarter] * 4, [tkx, trx, tky, try_], 4, "attn_add1")
        trx, try_ = over_y(tx), over_x(ty)
        keep, send = chain(mlp_third_kernel, [sds((208, D), BF16)] * 2, [keep, recv], 4, "mlp_z1")
        recv = swap(send, "seq", seqs, 4)
        rows = 96 + cap_rows
        c_keep, c_send = chain(
            second_kernel, [sds((2, rows, D), BF16)] * 2, [ckx, crx, cky, cry, dcap], 4, "cross_add2",
        )
        c_recv = swap(c_send, "seq", seqs, 2)
        t_keep, t_send = chain(second_kernel, [quarter] * 2, [tkx, trx, tky, try_], 4, "attn_add2")
        t_recv = swap(t_send, "seq", seqs, 2)
        a_all = to_band(chain(mlp_fourth_kernel, [sds((224, D), BF16)], [keep, recv], 4, "mlp_z2")[0])
        c_keep, c_send = chain(third_kernel, [sds((rows, D), BF16)] * 2, [c_keep, c_recv], 4, "cross_z1")
        c_recv = swap(c_send, "seq", seqs, 4)
        t_keep, t_send = chain(third_kernel, [tile] * 2, [t_keep, t_recv], 4, "attn_z1")
        t_recv = swap(t_send, "seq", seqs, 4)
        g_down, g_up = finish(chain, mlp_finish_kernel, info, a_all, [(384, D), (96, FF)], "mlp_finish")
        t_done, cap_same, cap_away = chain(
            fourth_kernel, [sds((192, D), BF16)] + [sds((cap_rows, D), F32)] * 2,
            [t_keep, t_recv, c_keep, c_recv], 4, "other_z2",
        )
        t_all = to_band(t_done)
        grad_caption = place(chain, info, [(cap_same, cap_away)], [F32], "place_caption")[0]
        sums = a_all
    else:
        grad_frames, out = place(
            chain, info, [(grad_own, (back, 0)), (out, (back, 1))], [F32, BF16], "place_frames"
        )
        dkv2 = jnp.concatenate([fac[4 * own : 4 * own + cap_total], fac[5 * own : 5 * own + cap_total]], axis=1)
        dcap = dot_nt(dkv2, cross_keyval).astype(BF16).reshape(seqs, cap_rows, D)
        place_of = jnp.asarray([order.index(k) for k in range(seqs)])
        dcap = dcap[place_of[jnp.bitwise_xor(seq, jnp.arange(seqs))]].reshape(cap_total, D)
        dcap = jnp.where(half == 0, jnp.stack([dcap, 0 * dcap]), jnp.stack([0 * dcap, dcap]))
        grad_caption = lax.psum_scatter(dcap, "seq", scatter_dimension=1, tiled=True).astype(F32)
        rows = jnp.concatenate([dqkv[3 * own : 3 * own + 2].astype(F32), early[0:12], jnp.zeros((2, D), F32)])
        for k in range(1, halves):
            if k & (k - 1) == 0:
                rows = rows + swap(rows, "seq", seqs, k)
        rows = jnp.concatenate([rows, swap(rows, "seq", seqs, halves)]).astype(BF16)
        sums = [rows] + [swap(rows, "band", bands, t) for t in range(1, bands)]

    g_ada, gb_ada, g_t2, gb_t2, g_t1, gb_t1, gb_down, gb_up = mod_back(
        chain, info, sums, ada_weight, pre_cond, embed, time_second, seqs
    )

    if fast:
        g_in, g_out, g_cq, g_ckv, g_co = finish(
            chain, last_finish_kernel, info, t_all, [(96, 3 * D), (96, D), (96, D), (96, 2 * D), (96, D)],
            "last_finish", [pltpu.VMEM((4, 192, D), BF16)],
        )
    else:
        slot = lambda i: fac[i * own : (i + 1) * own]
        acted = jnp.concatenate([big[i] for i in range(FF // D)], axis=1)
        dupper = jnp.concatenate([big[FF // D + i] for i in range(FF // D)], axis=1)
        g_down = plain_reduce(acted, big[2 * STEPS + 1], seqs)
        g_up = plain_reduce(big[2 * STEPS], dupper, seqs)
        g_cq = plain_reduce(slot(0), slot(1), seqs)
        g_ckv = plain_reduce(cap_all, jnp.concatenate([slot(4), slot(5)], axis=1), seqs)
        g_co = plain_reduce(slot(2), slot(3), seqs)
        g_out = plain_reduce(mixed, slot(6), seqs)
        g_in = plain_reduce(h1, jnp.concatenate([dqkv[i * own : (i + 1) * own] for i in range(3)], axis=1), seqs)

    flat = lambda v: v.reshape(-1)
    return (
        out, grad_frames, grad_caption, g_in, g_out, g_cq, g_ckv, g_co, g_up, flat(gb_up), g_down,
        flat(gb_down), g_ada, flat(gb_ada), g_t1, flat(gb_t1), g_t2, flat(gb_t2),
    )


def solution(mesh):
    split = P("band", "seq", None)
    rows, flat = P("seq", None), P("seq")
    return jax.shard_map(
        functools.partial(on_device, mesh.shape["band"], mesh.shape["seq"]),
        mesh=mesh,
        in_specs=(split, split) + (P(),) * 17 + (split,),
        out_specs=(split, split, split, rows, rows, rows, rows, rows, rows, flat, rows, flat, rows, flat,
                   rows, flat, rows, flat),
        check_vma=False,
    )
```
